32 devices in a mesh: grp: 4 (over y, core), tok: 8 (over z, x).
Axes of the slice: x: 2, y: 2, z: 4, core: 2. Of those that a mesh axis runs over, the one named last changes fastest.
Arguments:
- probe_states: bfloat16 [256, 2048], P('tok'), may hold values from -40 to 40
- norm_gain: float32 [2048], replicated, may hold values from 0.1 to 1.9
- gate_weight: bfloat16 [6144, 2048], P(('grp', 'tok')), may hold values from -1 to 1
- up_weight: bfloat16 [6144, 2048], P(('grp', 'tok')), may hold values from -1 to 1
- down_weight: bfloat16 [6144, 2048], P(('grp', 'tok')), may hold values from -1 to 1
- route_weight: float32 [32, 64], P(('grp', 'tok')), may hold values from 0.02 to 1
Outputs:
- features: bfloat16 [2048, 2048], P(('grp', 'tok'))
- cka: float32 [8, 8], replicated
The draws below stay inside these ranges and needn't reach their ends.
All inputs are finite; a program needn't handle non-finite values.
Results may differ from the reference program's by a relative error of at most 0.0015.
The reference program's roundings to bfloat16 on the way (of `normed`, `hidden` and `centered`) count: a program that leaves them out, or rounds other values in their place, can miss the bound.
Values may be sent and summed in bfloat16 or wider, within the bound.
No kernel may reach another device: no remote copies, remote signals or barrier semaphores. Data moves between devices by JAX's collectives and lax.ppermute only.
A program may use at most 64 MiB of HBM per device.

```python
import math
import jax
import jax.numpy as jnp
from jax import lax

D = 2048
FF = 768
TOKENS = 256
EXPERTS = 8


def fresh_noise(key, shape):
    return jnp.clip(jax.random.normal(key, shape, jnp.float32), -6.0, 6.0)


def cluster_mix(key):
    clusters = jax.random.randint(jax.random.fold_in(key, 101), (EXPERTS,), 0, 4).astype(jnp.int32)
    mixing = jax.random.uniform(jax.random.fold_in(key, 102), (EXPERTS,), jnp.float32, 0.35, 0.95)
    return (clusters, mixing)


def clustered_weight(key, salt_value, fan_count):
    clusters, mixing = cluster_mix(key)
    shared = fresh_noise(jax.random.fold_in(key, salt_value), (4, FF, D))
    own_key = jax.random.fold_in(key, salt_value + 1)

    def one_slab(inputs):
        expert_index, cluster_index, weight_mix = inputs
        common = lax.dynamic_index_in_dim(shared, cluster_index, 0, keepdims=False)
        private = fresh_noise(jax.random.fold_in(own_key, expert_index), (FF, D))
        mixed = weight_mix * common + jnp.sqrt(1.0 - weight_mix * weight_mix) * private
        return mixed / jnp.sqrt(jnp.float32(fan_count))
    slabs = lax.map(one_slab, (jnp.arange(EXPERTS, dtype=jnp.int32), clusters, mixing))
    return slabs.reshape(EXPERTS * FF, D).astype(jnp.bfloat16)


def draw_gate_weight(key, part):
    return clustered_weight(key, 201, D)


def draw_up_weight(key, part):
    return clustered_weight(key, 301, D)


def draw_down_weight(key, part):
    return clustered_weight(key, 401, FF)


def draw_probe_states(key, part):
    directions = jax.random.normal(jax.random.fold_in(key, 501), (4, 2, D), jnp.float32)
    loadings = jax.random.normal(jax.random.fold_in(key, 502), (TOKENS, 2), jnp.float32)
    private = fresh_noise(jax.random.fold_in(key, 503), (TOKENS, D))
    block_of_row = (jnp.arange(TOKENS, dtype=jnp.int32) // (TOKENS // 4)).astype(jnp.int32)
    chosen = directions[block_of_row]
    structured = (loadings[:, 0:1] * chosen[:, 0, :] + loadings[:, 1:2] * chosen[:, 1, :]) / jnp.sqrt(jnp.float32(2.0))
    states = jnp.sqrt(jnp.float32(0.4)) * structured + jnp.sqrt(jnp.float32(0.6)) * private
    return jnp.clip(states, -40.0, 40.0).astype(jnp.bfloat16)


def level_of(key, extent, cuts, low, high):
    factor_of = 1.0
    for position, blocks in cuts:
        draws = jax.random.uniform(jax.random.fold_in(jax.random.fold_in(key, 6), position), (blocks,), jnp.float32, low / len(cuts), high / len(cuts))
        factor_of = factor_of * jnp.repeat(jnp.exp(draws), extent[position] // blocks).reshape((-1,) + (1,) * (len(extent) - 1 - position))
    return factor_of


def setup_inputs(seed: int = 0) -> dict:
    splits = jax.random.split(jax.random.key(seed), 7)
    return {
        "probe_states": draw_probe_states(jax.random.fold_in(splits[6], 71), 0),
        "norm_gain": jnp.clip(1.0 + 0.18 * jax.random.normal(splits[1], (D,), jnp.float32), 0.1, 1.9),
        "gate_weight": draw_gate_weight(jax.random.fold_in(splits[6], 71), 0),
        "up_weight": draw_up_weight(jax.random.fold_in(splits[6], 71), 0),
        "down_weight": draw_down_weight(jax.random.fold_in(splits[6], 71), 0),
        "route_weight": jnp.clip(jnp.exp(math.log(1.0) - 3.912023 * jax.random.uniform(splits[5], (EXPERTS * 4, TOKENS // 4), jnp.float32) ** level_of(splits[5], (EXPERTS * 4, TOKENS // 4), ((0, 32),), -0.2, 0.2)), 0.02, 1.0),
    }


def reference(probe_states, norm_gain, gate_weight, up_weight, down_weight, route_weight):
    states = probe_states.astype(jnp.float32)
    scaled = states * lax.rsqrt(lax.optimization_barrier(jnp.mean(states * states, axis=1, keepdims=True)) + 1e-06) * norm_gain
    normed = scaled.astype(jnp.bfloat16)
    gates = gate_weight.reshape(EXPERTS, FF, D)
    uppers = up_weight.reshape(EXPERTS, FF, D)
    downs = down_weight.reshape(EXPERTS, FF, D)
    routes = route_weight.reshape(EXPERTS, TOKENS)
    contract = (((1,), (1,)), ((), ()))

    def one_expert(weights):
        w_gate, w_up, w_down, route_row = weights
        gate = lax.dot_general(normed, w_gate, contract, preferred_element_type=jnp.float32)
        upward = lax.dot_general(normed, w_up, contract, preferred_element_type=jnp.float32)
        hidden = (jax.nn.silu(gate) * upward).astype(jnp.bfloat16)
        output = jnp.dot(hidden, w_down, preferred_element_type=jnp.float32)
        feats = (output * route_row[:, None]).astype(jnp.bfloat16)
        column_mean = lax.optimization_barrier(jnp.sum(feats, axis=0, dtype=jnp.float32)) / TOKENS
        projection = lax.optimization_barrier(jnp.sum(feats.astype(jnp.float32) * column_mean, axis=1))
        mean_square = jnp.sum(column_mean * column_mean)
        gram = lax.dot_general(feats, feats, contract, preferred_element_type=jnp.float32)
        centered = (gram - projection[:, None] - projection[None, :] + mean_square).astype(jnp.bfloat16)
        return (feats, centered.reshape(-1))
    feats_all, flat = lax.map(one_expert, (gates, uppers, downs, routes))
    pair_totals = jnp.dot(flat, flat.T, preferred_element_type=jnp.float32)
    diagonal = jnp.diagonal(pair_totals)
    cka = pair_totals / jnp.sqrt(diagonal[:, None] * diagonal[None, :])
    return (feats_all.reshape(EXPERTS * TOKENS, D), cka)
```

```python
import functools

import jax
import jax.numpy as jnp
from jax import lax
from jax.experimental import pallas as pl
from jax.experimental.pallas import tpu as pltpu
from jax.sharding import PartitionSpec as P

HOLDERS = 4
LANES = 128
TRANSPOSED = (((1,), (1,)), ((), ()))
VMEM = pl.BlockSpec(memory_space=pltpu.VMEM)
SMEM = pl.BlockSpec(memory_space=pltpu.SMEM)


def swapped(array, axis, mask):
    return lax.ppermute(array, axis, [(i, i ^ mask) for i in range(lax.axis_size(axis))])


def dot_f32(a, b, dims):
    return lax.dot_general(a, b, dims, preferred_element_type=jnp.float32)


def call(body, outs, vmem_bytes, *operands, scalars=0):
    return pl.pallas_call(
        body,
        out_shape=outs,
        in_specs=[SMEM] * scalars + [VMEM] * (len(operands) - scalars),
        out_specs=jax.tree.map(lambda _: VMEM, outs),
        compiler_params=pltpu.CompilerParams(vmem_limit_bytes=vmem_bytes),
    )(*operands)


def norm_kernel(states_ref, gain_ref, out_ref):
    states = states_ref[...].astype(jnp.float32)
    scale = lax.rsqrt(jnp.mean(states * states, axis=1, keepdims=True) + 1e-06)
    out_ref[...] = (states * scale * gain_ref[...]).astype(jnp.bfloat16)


def hidden_kernel(half_ref, mine_ref, other_ref, gate_ref, up_ref, out_ref):
    width = mine_ref.shape[1]
    own = pl.ds(pl.multiple_of(half_ref[0] * width, width), width)
    far = pl.ds(pl.multiple_of((1 - half_ref[0]) * width, width), width)
    mine, other = mine_ref[...], other_ref[...]
    gate = dot_f32(mine, gate_ref[:, own], TRANSPOSED) + dot_f32(other, gate_ref[:, far], TRANSPOSED)
    upward = dot_f32(mine, up_ref[:, own], TRANSPOSED) + dot_f32(other, up_ref[:, far], TRANSPOSED)
    out_ref[...] = (gate / (1.0 + jnp.exp(-gate)) * upward).astype(jnp.bfloat16)


def features_kernel(*refs):
    hidden_refs, down_refs = refs[:HOLDERS], refs[HOLDERS : 2 * HOLDERS]
    route_ref, features_ref, centered_ref = refs[2 * HOLDERS :]
    plain = (((1,), (0,)), ((), ()))
    output = dot_f32(hidden_refs[0][...], down_refs[0][...], plain)
    for h, w in zip(hidden_refs[1:], down_refs[1:]):
        output = output + dot_f32(h[...], w[...], plain)
    features = (output * route_ref[...]).astype(jnp.bfloat16)
    features_ref[...] = features
    tokens = features.shape[0]
    wide = features.astype(jnp.float32)
    mean = jnp.sum(wide, axis=0, keepdims=True) / tokens
    column = jnp.sum(wide * mean, axis=1, keepdims=True)
    row = jnp.transpose(jnp.broadcast_to(column, (tokens, LANES)))[:1]
    gram = dot_f32(features, features, TRANSPOSED)
    centered = (gram - column - row + jnp.sum(mean * mean)).astype(jnp.bfloat16)
    depth = 16
    at = 0
    for i in range(tokens // depth):
        for j in range(tokens // LANES):
            centered_ref[at * depth : (at + 1) * depth] = centered[
                i * depth : (i + 1) * depth, j * LANES : (j + 1) * LANES
            ]
            at += 1


def pair_kernel(parts_ref, out_ref):
    experts, holders, depth, lanes = parts_ref.shape
    flat = jnp.sum(parts_ref[...].astype(jnp.float32), axis=1).astype(jnp.bfloat16)
    flat = flat.reshape(experts, depth * lanes)
    out_ref[...] = dot_f32(flat, flat, TRANSPOSED)


def cka_of(totals):
    diagonal = jnp.diagonal(totals)
    return totals / jnp.sqrt(diagonal[:, None] * diagonal[None, :])


def shards(probe_states, norm_gain, gate_weight, up_weight, down_weight, route_weight):
    group, position = lax.axis_index("grp"), lax.axis_index("tok")
    groups, members = lax.axis_size("grp"), lax.axis_size("tok")
    devices = groups * members
    rows, model = probe_states.shape
    tokens = rows * members
    hidden_rows = gate_weight.shape[0]
    holder = position % HOLDERS
    big = 48 * 1024 * 1024

    normed = call(
        norm_kernel,
        jax.ShapeDtypeStruct((rows, model), jnp.bfloat16),
        big,
        probe_states,
        norm_gain[None, :],
    )
    half_width = model // 2
    half = group % 2
    own_half = lax.dynamic_slice_in_dim(normed, half * half_width, half_width, 1)
    spread = jnp.broadcast_to(own_half[None], (members, rows, half_width))
    mine = lax.all_to_all(spread, "tok", split_axis=0, concat_axis=0, tiled=True)
    mine = mine.reshape(tokens, half_width)
    down_weight, mine = lax.optimization_barrier((down_weight, mine))
    other = swapped(mine, "grp", 1)

    part = model // HOLDERS
    column = route_weight.reshape(-1, 1)
    downs, routes = [], []
    for mask in range(HOLDERS):
        block = lax.dynamic_slice_in_dim(down_weight, (holder ^ mask) * part, part, 1)
        downs.append(swapped(block, "tok", mask) if mask else block)
        routes.append(swapped(route_weight, "tok", mask) if mask else route_weight)
    every_route = jnp.stack(routes)[:, 0]
    every_route = jnp.stack([every_route[0], every_route[1], every_route[2], every_route[3]])
    swap_low = jnp.where(holder & 1, every_route[jnp.array([1, 0, 3, 2])], every_route)
    ordered = jnp.where(holder & 2, swap_low[jnp.array([2, 3, 0, 1])], swap_low)
    route_column = ordered.reshape(tokens, 1)

    hidden = call(
        hidden_kernel,
        jax.ShapeDtypeStruct((tokens, hidden_rows), jnp.bfloat16),
        big,
        half[None].astype(jnp.int32),
        mine,
        other,
        gate_weight,
        up_weight,
        scalars=1,
    )
    hiddens = [hidden] + [swapped(hidden, "tok", mask) for mask in range(1, HOLDERS)]
    depth = tokens * tokens // LANES // devices
    features_part, centered = call(
        features_kernel,
        (
            jax.ShapeDtypeStruct((tokens, part), jnp.bfloat16),
            jax.ShapeDtypeStruct((devices * depth, LANES), jnp.bfloat16),
        ),
        big,
        *hiddens,
        *downs,
        route_column,
    )
    arrived = lax.all_to_all(centered, ("grp", "tok"), split_axis=0, concat_axis=0, tiled=True)
    arrived = arrived.reshape(devices // HOLDERS, HOLDERS, depth, LANES)
    experts = devices // HOLDERS
    flat = jnp.sum(arrived.astype(jnp.float32), axis=1).astype(jnp.bfloat16).reshape(experts, -1)
    partial_value = dot_f32(flat, flat, TRANSPOSED)
    if devices * partial_value.size <= 1 << 16:
        copies = jnp.broadcast_to(partial_value[None], (devices, experts, experts))
        totals = jnp.sum(
            lax.all_to_all(copies, ("grp", "tok"), split_axis=0, concat_axis=0, tiled=True), axis=0
        )
    else:
        totals = lax.psum(partial_value, ("grp", "tok"))

    token_part = tokens // HOLDERS
    features = jnp.zeros((token_part, model), jnp.bfloat16)
    for mask in range(HOLDERS):
        block = lax.dynamic_slice_in_dim(features_part, (holder ^ mask) * token_part, token_part, 0)
        got = swapped(block, "tok", mask) if mask else block
        features = lax.dynamic_update_slice_in_dim(features, got, (holder ^ mask) * part, 1)
    return (features, cka_of(totals))


def solution(mesh):
    return jax.shard_map(
        shards,
        mesh=mesh,
        in_specs=(
            P("tok", None),
            P(),
            P(("grp", "tok"), None),
            P(("grp", "tok"), None),
            P(("grp", "tok"), None),
            P(("grp", "tok"), None),
        ),
        out_specs=(P(("grp", "tok"), None), P()),
        check_vma=False,
    )
```

```python
import jax
import jax.numpy as jnp
from jax import lax
from jax.experimental import pallas as pl
from jax.experimental.pallas import tpu as pltpu
from jax.sharding import PartitionSpec as P

HOLDERS = 4
LANES = 128
TILE = 16
BIG = 48 * 1024 * 1024
TRANSPOSED = (((1,), (1,)), ((), ()))
VMEM = pl.BlockSpec(memory_space=pltpu.VMEM)
SMEM = pl.BlockSpec(memory_space=pltpu.SMEM)
ANY = pl.BlockSpec(memory_space=pl.ANY)
bf16 = jnp.bfloat16
f32 = jnp.float32


def swapped(array, axis, mask):
    return lax.ppermute(array, axis, [(i, i ^ mask) for i in range(lax.axis_size(axis))])


def dot_f32(a, b, dims):
    return lax.dot_general(a, b, dims, preferred_element_type=f32)


def call(body, outs, in_specs, operands, out_specs=None, scratch=()):
    return pl.pallas_call(
        body,
        out_shape=outs,
        in_specs=in_specs,
        out_specs=jax.tree.map(lambda _: VMEM, outs) if out_specs is None else out_specs,
        scratch_shapes=list(scratch),
        compiler_params=pltpu.CompilerParams(vmem_limit_bytes=BIG),
    )(*operands)


def norm_kernel(place_ref, states_ref, gain_ref, out_ref):
    states = states_ref[...].astype(f32)
    scale = lax.rsqrt(jnp.mean(states * states, axis=1, keepdims=True) + 1e-06)
    width = out_ref.shape[1]
    own = pl.ds(pl.multiple_of(place_ref[0] * width, width), width)
    out_ref[...] = (states_ref[:, own].astype(f32) * scale * gain_ref[:, own]).astype(bf16)


def stack_kernel(place_ref, *refs):
    pieces, out_ref = refs[:-1], refs[-1]
    rows = pieces[0].shape[0]
    for m, piece in enumerate(pieces):
        place = (place_ref[1] >> 1) ^ m
        out_ref[pl.ds(pl.multiple_of(place * rows, rows), rows)] = piece[...]


def stacked(place, pieces):
    rows, width = pieces[0].shape
    out = jax.ShapeDtypeStruct((rows * len(pieces), width), bf16)
    return call(stack_kernel, out, [SMEM] + [VMEM] * len(pieces), (place, *pieces))


def cut_kernel(place_ref, route_ref, after_ref, down_ref, *refs):
    outs, sems = refs[:-1], refs[-1]
    rows, width = down_ref.shape[0], outs[0].shape[1]
    holder = place_ref[1] & (HOLDERS - 1)
    copies = []
    for m, out_ref in enumerate(outs):
        columns = pl.ds(pl.multiple_of((holder ^ m) * width, width), width)
        copies.append(
            pltpu.make_async_copy(
                down_ref.at[:, columns], out_ref.at[pl.ds(0, rows)], sems.at[m]
            )
        )
        copies[-1].start()
    route = route_ref[...]
    high = route.astype(bf16)
    middle = (route - high.astype(f32)).astype(bf16)
    low = (route - high.astype(f32) - middle.astype(f32)).astype(bf16)
    count = route.shape[1]
    row = lax.broadcasted_iota(jnp.int32, (TILE, count), 0)
    terms = jnp.where(
        row == 0,
        high.astype(f32),
        jnp.where(row == 1, middle.astype(f32), jnp.where(row == 2, low.astype(f32), 0.0)),
    )
    terms = jnp.concatenate([terms, jnp.zeros((TILE, width - count), f32)], 1).astype(bf16)
    for out_ref in outs:
        out_ref[rows : rows + TILE] = terms
    for copy in copies:
        copy.wait()


def hidden_kernel(count, place_ref, near_ref, far_ref, near2_ref, far2_ref, gate_ref, up_ref, out_ref, tokens_ref):
    width = near_ref.shape[1]
    rows = near_ref.shape[0] // count
    x = place_ref[1] & 1
    for half, near, far in ((place_ref[0], near_ref, far_ref), (1 - place_ref[0], near2_ref, far2_ref)):
        columns = pl.ds(pl.multiple_of(half * width, width), width)
        for at, block in ((x, near), (1 - x, far)):
            for z in range(count):
                place = pl.multiple_of((2 * z + at) * rows, rows)
                tokens_ref[pl.ds(place, rows), columns] = block[z * rows : (z + 1) * rows]
    tokens = tokens_ref[...]
    gate = dot_f32(gate_ref[...], tokens, TRANSPOSED)
    upward = dot_f32(up_ref[...], tokens, TRANSPOSED)
    out_ref[...] = (gate / (1.0 + jnp.exp(-gate)) * upward).astype(bf16)


def features_kernel(place_ref, *refs):
    hidden_refs, down_refs = refs[:HOLDERS], refs[HOLDERS : 2 * HOLDERS]
    block_refs, centered_ref = refs[2 * HOLDERS : 3 * HOLDERS], refs[3 * HOLDERS]
    route_ref, features_ref = refs[3 * HOLDERS + 1 :]
    holder = place_ref[1] & (HOLDERS - 1)
    depth, tokens = hidden_refs[0].shape
    part = tokens // HOLDERS
    eye = lax.broadcasted_iota(jnp.int32, (part, part), 0) == lax.broadcasted_iota(
        jnp.int32, (part, part), 1
    )
    output = None
    for m, (hidden_ref, down_ref) in enumerate(zip(hidden_refs, down_refs)):
        product = dot_f32(hidden_ref[...], down_ref[:depth], (((0,), (0,)), ((), ())))
        output = product if output is None else output + product
        terms = down_ref[depth:, :part].astype(f32)
        route = jnp.sum(terms[:HOLDERS], axis=0, keepdims=True)
        column = jnp.sum(jnp.where(eye, route, 0.0), axis=1, keepdims=True)
        place = pl.multiple_of((holder ^ m) * part, part)
        route_ref[pl.ds(place, part)] = jnp.broadcast_to(column, (part, LANES))
    features = (output * route_ref[:, :1]).astype(bf16)
    features_ref[...] = features
    wide = features.astype(f32)
    mean = jnp.sum(wide, axis=0, keepdims=True) / tokens
    column = jnp.sum(wide * mean, axis=1, keepdims=True)
    row = jnp.transpose(jnp.broadcast_to(column, (tokens, LANES)))[:1]
    gram = dot_f32(features, features, TRANSPOSED)
    centered = (gram - column - row + jnp.sum(mean * mean)).astype(bf16)
    at = 0
    for i in range(tokens // TILE):
        for j in range(tokens // LANES):
            centered_ref[at * TILE : (at + 1) * TILE] = centered[
                i * TILE : (i + 1) * TILE, j * LANES : (j + 1) * LANES
            ]
            at += 1
    for m, block_ref in enumerate(block_refs):
        block_ref[...] = features_ref[pl.ds(pl.multiple_of((holder ^ m) * part, part), part)]


def place_kernel(place_ref, *refs):
    blocks, out_ref, sems = refs[:HOLDERS], refs[HOLDERS], refs[HOLDERS + 1]
    width = blocks[0].shape[1]
    holder = place_ref[1] & (HOLDERS - 1)
    copies = []
    for m, block in enumerate(blocks):
        columns = pl.ds(pl.multiple_of((holder ^ m) * width, width), width)
        copies.append(pltpu.make_async_copy(block, out_ref.at[:, columns], sems.at[m]))
        copies[-1].start()
    for copy in copies:
        copy.wait()


def pair_kernel(parts_ref, out_ref, flat_ref):
    copies, experts, _ = out_ref.shape
    parts = parts_ref[...].astype(f32)
    total = parts[:, 0]
    for holder in range(1, parts.shape[1]):
        total = total + parts[:, holder]
    flat_ref[...] = total.astype(bf16).astype(f32)
    lane = lax.broadcasted_iota(jnp.int32, (experts, experts), 1)

    def one(expert, table):
        products = jnp.sum(flat_ref[...] * flat_ref[pl.ds(expert, 1)], axis=1)
        return jnp.where(lane == expert, jnp.sum(products, axis=1, keepdims=True), table)

    table = lax.fori_loop(0, experts, one, jnp.zeros((experts, experts), f32), unroll=experts <= 8)
    for copy in range(copies):
        out_ref[copy] = table


def cka_kernel(tables_ref, out_ref):
    totals = jnp.sum(tables_ref[...], axis=0)
    shape = totals.shape
    eye = lax.broadcasted_iota(jnp.int32, shape, 0) == lax.broadcasted_iota(jnp.int32, shape, 1)
    kept = jnp.where(eye, totals, 0.0)
    down = jnp.sum(kept, axis=1, keepdims=True)
    across = jnp.sum(kept, axis=0, keepdims=True)
    out_ref[...] = totals / jnp.sqrt(down * across)


def shards(probe_states, norm_gain, gate_weight, up_weight, down_weight, route_weight):
    groups, members = lax.axis_size("grp"), lax.axis_size("tok")
    devices = groups * members
    experts = devices // HOLDERS
    rows, model = probe_states.shape
    tokens = rows * members
    depth = gate_weight.shape[0]
    part, token_part = model // HOLDERS, tokens // HOLDERS
    place = jnp.stack([lax.axis_index("grp") & 1, lax.axis_index("tok")]).astype(jnp.int32)

    own = call(
        norm_kernel,
        jax.ShapeDtypeStruct((rows, model // 2), bf16),
        [SMEM, VMEM, VMEM],
        (place, probe_states, norm_gain[None, :]),
    )
    count = members // 2
    near = {0: own}
    for m in range(count - 1, 0, -1):
        near[m] = swapped(own, "tok", 2 * m)
    far = {m: swapped(near[m], "tok", 1) for m in range(count)}
    near = stacked(place, [near[m] for m in range(count)])
    near2 = swapped(near, "grp", 1)
    far = stacked(place, [far[m] for m in range(count)])
    far2 = swapped(far, "grp", 1)

    blocks = call(
        cut_kernel,
        [jax.ShapeDtypeStruct((depth + TILE, part), bf16)] * HOLDERS,
        [SMEM, VMEM, ANY, ANY],
        (place, route_weight, own, down_weight),
        scratch=[pltpu.SemaphoreType.DMA((HOLDERS,))],
    )
    downs = [swapped(b, "tok", m) if m else b for m, b in enumerate(blocks)]

    hidden = call(
        lambda *refs: hidden_kernel(count, *refs),
        jax.ShapeDtypeStruct((depth, tokens), bf16),
        [SMEM] + [VMEM] * 6,
        (place, near, far, near2, far2, gate_weight, up_weight),
        scratch=[pltpu.VMEM((tokens, model), bf16)],
    )
    hiddens = [swapped(hidden, "tok", m) if m else hidden for m in range(HOLDERS)]
    entries = tokens * tokens // LANES
    *blocks, centered = call(
        features_kernel,
        [jax.ShapeDtypeStruct((token_part, part), bf16)] * HOLDERS
        + [jax.ShapeDtypeStruct((entries, LANES), bf16)],
        [SMEM] + [VMEM] * (2 * HOLDERS),
        (place, *hiddens, *downs),
        scratch=[pltpu.VMEM((tokens, LANES), f32), pltpu.VMEM((tokens, part), bf16)],
    )
    arrived = lax.all_to_all(centered, ("grp", "tok"), split_axis=0, concat_axis=0, tiled=True)
    arrived = arrived.reshape(experts, HOLDERS, entries // devices, LANES)
    direct = devices * experts * experts <= 1 << 16
    tables = call(
        pair_kernel,
        jax.ShapeDtypeStruct((devices if direct else 1, experts, experts), f32),
        [VMEM],
        (arrived,),
        scratch=[pltpu.VMEM((experts, entries // devices, LANES), f32)],
    )
    if direct:
        tables = lax.all_to_all(tables, ("grp", "tok"), split_axis=0, concat_axis=0, tiled=True)
    else:
        tables = lax.psum(tables, ("grp", "tok"))
    cka = call(cka_kernel, jax.ShapeDtypeStruct((experts, experts), f32), [VMEM], (tables,))

    blocks = [swapped(b, "tok", m) if m else b for m, b in enumerate(blocks)]
    features = call(
        place_kernel,
        jax.ShapeDtypeStruct((token_part, model), bf16),
        [SMEM] + [VMEM] * HOLDERS,
        (place, *blocks),
        out_specs=ANY,
        scratch=[pltpu.SemaphoreType.DMA((HOLDERS,))],
    )
    return (features, cka)


def solution(mesh):
    return jax.shard_map(
        shards,
        mesh=mesh,
        in_specs=(
            P("tok", None),
            P(),
            P(("grp", "tok"), None),
            P(("grp", "tok"), None),
            P(("grp", "tok"), None),
            P(("grp", "tok"), None),
        ),
        out_specs=(P(("grp", "tok"), None), P()),
        check_vma=False,
    )
```

```python
import jax
import jax.numpy as jnp
from jax import lax
from jax.experimental import pallas as pl
from jax.experimental.pallas import tpu as pltpu
from jax.sharding import PartitionSpec as P

HOLDERS = 4
LANES = 128
TILE = 16
BIG = 24 * 1024 * 1024
TRANSPOSED = (((1,), (1,)), ((), ()))
VMEM = pl.BlockSpec(memory_space=pltpu.VMEM)
ANY = pl.BlockSpec(memory_space=pl.ANY)
HBM = pl.BlockSpec(memory_space=pltpu.HBM)
bf16 = jnp.bfloat16
f32 = jnp.float32


def swapped(array, axis, mask):
    return lax.ppermute(array, axis, [(i, i ^ mask) for i in range(lax.axis_size(axis))])


def dot_f32(a, b, dims):
    return lax.dot_general(a, b, dims, preferred_element_type=f32)


def call(body, outs, in_specs, operands, out_specs=None, scratch=(), aliases={}):
    return pl.pallas_call(
        body,
        out_shape=outs,
        in_specs=in_specs,
        out_specs=jax.tree.map(lambda _: VMEM, outs) if out_specs is None else out_specs,
        scratch_shapes=list(scratch),
        compiler_params=pltpu.CompilerParams(vmem_limit_bytes=BIG),
        input_output_aliases=aliases,
    )(*operands)


def core():
    return lax.axis_index("grp") & 1


def holder():
    return lax.axis_index("tok") & (HOLDERS - 1)


def first_kernel(states_hbm, gain_hbm, down_hbm, *refs):
    out_ref, downs = refs[0], refs[1 : 1 + HOLDERS]
    states_ref, gain_ref, sems = refs[1 + HOLDERS :]
    copies = [
        pltpu.make_async_copy(states_hbm, states_ref, sems.at[0]),
        pltpu.make_async_copy(gain_hbm, gain_ref, sems.at[1]),
    ]
    width = downs[0].shape[1]
    for m, down_ref in enumerate(downs):
        columns = pl.ds(pl.multiple_of((holder() ^ m) * width, width), width)
        copies.append(pltpu.make_async_copy(down_hbm.at[:, columns], down_ref, sems.at[2 + m]))
    for copy in copies:
        copy.start()
    for copy in copies[:2]:
        copy.wait()
    states = states_ref[...].astype(f32)
    scale = lax.rsqrt(jnp.mean(states * states, axis=1, keepdims=True) + 1e-06)
    width = out_ref.shape[1]
    own = pl.ds(pl.multiple_of(core() * width, width), width)
    out_ref[...] = (states_ref[:, own].astype(f32) * scale * gain_ref[:, own]).astype(bf16)
    for copy in copies[2:]:
        copy.wait()


def hold_kernel(*refs):
    pass


def held(arrays, after):
    return call(
        hold_kernel,
        [jax.ShapeDtypeStruct(a.shape, a.dtype) for a in arrays],
        [ANY] * (len(arrays) + 1),
        (*arrays, after),
        out_specs=[ANY] * len(arrays),
        aliases={i: i for i in range(len(arrays))},
    )


def stack_kernel(*refs):
    pieces, out_ref = refs[1:-1], refs[-1]
    rows = pieces[0].shape[0]
    for m, piece in enumerate(pieces):
        place = lax.axis_index("tok") ^ m
        out_ref[pl.ds(pl.multiple_of(place * rows, rows), rows)] = piece[...]


def hidden_kernel(mine_ref, other_ref, gate_ref, up_ref, route_ref, out_ref):
    tokens, width = mine_ref.shape
    gate, upward = [
        sum(
            dot_f32(ref[:, pl.ds(pl.multiple_of(half * width, width), width)], block[...], TRANSPOSED)
            for half, block in ((core(), mine_ref), (1 - core(), other_ref))
        )
        for ref in (gate_ref, up_ref)
    ]
    depth = gate.shape[0]
    out_ref[:depth] = (gate / (1.0 + jnp.exp(-gate)) * upward).astype(bf16)
    route = route_ref[...]
    high = route.astype(bf16).astype(f32)
    middle = (route - high).astype(bf16).astype(f32)
    low = route - high - middle
    part = route.shape[1]
    row = lax.broadcasted_iota(jnp.int32, (TILE, part), 0)
    terms = jnp.where(row == 0, high, jnp.where(row == 1, middle, jnp.where(row == 2, low, 0.0)))
    terms = jnp.concatenate([terms, jnp.zeros((TILE, tokens - part), f32)], 1)
    out_ref[depth:] = terms.astype(bf16)


def features_kernel(*refs):
    hidden_refs, down_refs = refs[:HOLDERS], refs[HOLDERS : 2 * HOLDERS]
    block_refs, centered_ref = refs[2 * HOLDERS : 3 * HOLDERS], refs[3 * HOLDERS]
    route_ref, features_ref = refs[3 * HOLDERS + 1 :]
    depth, tokens = down_refs[0].shape[0], hidden_refs[0].shape[1]
    part = tokens // HOLDERS
    eye = lax.broadcasted_iota(jnp.int32, (part, part), 0) == lax.broadcasted_iota(
        jnp.int32, (part, part), 1
    )
    output = None
    for m, (hidden_ref, down_ref) in enumerate(zip(hidden_refs, down_refs)):
        product = dot_f32(hidden_ref[:depth], down_ref[...], (((0,), (0,)), ((), ())))
        output = product if output is None else output + product
        terms = hidden_ref[depth:, :part].astype(f32)
        route = jnp.sum(terms[:HOLDERS], axis=0, keepdims=True)
        column = jnp.sum(jnp.where(eye, route, 0.0), axis=1, keepdims=True)
        place = pl.multiple_of((holder() ^ m) * part, part)
        route_ref[pl.ds(place, part)] = jnp.broadcast_to(column, (part, LANES))
    features = (output * route_ref[:, :1]).astype(bf16)
    features_ref[...] = features
    wide = features.astype(f32)
    mean = jnp.sum(wide, axis=0, keepdims=True) / tokens
    column = jnp.sum(wide * mean, axis=1, keepdims=True)
    row = jnp.transpose(jnp.broadcast_to(column, (tokens, LANES)))[:1]
    gram = dot_f32(features, features, TRANSPOSED)
    centered = (gram - column - row + jnp.sum(mean * mean)).astype(bf16)
    at = 0
    for i in range(tokens // TILE):
        for j in range(tokens // LANES):
            centered_ref[at * TILE : (at + 1) * TILE] = centered[
                i * TILE : (i + 1) * TILE, j * LANES : (j + 1) * LANES
            ]
            at += 1
    for m, block_ref in enumerate(block_refs):
        block_ref[...] = features_ref[pl.ds(pl.multiple_of((holder() ^ m) * part, part), part)]


def place_kernel(*refs):
    blocks, out_ref, sems = refs[:HOLDERS], refs[HOLDERS], refs[HOLDERS + 1]
    width = blocks[0].shape[1]
    copies = []
    for m, block in enumerate(blocks):
        columns = pl.ds(pl.multiple_of((holder() ^ m) * width, width), width)
        copies.append(pltpu.make_async_copy(block, out_ref.at[:, columns], sems.at[m]))
        copies[-1].start()
    for copy in copies:
        copy.wait()


def pair_kernel(parts_ref, out_ref, flat_ref):
    copies, experts, _ = out_ref.shape
    parts = parts_ref[...].astype(f32)
    total = parts[:, 0]
    for holder in range(1, parts.shape[1]):
        total = total + parts[:, holder]
    flat_ref[...] = total.astype(bf16).astype(f32)
    lane = lax.broadcasted_iota(jnp.int32, (experts, experts), 1)

    def one(expert, table):
        products = jnp.sum(flat_ref[...] * flat_ref[pl.ds(expert, 1)], axis=1)
        return jnp.where(lane == expert, jnp.sum(products, axis=1, keepdims=True), table)

    table = lax.fori_loop(0, experts, one, jnp.zeros((experts, experts), f32), unroll=experts <= 8)
    for copy in range(copies):
        out_ref[copy] = table


def cka_kernel(tables_ref, out_ref):
    totals = jnp.sum(tables_ref[...], axis=0)
    shape = totals.shape
    eye = lax.broadcasted_iota(jnp.int32, shape, 0) == lax.broadcasted_iota(jnp.int32, shape, 1)
    kept = jnp.where(eye, totals, 0.0)
    down = jnp.sum(kept, axis=1, keepdims=True)
    across = jnp.sum(kept, axis=0, keepdims=True)
    out_ref[...] = totals / jnp.sqrt(down * across)


def shards(probe_states, norm_gain, gate_weight, up_weight, down_weight, route_weight):
    groups, members = lax.axis_size("grp"), lax.axis_size("tok")
    devices = groups * members
    experts = devices // HOLDERS
    rows, model = probe_states.shape
    tokens = rows * members
    depth = gate_weight.shape[0]
    part, token_part = model // HOLDERS, tokens // HOLDERS

    own, down_own, down_x, down_z, down_xz = call(
        first_kernel,
        [jax.ShapeDtypeStruct((rows, model // 2), bf16)]
        + [jax.ShapeDtypeStruct((depth, part), bf16)] * HOLDERS,
        [HBM] * 3,
        [
            pltpu.with_memory_space_constraint(a, pltpu.HBM)
            for a in (probe_states, norm_gain[None, :], down_weight)
        ],
        scratch=[
            pltpu.VMEM((rows, model), bf16),
            pltpu.VMEM((1, model), f32),
            pltpu.SemaphoreType.DMA((2 + HOLDERS,)),
        ],
    )
    pieces = {0: own}
    for m in range(members - 2, 0, -2):
        pieces[m] = swapped(own, "tok", m)
    for m in range(0, members, 2):
        pieces[m + 1] = swapped(pieces[m], "tok", 1)
    down_x = swapped(down_x, "tok", 1)
    mine = call(
        stack_kernel,
        jax.ShapeDtypeStruct((tokens, model // 2), bf16),
        [ANY] + [VMEM] * members,
        (down_x, *[pieces[m] for m in range(members)]),
    )
    other = swapped(mine, "grp", 1)
    (down_z,) = held((down_z,), pieces[2])
    (down_xz,) = held((down_xz,), mine)
    downs = [down_own, down_x, swapped(down_z, "tok", 2), swapped(down_xz, "tok", 3)]

    hidden = call(
        hidden_kernel,
        jax.ShapeDtypeStruct((depth + TILE, tokens), bf16),
        [VMEM] * 5,
        (mine, other, gate_weight, up_weight, route_weight),
    )
    hiddens = [swapped(hidden, "tok", m) if m else hidden for m in range(HOLDERS)]
    entries = tokens * tokens // LANES
    *blocks, centered = call(
        features_kernel,
        [jax.ShapeDtypeStruct((token_part, part), bf16)] * HOLDERS
        + [jax.ShapeDtypeStruct((entries, LANES), bf16)],
        [VMEM] * (2 * HOLDERS),
        (*hiddens, *downs),
        scratch=[pltpu.VMEM((tokens, LANES), f32), pltpu.VMEM((tokens, part), bf16)],
    )
    arrived = lax.all_to_all(centered, ("grp", "tok"), split_axis=0, concat_axis=0, tiled=True)
    arrived = arrived.reshape(experts, HOLDERS, entries // devices, LANES)
    direct = devices * experts * experts <= 1 << 16
    tables = call(
        pair_kernel,
        jax.ShapeDtypeStruct((devices if direct else 1, experts, experts), f32),
        [VMEM],
        (arrived,),
        scratch=[pltpu.VMEM((experts, entries // devices, LANES), f32)],
    )
    if direct:
        tables = lax.all_to_all(tables, ("grp", "tok"), split_axis=0, concat_axis=0, tiled=True)
    else:
        tables = lax.psum(tables, ("grp", "tok"))
    cka = call(cka_kernel, jax.ShapeDtypeStruct((experts, experts), f32), [VMEM], (tables,))

    blocks = [swapped(b, "tok", m) if m else b for m, b in enumerate(blocks)]
    features = call(
        place_kernel,
        jax.ShapeDtypeStruct((token_part, model), bf16),
        [VMEM] * HOLDERS,
        blocks,
        out_specs=ANY,
        scratch=[pltpu.SemaphoreType.DMA((HOLDERS,))],
    )
    return (features, cka)


def solution(mesh):
    return jax.shard_map(
        shards,
        mesh=mesh,
        in_specs=(
            P("tok", None),
            P(),
            P(("grp", "tok"), None),
            P(("grp", "tok"), None),
            P(("grp", "tok"), None),
            P(("grp", "tok"), None),
        ),
        out_specs=(P(("grp", "tok"), None), P()),
        check_vma=False,
    )
```

```python
import jax
import jax.numpy as jnp
from jax import lax
from jax.experimental import pallas as pl
from jax.experimental.pallas import tpu as pltpu
from jax.sharding import PartitionSpec as P

HOLDERS = 4
LANES = 128
TILE = 16
BIG = 24 * 1024 * 1024
TRANSPOSED = (((1,), (1,)), ((), ()))
VMEM = pl.BlockSpec(memory_space=pltpu.VMEM)
ANY = pl.BlockSpec(memory_space=pl.ANY)
HBM = pl.BlockSpec(memory_space=pltpu.HBM)
bf16 = jnp.bfloat16
f32 = jnp.float32


def swapped(array, axis, mask):
    return lax.ppermute(array, axis, [(i, i ^ mask) for i in range(lax.axis_size(axis))])


def dot_f32(a, b, dims):
    return lax.dot_general(a, b, dims, preferred_element_type=f32)


def call(body, outs, in_specs, operands, out_specs=None, scratch=(), aliases={}):
    return pl.pallas_call(
        body,
        out_shape=outs,
        in_specs=in_specs,
        out_specs=jax.tree.map(lambda _: VMEM, outs) if out_specs is None else out_specs,
        scratch_shapes=list(scratch),
        compiler_params=pltpu.CompilerParams(vmem_limit_bytes=BIG),
        input_output_aliases=aliases,
    )(*operands)


def core():
    return lax.axis_index("grp") & 1


def holder():
    return lax.axis_index("tok") & (HOLDERS - 1)


def first_kernel(states_hbm, gain_hbm, down_hbm, *refs):
    out_ref, downs = refs[0], refs[1 : 1 + HOLDERS]
    states_ref, gain_ref, sems = refs[1 + HOLDERS :]
    copies = [
        pltpu.make_async_copy(states_hbm, states_ref, sems.at[0]),
        pltpu.make_async_copy(gain_hbm, gain_ref, sems.at[1]),
    ]
    width = downs[0].shape[1]
    for m, down_ref in enumerate(downs):
        columns = pl.ds(pl.multiple_of((holder() ^ m) * width, width), width)
        copies.append(pltpu.make_async_copy(down_hbm.at[:, columns], down_ref, sems.at[2 + m]))
    for copy in copies:
        copy.start()
    for copy in copies[:2]:
        copy.wait()
    states = states_ref[...].astype(f32)
    scale = lax.rsqrt(jnp.mean(states * states, axis=1, keepdims=True) + 1e-06)
    width = out_ref.shape[1]
    own = pl.ds(pl.multiple_of(core() * width, width), width)
    out_ref[...] = (states_ref[:, own].astype(f32) * scale * gain_ref[:, own]).astype(bf16)
    for copy in copies[2:]:
        copy.wait()


def hold_kernel(*refs):
    pass


def held(array, after):
    return call(
        hold_kernel,
        jax.ShapeDtypeStruct(array.shape, array.dtype),
        [ANY] * 2,
        (array, after),
        out_specs=ANY,
        aliases={0: 0},
    )


def stack_kernel(*refs):
    pieces, out_ref = refs[2:-1], refs[-1]
    rows = pieces[0].shape[0]
    for m, piece in enumerate(pieces):
        place = lax.axis_index("tok") ^ m
        out_ref[pl.ds(pl.multiple_of(place * rows, rows), rows)] = piece[...]


def hidden_kernel(mine_ref, other_ref, gate_ref, up_ref, route_ref, out_ref):
    tokens, width = mine_ref.shape
    gate, upward = [
        sum(
            dot_f32(ref[:, pl.ds(pl.multiple_of(half * width, width), width)], block[...], TRANSPOSED)
            for half, block in ((core(), mine_ref), (1 - core(), other_ref))
        )
        for ref in (gate_ref, up_ref)
    ]
    depth = gate.shape[0]
    out_ref[:depth] = (gate / (1.0 + jnp.exp(-gate)) * upward).astype(bf16)
    route = route_ref[...]
    high = route.astype(bf16).astype(f32)
    middle = (route - high).astype(bf16).astype(f32)
    low = route - high - middle
    part = route.shape[1]
    row = lax.broadcasted_iota(jnp.int32, (TILE, part), 0)
    terms = jnp.where(row == 0, high, jnp.where(row == 1, middle, jnp.where(row == 2, low, 0.0)))
    terms = jnp.concatenate([terms, jnp.zeros((TILE, tokens - part), f32)], 1)
    out_ref[depth:] = terms.astype(bf16)


def features_kernel(*refs):
    hidden_refs, down_refs = refs[:HOLDERS], refs[HOLDERS : 2 * HOLDERS]
    block_refs, centered_ref = refs[2 * HOLDERS : 3 * HOLDERS], refs[3 * HOLDERS]
    route_ref, features_ref = refs[3 * HOLDERS + 1 :]
    depth, tokens = down_refs[0].shape[0], hidden_refs[0].shape[1]
    part = tokens // HOLDERS
    eye = lax.broadcasted_iota(jnp.int32, (part, part), 0) == lax.broadcasted_iota(
        jnp.int32, (part, part), 1
    )
    output = None
    for m, (hidden_ref, down_ref) in enumerate(zip(hidden_refs, down_refs)):
        product = dot_f32(hidden_ref[:depth], down_ref[...], (((0,), (0,)), ((), ())))
        output = product if output is None else output + product
        terms = hidden_ref[depth:, :part].astype(f32)
        route = jnp.sum(terms[:HOLDERS], axis=0, keepdims=True)
        column = jnp.sum(jnp.where(eye, route, 0.0), axis=1, keepdims=True)
        place = pl.multiple_of((holder() ^ m) * part, part)
        route_ref[pl.ds(place, part)] = jnp.broadcast_to(column, (part, LANES))
    features = (output * route_ref[:, :1]).astype(bf16)
    features_ref[...] = features
    wide = features.astype(f32)
    mean = jnp.sum(wide, axis=0, keepdims=True) / tokens
    column = jnp.sum(wide * mean, axis=1, keepdims=True)
    row = jnp.transpose(jnp.broadcast_to(column, (tokens, LANES)))[:1]
    gram = dot_f32(features, features, TRANSPOSED)
    centered = (gram - column - row + jnp.sum(mean * mean)).astype(bf16)
    at = 0
    for i in range(tokens // TILE):
        for j in range(tokens // LANES):
            centered_ref[at * TILE : (at + 1) * TILE] = centered[
                i * TILE : (i + 1) * TILE, j * LANES : (j + 1) * LANES
            ]
            at += 1
    for m, block_ref in enumerate(block_refs):
        block_ref[...] = features_ref[pl.ds(pl.multiple_of((holder() ^ m) * part, part), part)]


def place_kernel(*refs):
    blocks, out_ref, sems = refs[:HOLDERS], refs[HOLDERS], refs[HOLDERS + 1]
    width = blocks[0].shape[1]
    copies = []
    for m, block in enumerate(blocks):
        columns = pl.ds(pl.multiple_of((holder() ^ m) * width, width), width)
        copies.append(pltpu.make_async_copy(block, out_ref.at[:, columns], sems.at[m]))
        copies[-1].start()
    for copy in copies:
        copy.wait()


def pair_kernel(parts_ref, out_ref, flat_ref):
    copies, experts, _ = out_ref.shape
    parts = parts_ref[...].astype(f32)
    total = parts[:, 0]
    for holder in range(1, parts.shape[1]):
        total = total + parts[:, holder]
    flat_ref[...] = total.astype(bf16).astype(f32)
    lane = lax.broadcasted_iota(jnp.int32, (experts, experts), 1)

    def one(expert, table):
        products = jnp.sum(flat_ref[...] * flat_ref[pl.ds(expert, 1)], axis=1)
        return jnp.where(lane == expert, jnp.sum(products, axis=1, keepdims=True), table)

    table = lax.fori_loop(0, experts, one, jnp.zeros((experts, experts), f32), unroll=experts <= 8)
    for copy in range(copies):
        out_ref[copy] = table


def cka_kernel(tables_ref, out_ref):
    totals = jnp.sum(tables_ref[...], axis=0)
    shape = totals.shape
    eye = lax.broadcasted_iota(jnp.int32, shape, 0) == lax.broadcasted_iota(jnp.int32, shape, 1)
    kept = jnp.where(eye, totals, 0.0)
    down = jnp.sum(kept, axis=1, keepdims=True)
    across = jnp.sum(kept, axis=0, keepdims=True)
    out_ref[...] = totals / jnp.sqrt(down * across)


def shards(probe_states, norm_gain, gate_weight, up_weight, down_weight, route_weight):
    groups, members = lax.axis_size("grp"), lax.axis_size("tok")
    devices = groups * members
    experts = devices // HOLDERS
    rows, model = probe_states.shape
    tokens = rows * members
    depth = gate_weight.shape[0]
    part, token_part = model // HOLDERS, tokens // HOLDERS

    own, *downs = call(
        first_kernel,
        [jax.ShapeDtypeStruct((rows, model // 2), bf16)]
        + [jax.ShapeDtypeStruct((depth, part), bf16)] * HOLDERS,
        [HBM] * 3,
        [
            pltpu.with_memory_space_constraint(a, pltpu.HBM)
            for a in (probe_states, norm_gain[None, :], down_weight)
        ],
        scratch=[
            pltpu.VMEM((rows, model), bf16),
            pltpu.VMEM((1, model), f32),
            pltpu.SemaphoreType.DMA((2 + HOLDERS,)),
        ],
    )
    pieces = {0: own}
    for m in range(members - 2, 0, -2):
        pieces[m] = swapped(own, "tok", m)
    for m in range(0, members, 2):
        pieces[m + 1] = swapped(pieces[m], "tok", 1)
    down_x, down_z = swapped(downs[1], "tok", 1), swapped(downs[2], "tok", 2)
    mine = call(
        stack_kernel,
        jax.ShapeDtypeStruct((tokens, model // 2), bf16),
        [ANY] * 2 + [VMEM] * members,
        (down_x, down_z, *[pieces[m] for m in range(members)]),
    )
    other = swapped(mine, "grp", 1)

    downs = [downs[0], down_x, down_z, swapped(held(downs[3], mine), "tok", 3)]
    hidden = call(
        hidden_kernel,
        jax.ShapeDtypeStruct((depth + TILE, tokens), bf16),
        [VMEM] * 5,
        (mine, other, gate_weight, up_weight, route_weight),
    )
    hiddens = [swapped(hidden, "tok", m) if m else hidden for m in range(HOLDERS)]
    entries = tokens * tokens // LANES
    *blocks, centered = call(
        features_kernel,
        [jax.ShapeDtypeStruct((token_part, part), bf16)] * HOLDERS
        + [jax.ShapeDtypeStruct((entries, LANES), bf16)],
        [VMEM] * (2 * HOLDERS),
        (*hiddens, *downs),
        scratch=[pltpu.VMEM((tokens, LANES), f32), pltpu.VMEM((tokens, part), bf16)],
    )
    arrived = lax.all_to_all(centered, ("grp", "tok"), split_axis=0, concat_axis=0, tiled=True)
    arrived = arrived.reshape(experts, HOLDERS, entries // devices, LANES)
    direct = devices * experts * experts <= 1 << 16
    tables = call(
        pair_kernel,
        jax.ShapeDtypeStruct((devices if direct else 1, experts, experts), f32),
        [VMEM],
        (arrived,),
        scratch=[pltpu.VMEM((experts, entries // devices, LANES), f32)],
    )
    if direct:
        tables = lax.all_to_all(tables, ("grp", "tok"), split_axis=0, concat_axis=0, tiled=True)
    else:
        tables = lax.psum(tables, ("grp", "tok"))
    cka = call(cka_kernel, jax.ShapeDtypeStruct((experts, experts), f32), [VMEM], (tables,))

    blocks = [swapped(b, "tok", m) if m else b for m, b in enumerate(blocks)]
    features = call(
        place_kernel,
        jax.ShapeDtypeStruct((token_part, model), bf16),
        [VMEM] * HOLDERS,
        blocks,
        out_specs=ANY,
        scratch=[pltpu.SemaphoreType.DMA((HOLDERS,))],
    )
    return (features, cka)


def solution(mesh):
    return jax.shard_map(
        shards,
        mesh=mesh,
        in_specs=(
            P("tok", None),
            P(),
            P(("grp", "tok"), None),
            P(("grp", "tok"), None),
            P(("grp", "tok"), None),
            P(("grp", "tok"), None),
        ),
        out_specs=(P(("grp", "tok"), None), P()),
        check_vma=False,
    )
```

```python
import functools

import jax
import jax.numpy as jnp
from jax import lax
from jax.experimental import pallas as pl
from jax.experimental.pallas import tpu as pltpu
from jax.sharding import PartitionSpec as P

HOLDERS = 4
LANES = 128
TILE = 16
BIG = 24 * 1024 * 1024
TRANSPOSED = (((1,), (1,)), ((), ()))
VMEM = pl.BlockSpec(memory_space=pltpu.VMEM)
ANY = pl.BlockSpec(memory_space=pl.ANY)
HBM = pl.BlockSpec(memory_space=pltpu.HBM)
bf16 = jnp.bfloat16
f32 = jnp.float32


def swapped(array, axis, mask):
    return lax.ppermute(array, axis, [(i, i ^ mask) for i in range(lax.axis_size(axis))])


def dot_f32(a, b, dims):
    return lax.dot_general(a, b, dims, preferred_element_type=f32)


def call(body, outs, in_specs, operands, out_specs=None, scratch=(), aliases={}):
    return pl.pallas_call(
        body,
        out_shape=outs,
        in_specs=in_specs,
        out_specs=jax.tree.map(lambda _: VMEM, outs) if out_specs is None else out_specs,
        scratch_shapes=list(scratch),
        compiler_params=pltpu.CompilerParams(vmem_limit_bytes=BIG),
        input_output_aliases=aliases,
    )(*operands)


def core():
    return lax.axis_index("grp") & 1


def holder():
    return lax.axis_index("tok") & (HOLDERS - 1)


def first_kernel(states_hbm, gain_hbm, down_hbm, *refs):
    out_ref, downs = refs[0], refs[1 : 1 + HOLDERS]
    states_ref, gain_ref, sems = refs[1 + HOLDERS :]
    copies = [
        pltpu.make_async_copy(states_hbm, states_ref, sems.at[0]),
        pltpu.make_async_copy(gain_hbm, gain_ref, sems.at[1]),
    ]
    width = downs[0].shape[1]
    for m, down_ref in enumerate(downs):
        columns = pl.ds(pl.multiple_of((holder() ^ m) * width, width), width)
        copies.append(pltpu.make_async_copy(down_hbm.at[:, columns], down_ref, sems.at[2 + m]))
    for copy in copies:
        copy.start()
    for copy in copies[:2]:
        copy.wait()
    states = states_ref[...].astype(f32)
    scale = lax.rsqrt(jnp.mean(states * states, axis=1, keepdims=True) + 1e-06)
    width = out_ref.shape[1]
    own = pl.ds(pl.multiple_of(core() * width, width), width)
    out_ref[...] = (states_ref[:, own].astype(f32) * scale * gain_ref[:, own]).astype(bf16)
    for copy in copies[2:]:
        copy.wait()


def hold_kernel(*refs):
    pass


def held(array, after):
    return call(
        hold_kernel,
        jax.ShapeDtypeStruct(array.shape, array.dtype),
        [ANY] * 2,
        (array, after),
        out_specs=ANY,
        aliases={0: 0},
    )


def stack_kernel(order, *refs):
    pieces, out_ref = refs[1:-1], refs[-1]
    rows = out_ref.shape[0] // lax.axis_size("tok")
    count = 0
    for piece in pieces:
        for at in range(piece.shape[0] // rows):
            place = lax.axis_index("tok") ^ order[count]
            out_ref[pl.ds(pl.multiple_of(place * rows, rows), rows)] = piece[
                at * rows : (at + 1) * rows
            ]
            count += 1


def pair_up_kernel(after_ref, *refs):
    rows = refs[0].shape[0]
    for at, ref in enumerate(refs[:-1]):
        refs[-1][at * rows : (at + 1) * rows] = ref[...]


def together(pieces, after):
    rows, width = pieces[0].shape
    out = jax.ShapeDtypeStruct((rows * len(pieces), width), bf16)
    return call(pair_up_kernel, out, [ANY] + [VMEM] * len(pieces), (after, *pieces))


def hidden_kernel(after_ref, mine_ref, other_ref, gate_ref, up_ref, route_ref, out_ref):
    tokens, width = mine_ref.shape
    gate, upward = [
        sum(
            dot_f32(ref[:, pl.ds(pl.multiple_of(half * width, width), width)], block[...], TRANSPOSED)
            for half, block in ((core(), mine_ref), (1 - core(), other_ref))
        )
        for ref in (gate_ref, up_ref)
    ]
    depth = gate.shape[0]
    out_ref[:depth] = (gate / (1.0 + jnp.exp(-gate)) * upward).astype(bf16)
    route = route_ref[...]
    high = route.astype(bf16).astype(f32)
    middle = (route - high).astype(bf16).astype(f32)
    low = route - high - middle
    part = route.shape[1]
    row = lax.broadcasted_iota(jnp.int32, (TILE, part), 0)
    terms = jnp.where(row == 0, high, jnp.where(row == 1, middle, jnp.where(row == 2, low, 0.0)))
    terms = jnp.concatenate([terms, jnp.zeros((TILE, tokens - part), f32)], 1)
    out_ref[depth:] = terms.astype(bf16)


def features_kernel(*refs):
    hidden_refs, down_refs = refs[:HOLDERS], refs[HOLDERS : 2 * HOLDERS]
    block_refs, centered_ref = refs[2 * HOLDERS : 3 * HOLDERS], refs[3 * HOLDERS]
    route_ref, features_ref = refs[3 * HOLDERS + 1 :]
    depth, tokens = down_refs[0].shape[0], hidden_refs[0].shape[1]
    part = tokens // HOLDERS
    eye = lax.broadcasted_iota(jnp.int32, (part, part), 0) == lax.broadcasted_iota(
        jnp.int32, (part, part), 1
    )
    output = None
    for m, (hidden_ref, down_ref) in enumerate(zip(hidden_refs, down_refs)):
        product = dot_f32(hidden_ref[:depth], down_ref[...], (((0,), (0,)), ((), ())))
        output = product if output is None else output + product
        terms = hidden_ref[depth:, :part].astype(f32)
        route = jnp.sum(terms[:HOLDERS], axis=0, keepdims=True)
        column = jnp.sum(jnp.where(eye, route, 0.0), axis=1, keepdims=True)
        place = pl.multiple_of((holder() ^ m) * part, part)
        route_ref[pl.ds(place, part)] = jnp.broadcast_to(column, (part, LANES))
    features = (output * route_ref[:, :1]).astype(bf16)
    features_ref[...] = features
    wide = features.astype(f32)
    mean = jnp.sum(wide, axis=0, keepdims=True) / tokens
    column = jnp.sum(wide * mean, axis=1, keepdims=True)
    row = jnp.transpose(jnp.broadcast_to(column, (tokens, LANES)))[:1]
    gram = dot_f32(features, features, TRANSPOSED)
    centered = (gram - column - row + jnp.sum(mean * mean)).astype(bf16)
    at = 0
    for i in range(tokens // TILE):
        for j in range(tokens // LANES):
            centered_ref[at * TILE : (at + 1) * TILE] = centered[
                i * TILE : (i + 1) * TILE, j * LANES : (j + 1) * LANES
            ]
            at += 1
    for m, block_ref in enumerate(block_refs):
        block_ref[...] = features_ref[pl.ds(pl.multiple_of((holder() ^ m) * part, part), part)]


def place_kernel(*refs):
    blocks, out_ref, sems = refs[:HOLDERS], refs[HOLDERS], refs[HOLDERS + 1]
    width = blocks[0].shape[1]
    copies = []
    for m, block in enumerate(blocks):
        columns = pl.ds(pl.multiple_of((holder() ^ m) * width, width), width)
        copies.append(pltpu.make_async_copy(block, out_ref.at[:, columns], sems.at[m]))
        copies[-1].start()
    for copy in copies:
        copy.wait()


def pair_kernel(parts_ref, out_ref, flat_ref):
    copies, experts, _ = out_ref.shape
    parts = parts_ref[...].astype(f32)
    total = parts[:, 0]
    for holder in range(1, parts.shape[1]):
        total = total + parts[:, holder]
    flat_ref[...] = total.astype(bf16).astype(f32)
    lane = lax.broadcasted_iota(jnp.int32, (experts, experts), 1)

    def one(expert, table):
        products = jnp.sum(flat_ref[...] * flat_ref[pl.ds(expert, 1)], axis=1)
        return jnp.where(lane == expert, jnp.sum(products, axis=1, keepdims=True), table)

    table = lax.fori_loop(0, experts, one, jnp.zeros((experts, experts), f32), unroll=experts <= 8)
    for copy in range(copies):
        out_ref[copy] = table


def cka_kernel(tables_ref, out_ref):
    totals = jnp.sum(tables_ref[...], axis=0)
    shape = totals.shape
    eye = lax.broadcasted_iota(jnp.int32, shape, 0) == lax.broadcasted_iota(jnp.int32, shape, 1)
    kept = jnp.where(eye, totals, 0.0)
    down = jnp.sum(kept, axis=1, keepdims=True)
    across = jnp.sum(kept, axis=0, keepdims=True)
    out_ref[...] = totals / jnp.sqrt(down * across)


def shards(probe_states, norm_gain, gate_weight, up_weight, down_weight, route_weight):
    groups, members = lax.axis_size("grp"), lax.axis_size("tok")
    devices = groups * members
    experts = devices // HOLDERS
    rows, model = probe_states.shape
    tokens = rows * members
    depth = gate_weight.shape[0]
    part, token_part = model // HOLDERS, tokens // HOLDERS

    own, *downs = call(
        first_kernel,
        [jax.ShapeDtypeStruct((rows, model // 2), bf16)]
        + [jax.ShapeDtypeStruct((depth, part), bf16)] * HOLDERS,
        [HBM] * 3,
        [
            pltpu.with_memory_space_constraint(a, pltpu.HBM)
            for a in (probe_states, norm_gain[None, :], down_weight)
        ],
        scratch=[
            pltpu.VMEM((rows, model), bf16),
            pltpu.VMEM((1, model), f32),
            pltpu.SemaphoreType.DMA((2 + HOLDERS,)),
        ],
    )
    far = range(members - 2, 0, -2)
    along = {m: swapped(own, "tok", m) for m in far}
    first, second = (0, *far[: len(far) // 2]), far[len(far) // 2 :]
    down_x, down_z = swapped(downs[1], "tok", 1), swapped(downs[2], "tok", 2)
    along[0] = own
    parts = [together([along[m] for m in half], down_x) for half in (first, second)]
    crossed = [swapped(half, "tok", 1) for half in parts]
    down_xz = swapped(held(downs[3], crossed[0]), "tok", 3)
    order = (*first, *second, *(m + 1 for m in (*first, *second)))
    mine = call(
        functools.partial(stack_kernel, order),
        jax.ShapeDtypeStruct((tokens, model // 2), bf16),
        [ANY] + [VMEM] * (members // 2 + 2),
        (down_z, *[along[m] for m in (*first, *second)], *crossed),
    )
    downs = [downs[0], down_x, down_z, down_xz]
    other = swapped(mine, "grp", 1)

    hidden = call(
        hidden_kernel,
        jax.ShapeDtypeStruct((depth + TILE, tokens), bf16),
        [ANY] + [VMEM] * 5,
        (down_xz, mine, other, gate_weight, up_weight, route_weight),
    )
    hiddens = [swapped(hidden, "tok", m) if m else hidden for m in range(HOLDERS)]
    entries = tokens * tokens // LANES
    *blocks, centered = call(
        features_kernel,
        [jax.ShapeDtypeStruct((token_part, part), bf16)] * HOLDERS
        + [jax.ShapeDtypeStruct((entries, LANES), bf16)],
        [VMEM] * (2 * HOLDERS),
        (*hiddens, *downs),
        scratch=[pltpu.VMEM((tokens, LANES), f32), pltpu.VMEM((tokens, part), bf16)],
    )
    arrived = lax.all_to_all(centered, ("grp", "tok"), split_axis=0, concat_axis=0, tiled=True)
    arrived = arrived.reshape(experts, HOLDERS, entries // devices, LANES)
    direct = devices * experts * experts <= 1 << 16
    tables = call(
        pair_kernel,
        jax.ShapeDtypeStruct((devices if direct else 1, experts, experts), f32),
        [VMEM],
        (arrived,),
        scratch=[pltpu.VMEM((experts, entries // devices, LANES), f32)],
    )
    if direct:
        tables = lax.all_to_all(tables, ("grp", "tok"), split_axis=0, concat_axis=0, tiled=True)
    else:
        tables = lax.psum(tables, ("grp", "tok"))
    cka = call(cka_kernel, jax.ShapeDtypeStruct((experts, experts), f32), [VMEM], (tables,))

    blocks = [swapped(b, "tok", m) if m else b for m, b in enumerate(blocks)]
    features = call(
        place_kernel,
        jax.ShapeDtypeStruct((token_part, model), bf16),
        [VMEM] * HOLDERS,
        blocks,
        out_specs=ANY,
        scratch=[pltpu.SemaphoreType.DMA((HOLDERS,))],
    )
    return (features, cka)


def solution(mesh):
    return jax.shard_map(
        shards,
        mesh=mesh,
        in_specs=(
            P("tok", None),
            P(),
            P(("grp", "tok"), None),
            P(("grp", "tok"), None),
            P(("grp", "tok"), None),
            P(("grp", "tok"), None),
        ),
        out_specs=(P(("grp", "tok"), None), P()),
        check_vma=False,
    )
```

```python
import functools

import jax
import jax.numpy as jnp
from jax import lax
from jax.experimental import pallas as pl
from jax.experimental.pallas import tpu as pltpu
from jax.sharding import PartitionSpec as P

HOLDERS = 4
LANES = 128
TILE = 16
BIG = 24 * 1024 * 1024
TRANSPOSED = (((1,), (1,)), ((), ()))
VMEM = pl.BlockSpec(memory_space=pltpu.VMEM)
ANY = pl.BlockSpec(memory_space=pl.ANY)
HBM = pl.BlockSpec(memory_space=pltpu.HBM)
bf16 = jnp.bfloat16
f32 = jnp.float32


def swapped(array, axis, mask):
    return lax.ppermute(array, axis, [(i, i ^ mask) for i in range(lax.axis_size(axis))])


def dot_f32(a, b, dims):
    return lax.dot_general(a, b, dims, preferred_element_type=f32)


def call(body, outs, in_specs, operands, out_specs=None, scratch=(), aliases={}):
    return pl.pallas_call(
        body,
        out_shape=outs,
        in_specs=in_specs,
        out_specs=jax.tree.map(lambda _: VMEM, outs) if out_specs is None else out_specs,
        scratch_shapes=list(scratch),
        compiler_params=pltpu.CompilerParams(vmem_limit_bytes=BIG),
        input_output_aliases=aliases,
    )(*operands)


def core():
    return lax.axis_index("grp") & 1


def holder():
    return lax.axis_index("tok") & (HOLDERS - 1)


def first_kernel(states_hbm, gain_hbm, down_hbm, out_ref, own_ref, z_ref, x_ref, states_ref, gain_ref, sems):
    depth, width = own_ref.shape
    blocks = (own_ref, x_ref.at[pl.ds(0, depth)], z_ref, x_ref.at[pl.ds(depth, depth)])
    copies = [
        pltpu.make_async_copy(states_hbm, states_ref, sems.at[0]),
        pltpu.make_async_copy(gain_hbm, gain_ref, sems.at[1]),
    ]
    for m, block in enumerate(blocks):
        columns = pl.ds(pl.multiple_of((holder() ^ m) * width, width), width)
        copies.append(pltpu.make_async_copy(down_hbm.at[:, columns], block, sems.at[2 + m]))
    for copy in copies:
        copy.start()
    for copy in copies[:2]:
        copy.wait()
    states = states_ref[...].astype(f32)
    scale = lax.rsqrt(jnp.mean(states * states, axis=1, keepdims=True) + 1e-06)
    width = out_ref.shape[1]
    own = pl.ds(pl.multiple_of(core() * width, width), width)
    out_ref[...] = (states_ref[:, own].astype(f32) * scale * gain_ref[:, own]).astype(bf16)
    for copy in copies[2:]:
        copy.wait()


def onward_kernel(after_ref, own_ref, got_ref, out_ref):
    depth = own_ref.shape[0]
    out_ref[:depth] = own_ref[...]
    out_ref[depth:] = got_ref[depth:]


def stack_kernel(order, *refs):
    pieces, out_ref = refs[1:-1], refs[-1]
    rows = out_ref.shape[0] // lax.axis_size("tok")
    count = 0
    for piece in pieces:
        for at in range(piece.shape[0] // rows):
            place = lax.axis_index("tok") ^ order[count]
            out_ref[pl.ds(pl.multiple_of(place * rows, rows), rows)] = piece[
                at * rows : (at + 1) * rows
            ]
            count += 1


def pair_up_kernel(after_ref, *refs):
    rows = refs[0].shape[0]
    for at, ref in enumerate(refs[:-1]):
        refs[-1][at * rows : (at + 1) * rows] = ref[...]


def together(pieces, after):
    rows, width = pieces[0].shape
    out = jax.ShapeDtypeStruct((rows * len(pieces), width), bf16)
    return call(pair_up_kernel, out, [ANY] + [VMEM] * len(pieces), (after, *pieces))


def hidden_kernel(mine_ref, other_ref, gate_ref, up_ref, route_ref, out_ref):
    tokens, width = mine_ref.shape
    gate, upward = [
        sum(
            dot_f32(ref[:, pl.ds(pl.multiple_of(half * width, width), width)], block[...], TRANSPOSED)
            for half, block in ((core(), mine_ref), (1 - core(), other_ref))
        )
        for ref in (gate_ref, up_ref)
    ]
    depth = gate.shape[0]
    out_ref[:depth] = (gate / (1.0 + jnp.exp(-gate)) * upward).astype(bf16)
    route = route_ref[...]
    high = route.astype(bf16).astype(f32)
    middle = (route - high).astype(bf16).astype(f32)
    low = route - high - middle
    part = route.shape[1]
    row = lax.broadcasted_iota(jnp.int32, (TILE, part), 0)
    terms = jnp.where(row == 0, high, jnp.where(row == 1, middle, jnp.where(row == 2, low, 0.0)))
    terms = jnp.concatenate([terms, jnp.zeros((TILE, tokens - part), f32)], 1)
    out_ref[depth:] = terms.astype(bf16)


def features_kernel(*refs):
    hidden_refs, (own_ref, x_ref, z_ref) = refs[:HOLDERS], refs[HOLDERS : HOLDERS + 3]
    block_refs, centered_ref = refs[HOLDERS + 3 : 2 * HOLDERS + 3], refs[2 * HOLDERS + 3]
    route_ref, features_ref = refs[2 * HOLDERS + 4 :]
    depth, tokens = own_ref.shape[0], hidden_refs[0].shape[1]
    downs = (own_ref[...], x_ref[:depth], z_ref[:depth], z_ref[depth:])
    part = tokens // HOLDERS
    eye = lax.broadcasted_iota(jnp.int32, (part, part), 0) == lax.broadcasted_iota(
        jnp.int32, (part, part), 1
    )
    output = None
    for m, (hidden_ref, down) in enumerate(zip(hidden_refs, downs)):
        product = dot_f32(hidden_ref[:depth], down, (((0,), (0,)), ((), ())))
        output = product if output is None else output + product
        terms = hidden_ref[depth:, :part].astype(f32)
        route = jnp.sum(terms[:HOLDERS], axis=0, keepdims=True)
        column = jnp.sum(jnp.where(eye, route, 0.0), axis=1, keepdims=True)
        place = pl.multiple_of((holder() ^ m) * part, part)
        route_ref[pl.ds(place, part)] = jnp.broadcast_to(column, (part, LANES))
    features = (output * route_ref[:, :1]).astype(bf16)
    features_ref[...] = features
    wide = features.astype(f32)
    mean = jnp.sum(wide, axis=0, keepdims=True) / tokens
    column = jnp.sum(wide * mean, axis=1, keepdims=True)
    row = jnp.transpose(jnp.broadcast_to(column, (tokens, LANES)))[:1]
    gram = dot_f32(features, features, TRANSPOSED)
    centered = (gram - column - row + jnp.sum(mean * mean)).astype(bf16)
    at = 0
    for i in range(tokens // TILE):
        for j in range(tokens // LANES):
            centered_ref[at * TILE : (at + 1) * TILE] = centered[
                i * TILE : (i + 1) * TILE, j * LANES : (j + 1) * LANES
            ]
            at += 1
    for m, block_ref in enumerate(block_refs):
        block_ref[...] = features_ref[pl.ds(pl.multiple_of((holder() ^ m) * part, part), part)]


def place_kernel(*refs):
    blocks, out_ref, sems = refs[:HOLDERS], refs[HOLDERS], refs[HOLDERS + 1]
    width = blocks[0].shape[1]
    copies = []
    for m, block in enumerate(blocks):
        columns = pl.ds(pl.multiple_of((holder() ^ m) * width, width), width)
        copies.append(pltpu.make_async_copy(block, out_ref.at[:, columns], sems.at[m]))
        copies[-1].start()
    for copy in copies:
        copy.wait()


def pair_kernel(parts_ref, out_ref, flat_ref):
    copies, experts, _ = out_ref.shape
    parts = parts_ref[...].astype(f32)
    total = parts[:, 0]
    for holder in range(1, parts.shape[1]):
        total = total + parts[:, holder]
    flat_ref[...] = total.astype(bf16).astype(f32)
    lane = lax.broadcasted_iota(jnp.int32, (experts, experts), 1)

    def one(expert, table):
        products = jnp.sum(flat_ref[...] * flat_ref[pl.ds(expert, 1)], axis=1)
        return jnp.where(lane == expert, jnp.sum(products, axis=1, keepdims=True), table)

    table = lax.fori_loop(0, experts, one, jnp.zeros((experts, experts), f32), unroll=experts <= 8)
    for copy in range(copies):
        out_ref[copy] = table


def cka_kernel(tables_ref, out_ref):
    totals = jnp.sum(tables_ref[...], axis=0)
    shape = totals.shape
    eye = lax.broadcasted_iota(jnp.int32, shape, 0) == lax.broadcasted_iota(jnp.int32, shape, 1)
    kept = jnp.where(eye, totals, 0.0)
    down = jnp.sum(kept, axis=1, keepdims=True)
    across = jnp.sum(kept, axis=0, keepdims=True)
    out_ref[...] = totals / jnp.sqrt(down * across)


def shards(probe_states, norm_gain, gate_weight, up_weight, down_weight, route_weight):
    groups, members = lax.axis_size("grp"), lax.axis_size("tok")
    devices = groups * members
    experts = devices // HOLDERS
    rows, model = probe_states.shape
    tokens = rows * members
    depth = gate_weight.shape[0]
    part, token_part = model // HOLDERS, tokens // HOLDERS

    own, down_own, down_z, down_x = call(
        first_kernel,
        [jax.ShapeDtypeStruct((rows, model // 2), bf16)]
        + [jax.ShapeDtypeStruct((depth * n, part), bf16) for n in (1, 1, 2)],
        [HBM] * 3,
        [
            pltpu.with_memory_space_constraint(a, pltpu.HBM)
            for a in (probe_states, norm_gain[None, :], down_weight)
        ],
        scratch=[
            pltpu.VMEM((rows, model), bf16),
            pltpu.VMEM((1, model), f32),
            pltpu.SemaphoreType.DMA((2 + HOLDERS,)),
        ],
    )
    down_x = swapped(down_x, "tok", 1)
    order = (0, *range(members - 2, 0, -2))
    along = [swapped(own, "tok", m) if m else own for m in order]
    along = together(along, down_x)
    down_z = call(
        onward_kernel,
        jax.ShapeDtypeStruct(down_x.shape, bf16),
        [ANY, VMEM, VMEM],
        (along, down_z, down_x),
    )
    down_z = swapped(down_z, "tok", 2)
    across = swapped(along, "tok", 1)
    mine = call(
        functools.partial(stack_kernel, (*order, *(m + 1 for m in order))),
        jax.ShapeDtypeStruct((tokens, model // 2), bf16),
        [ANY, VMEM, VMEM],
        (down_z, along, across),
    )
    other = swapped(mine, "grp", 1)

    hidden = call(
        hidden_kernel,
        jax.ShapeDtypeStruct((depth + TILE, tokens), bf16),
        [VMEM] * 5,
        (mine, other, gate_weight, up_weight, route_weight),
    )
    hiddens = [swapped(hidden, "tok", m) if m else hidden for m in range(HOLDERS)]
    entries = tokens * tokens // LANES
    *blocks, centered = call(
        features_kernel,
        [jax.ShapeDtypeStruct((token_part, part), bf16)] * HOLDERS
        + [jax.ShapeDtypeStruct((entries, LANES), bf16)],
        [VMEM] * (HOLDERS + 3),
        (*hiddens, down_own, down_x, down_z),
        scratch=[pltpu.VMEM((tokens, LANES), f32), pltpu.VMEM((tokens, part), bf16)],
    )
    arrived = lax.all_to_all(centered, ("grp", "tok"), split_axis=0, concat_axis=0, tiled=True)
    arrived = arrived.reshape(experts, HOLDERS, entries // devices, LANES)
    direct = devices * experts * experts <= 1 << 16
    tables = call(
        pair_kernel,
        jax.ShapeDtypeStruct((devices if direct else 1, experts, experts), f32),
        [VMEM],
        (arrived,),
        scratch=[pltpu.VMEM((experts, entries // devices, LANES), f32)],
    )
    if direct:
        tables = lax.all_to_all(tables, ("grp", "tok"), split_axis=0, concat_axis=0, tiled=True)
    else:
        tables = lax.psum(tables, ("grp", "tok"))
    cka = call(cka_kernel, jax.ShapeDtypeStruct((experts, experts), f32), [VMEM], (tables,))

    blocks = [swapped(b, "tok", m) if m else b for m, b in enumerate(blocks)]
    features = call(
        place_kernel,
        jax.ShapeDtypeStruct((token_part, model), bf16),
        [VMEM] * HOLDERS,
        blocks,
        out_specs=ANY,
        scratch=[pltpu.SemaphoreType.DMA((HOLDERS,))],
    )
    return (features, cka)


def solution(mesh):
    return jax.shard_map(
        shards,
        mesh=mesh,
        in_specs=(
            P("tok", None),
            P(),
            P(("grp", "tok"), None),
            P(("grp", "tok"), None),
            P(("grp", "tok"), None),
            P(("grp", "tok"), None),
        ),
        out_specs=(P(("grp", "tok"), None), P()),
        check_vma=False,
    )
```

```python
import jax
import jax.numpy as jnp
from jax import lax
from jax.experimental import pallas as pl
from jax.experimental.pallas import tpu as pltpu
from jax.sharding import PartitionSpec as P

HOLDERS = 4
LANES = 128
TILE = 16
BIG = 24 * 1024 * 1024
TRANSPOSED = (((1,), (1,)), ((), ()))
VMEM = pl.BlockSpec(memory_space=pltpu.VMEM)
ANY = pl.BlockSpec(memory_space=pl.ANY)
HBM = pl.BlockSpec(memory_space=pltpu.HBM)
bf16 = jnp.bfloat16
f32 = jnp.float32


def swapped(array, axis, mask):
    return lax.ppermute(array, axis, [(i, i ^ mask) for i in range(lax.axis_size(axis))])


def dot_f32(a, b, dims):
    return lax.dot_general(a, b, dims, preferred_element_type=f32)


def call(body, outs, in_specs, operands, out_specs=None, scratch=(), aliases={}):
    return pl.pallas_call(
        body,
        out_shape=outs,
        in_specs=in_specs,
        out_specs=jax.tree.map(lambda _: VMEM, outs) if out_specs is None else out_specs,
        scratch_shapes=list(scratch),
        compiler_params=pltpu.CompilerParams(vmem_limit_bytes=BIG),
        input_output_aliases=aliases,
    )(*operands)


def core():
    return lax.axis_index("grp") & 1


def holder():
    return lax.axis_index("tok") & (HOLDERS - 1)


def first_kernel(states_hbm, gain_hbm, down_hbm, out_ref, own_ref, z_ref, x_ref, states_ref, gain_ref, sems):
    depth, width = own_ref.shape
    blocks = (own_ref, x_ref.at[pl.ds(0, depth)], z_ref, x_ref.at[pl.ds(depth, depth)])
    copies = [
        pltpu.make_async_copy(states_hbm, states_ref, sems.at[0]),
        pltpu.make_async_copy(gain_hbm, gain_ref, sems.at[1]),
    ]
    for m, block in enumerate(blocks):
        columns = pl.ds(pl.multiple_of((holder() ^ m) * width, width), width)
        copies.append(pltpu.make_async_copy(down_hbm.at[:, columns], block, sems.at[2 + m]))
    for copy in copies:
        copy.start()
    for copy in copies[:2]:
        copy.wait()
    states = states_ref[...].astype(f32)
    scale = lax.rsqrt(jnp.mean(states * states, axis=1, keepdims=True) + 1e-06)
    width = out_ref.shape[1]
    own = pl.ds(pl.multiple_of(core() * width, width), width)
    out_ref[...] = (states_ref[:, own].astype(f32) * scale * gain_ref[:, own]).astype(bf16)
    for copy in copies[2:]:
        copy.wait()


def onward_kernel(after_ref, own_ref, got_ref, out_ref):
    depth = own_ref.shape[0]
    out_ref[:depth] = own_ref[...]
    out_ref[depth:] = got_ref[depth:]


def stack_kernel(after_ref, *refs):
    rows = refs[0].shape[0]
    z = lax.axis_index("tok") >> 1
    for m, piece in enumerate(refs[:-1]):
        refs[-1][pl.ds(pl.multiple_of((z ^ m) * rows, rows), rows)] = piece[...]


def hidden_kernel(after_ref, near_ref, far_ref, near2_ref, far2_ref, gate_ref, up_ref, route_ref, out_ref):
    count, width = near_ref.shape
    depth = gate_ref.shape[0]
    x = lax.axis_index("tok") & 1
    own = pl.ds(pl.multiple_of(core() * width, width), width)
    rest = pl.ds(pl.multiple_of((1 - core()) * width, width), width)
    for at, block, block2 in ((x, near_ref[...], near2_ref[...]), (1 - x, far_ref[...], far2_ref[...])):
        gate, upward = [
            dot_f32(ref[:, own], block, TRANSPOSED) + dot_f32(ref[:, rest], block2, TRANSPOSED)
            for ref in (gate_ref, up_ref)
        ]
        place = pl.ds(pl.multiple_of(at * count, count), count)
        out_ref[:depth, place] = (gate / (1.0 + jnp.exp(-gate)) * upward).astype(bf16)
    route = route_ref[...]
    high = route.astype(bf16).astype(f32)
    middle = (route - high).astype(bf16).astype(f32)
    low = route - high - middle
    part = route.shape[1]
    row = lax.broadcasted_iota(jnp.int32, (TILE, part), 0)
    terms = jnp.where(row == 0, high, jnp.where(row == 1, middle, jnp.where(row == 2, low, 0.0)))
    terms = jnp.concatenate([terms, jnp.zeros((TILE, 2 * count - part), f32)], 1)
    out_ref[depth:] = terms.astype(bf16)


def features_kernel(*refs):
    hidden_refs, (own_ref, x_ref, z_ref) = refs[:HOLDERS], refs[HOLDERS : HOLDERS + 3]
    block_refs, centered_ref = refs[HOLDERS + 3 : 2 * HOLDERS + 3], refs[2 * HOLDERS + 3]
    route_ref, features_ref = refs[2 * HOLDERS + 4 :]
    depth, tokens = own_ref.shape[0], hidden_refs[0].shape[1]
    part, members = tokens // HOLDERS, lax.axis_size("tok")
    rows = tokens // members
    downs = (own_ref[...], x_ref[:depth], z_ref[:depth], z_ref[depth:])

    def place(m, piece):
        z = (holder() ^ m) * (members // HOLDERS // 2) + piece // 2
        return pl.ds(pl.multiple_of(piece % 2 * (tokens // 2) + z * rows, rows), rows)

    eye = lax.broadcasted_iota(jnp.int32, (part, part), 0) == lax.broadcasted_iota(
        jnp.int32, (part, part), 1
    )
    output = None
    for m, (hidden_ref, down) in enumerate(zip(hidden_refs, downs)):
        product = dot_f32(hidden_ref[:depth], down, (((0,), (0,)), ((), ())))
        output = product if output is None else output + product
        terms = hidden_ref[depth:, :part].astype(f32)
        route = jnp.sum(terms[:HOLDERS], axis=0, keepdims=True)
        column = jnp.sum(jnp.where(eye, route, 0.0), axis=1, keepdims=True)
        column = jnp.broadcast_to(column, (part, LANES))
        for piece in range(part // rows):
            route_ref[place(m, piece)] = column[piece * rows : (piece + 1) * rows]
    features = (output * route_ref[:, :1]).astype(bf16)
    features_ref[...] = features
    wide = features.astype(f32)
    mean = jnp.sum(wide, axis=0, keepdims=True) / tokens
    column = jnp.sum(wide * mean, axis=1, keepdims=True)
    row = jnp.transpose(jnp.broadcast_to(column, (tokens, LANES)))[:1]
    gram = dot_f32(features, features, TRANSPOSED)
    centered = (gram - column - row + jnp.sum(mean * mean)).astype(bf16)
    at = 0
    for i in range(tokens // TILE):
        for j in range(tokens // LANES):
            centered_ref[at * TILE : (at + 1) * TILE] = centered[
                i * TILE : (i + 1) * TILE, j * LANES : (j + 1) * LANES
            ]
            at += 1
    for m, block_ref in enumerate(block_refs):
        for piece in range(part // rows):
            block_ref[piece * rows : (piece + 1) * rows] = features_ref[place(m, piece)]


def place_kernel(*refs):
    blocks, out_ref, sems = refs[:HOLDERS], refs[HOLDERS], refs[HOLDERS + 1]
    width = blocks[0].shape[1]
    copies = []
    for m, block in enumerate(blocks):
        columns = pl.ds(pl.multiple_of((holder() ^ m) * width, width), width)
        copies.append(pltpu.make_async_copy(block, out_ref.at[:, columns], sems.at[m]))
        copies[-1].start()
    for copy in copies:
        copy.wait()


def pair_kernel(parts_ref, out_ref, flat_ref):
    copies, experts, _ = out_ref.shape
    parts = parts_ref[...].astype(f32)
    total = parts[:, 0]
    for holder in range(1, parts.shape[1]):
        total = total + parts[:, holder]
    flat_ref[...] = total.astype(bf16).astype(f32)
    lane = lax.broadcasted_iota(jnp.int32, (experts, experts), 1)

    def one(expert, table):
        products = jnp.sum(flat_ref[...] * flat_ref[pl.ds(expert, 1)], axis=1)
        return jnp.where(lane == expert, jnp.sum(products, axis=1, keepdims=True), table)

    table = lax.fori_loop(0, experts, one, jnp.zeros((experts, experts), f32), unroll=experts <= 8)
    for copy in range(copies):
        out_ref[copy] = table


def cka_kernel(tables_ref, out_ref):
    totals = jnp.sum(tables_ref[...], axis=0)
    shape = totals.shape
    eye = lax.broadcasted_iota(jnp.int32, shape, 0) == lax.broadcasted_iota(jnp.int32, shape, 1)
    kept = jnp.where(eye, totals, 0.0)
    down = jnp.sum(kept, axis=1, keepdims=True)
    across = jnp.sum(kept, axis=0, keepdims=True)
    out_ref[...] = totals / jnp.sqrt(down * across)


def shards(probe_states, norm_gain, gate_weight, up_weight, down_weight, route_weight):
    groups, members = lax.axis_size("grp"), lax.axis_size("tok")
    devices = groups * members
    experts = devices // HOLDERS
    rows, model = probe_states.shape
    tokens = rows * members
    depth = gate_weight.shape[0]
    part, token_part = model // HOLDERS, tokens // HOLDERS

    own, down_own, down_z, down_x = call(
        first_kernel,
        [jax.ShapeDtypeStruct((rows, model // 2), bf16)]
        + [jax.ShapeDtypeStruct((depth * n, part), bf16) for n in (1, 1, 2)],
        [HBM] * 3,
        [
            pltpu.with_memory_space_constraint(a, pltpu.HBM)
            for a in (probe_states, norm_gain[None, :], down_weight)
        ],
        scratch=[
            pltpu.VMEM((rows, model), bf16),
            pltpu.VMEM((1, model), f32),
            pltpu.SemaphoreType.DMA((2 + HOLDERS,)),
        ],
    )
    down_x = swapped(down_x, "tok", 1)
    pieces = [swapped(own, "tok", 2 * m) if m else own for m in range(members // 2)]
    near = call(
        stack_kernel,
        jax.ShapeDtypeStruct((tokens // 2, model // 2), bf16),
        [ANY] + [VMEM] * len(pieces),
        (down_x, *pieces),
    )
    down_z = call(
        onward_kernel,
        jax.ShapeDtypeStruct(down_x.shape, bf16),
        [ANY, VMEM, VMEM],
        (near, down_z, down_x),
    )
    far = swapped(near, "tok", 1)
    down_z = swapped(down_z, "tok", 2)
    hidden = call(
        hidden_kernel,
        jax.ShapeDtypeStruct((depth + TILE, tokens), bf16),
        [ANY] + [VMEM] * 7,
        (
            down_z,
            near,
            far,
            swapped(near, "grp", 1),
            swapped(far, "grp", 1),
            gate_weight,
            up_weight,
            route_weight,
        ),
    )
    hiddens = [swapped(hidden, "tok", m) if m else hidden for m in range(HOLDERS)]
    entries = tokens * tokens // LANES
    *blocks, centered = call(
        features_kernel,
        [jax.ShapeDtypeStruct((token_part, part), bf16)] * HOLDERS
        + [jax.ShapeDtypeStruct((entries, LANES), bf16)],
        [VMEM] * (HOLDERS + 3),
        (*hiddens, down_own, down_x, down_z),
        scratch=[pltpu.VMEM((tokens, LANES), f32), pltpu.VMEM((tokens, part), bf16)],
    )
    arrived = lax.all_to_all(centered, ("grp", "tok"), split_axis=0, concat_axis=0, tiled=True)
    arrived = arrived.reshape(experts, HOLDERS, entries // devices, LANES)
    direct = devices * experts * experts <= 1 << 16
    tables = call(
        pair_kernel,
        jax.ShapeDtypeStruct((devices if direct else 1, experts, experts), f32),
        [VMEM],
        (arrived,),
        scratch=[pltpu.VMEM((experts, entries // devices, LANES), f32)],
    )
    if direct:
        tables = lax.all_to_all(tables, ("grp", "tok"), split_axis=0, concat_axis=0, tiled=True)
    else:
        tables = lax.psum(tables, ("grp", "tok"))
    cka = call(cka_kernel, jax.ShapeDtypeStruct((experts, experts), f32), [VMEM], (tables,))

    blocks = [swapped(b, "tok", m) if m else b for m, b in enumerate(blocks)]
    features = call(
        place_kernel,
        jax.ShapeDtypeStruct((token_part, model), bf16),
        [VMEM] * HOLDERS,
        blocks,
        out_specs=ANY,
        scratch=[pltpu.SemaphoreType.DMA((HOLDERS,))],
    )
    return (features, cka)


def solution(mesh):
    return jax.shard_map(
        shards,
        mesh=mesh,
        in_specs=(
            P("tok", None),
            P(),
            P(("grp", "tok"), None),
            P(("grp", "tok"), None),
            P(("grp", "tok"), None),
            P(("grp", "tok"), None),
        ),
        out_specs=(P(("grp", "tok"), None), P()),
        check_vma=False,
    )
```

```python
import jax
import jax.numpy as jnp
from jax import lax
from jax.experimental import pallas as pl
from jax.experimental.pallas import tpu as pltpu
from jax.sharding import PartitionSpec as P

HOLDERS = 4
LANES = 128
TILE = 16
BIG = 24 * 1024 * 1024
TRANSPOSED = (((1,), (1,)), ((), ()))
VMEM = pl.BlockSpec(memory_space=pltpu.VMEM)
ANY = pl.BlockSpec(memory_space=pl.ANY)
HBM = pl.BlockSpec(memory_space=pltpu.HBM)
bf16 = jnp.bfloat16
f32 = jnp.float32


def swapped(array, axis, mask):
    return lax.ppermute(array, axis, [(i, i ^ mask) for i in range(lax.axis_size(axis))])


def dot_f32(a, b, dims):
    return lax.dot_general(a, b, dims, preferred_element_type=f32)


def call(body, outs, in_specs, operands, out_specs=None, scratch=(), aliases={}):
    return pl.pallas_call(
        body,
        out_shape=outs,
        in_specs=in_specs,
        out_specs=jax.tree.map(lambda _: VMEM, outs) if out_specs is None else out_specs,
        scratch_shapes=list(scratch),
        compiler_params=pltpu.CompilerParams(vmem_limit_bytes=BIG),
        input_output_aliases=aliases,
    )(*operands)


def core():
    return lax.axis_index("grp") & 1


def holder():
    return lax.axis_index("tok") & (HOLDERS - 1)


def first_kernel(states_hbm, gain_hbm, down_hbm, out_ref, own_ref, z_ref, x_ref, states_ref, gain_ref, sems):
    depth, width = own_ref.shape
    blocks = (own_ref, x_ref.at[pl.ds(0, depth)], z_ref, x_ref.at[pl.ds(depth, depth)])
    copies = [
        pltpu.make_async_copy(states_hbm, states_ref, sems.at[0]),
        pltpu.make_async_copy(gain_hbm, gain_ref, sems.at[1]),
    ]
    for m, block in enumerate(blocks):
        columns = pl.ds(pl.multiple_of((holder() ^ m) * width, width), width)
        copies.append(pltpu.make_async_copy(down_hbm.at[:, columns], block, sems.at[2 + m]))
    for copy in copies:
        copy.start()
    for copy in copies[:2]:
        copy.wait()
    states = states_ref[...].astype(f32)
    scale = lax.rsqrt(jnp.mean(states * states, axis=1, keepdims=True) + 1e-06)
    width = out_ref.shape[1]
    own = pl.ds(pl.multiple_of(core() * width, width), width)
    out_ref[...] = (states_ref[:, own].astype(f32) * scale * gain_ref[:, own]).astype(bf16)
    for copy in copies[2:]:
        copy.wait()


def onward_kernel(after_ref, own_ref, got_ref, out_ref):
    depth = own_ref.shape[0]
    out_ref[:depth] = own_ref[...]
    out_ref[depth:] = got_ref[depth:]


def stack_kernel(after_ref, *refs):
    rows = refs[0].shape[0]
    z = lax.axis_index("tok") >> 1
    for m, piece in enumerate(refs[:-1]):
        refs[-1][pl.ds(pl.multiple_of((z ^ m) * rows, rows), rows)] = piece[...]


def hidden_kernel(after_ref, near_ref, far_ref, near2_ref, far2_ref, gate_ref, up_ref, route_ref, out_ref):
    count, width = near_ref.shape
    depth = gate_ref.shape[0]
    x = lax.axis_index("tok") & 1
    own = pl.ds(pl.multiple_of(core() * width, width), width)
    rest = pl.ds(pl.multiple_of((1 - core()) * width, width), width)
    for at, block, block2 in ((x, near_ref[...], near2_ref[...]), (1 - x, far_ref[...], far2_ref[...])):
        gate, upward = [
            dot_f32(ref[:, own], block, TRANSPOSED) + dot_f32(ref[:, rest], block2, TRANSPOSED)
            for ref in (gate_ref, up_ref)
        ]
        place = pl.ds(pl.multiple_of(at * count, count), count)
        out_ref[:depth, place] = (gate / (1.0 + jnp.exp(-gate)) * upward).astype(bf16)
    route = route_ref[...]
    high = route.astype(bf16).astype(f32)
    middle = (route - high).astype(bf16).astype(f32)
    low = route - high - middle
    part = route.shape[1]
    row = lax.broadcasted_iota(jnp.int32, (TILE, part), 0)
    terms = jnp.where(row == 0, high, jnp.where(row == 1, middle, jnp.where(row == 2, low, 0.0)))
    terms = jnp.concatenate([terms, jnp.zeros((TILE, 2 * count - part), f32)], 1)
    out_ref[depth:] = terms.astype(bf16)


def features_kernel(gathered, *refs):
    hidden_refs, (own_ref, x_ref, z_ref) = refs[:HOLDERS], refs[HOLDERS : HOLDERS + 3]
    block_refs, centered_refs = refs[HOLDERS + 3 : 2 * HOLDERS + 3], refs[2 * HOLDERS + 3 : -3]
    route_ref, features_ref, whole_ref = refs[-3:]
    depth, tokens = own_ref.shape[0], hidden_refs[0].shape[1]
    part, members = tokens // HOLDERS, lax.axis_size("tok")
    rows = tokens // members
    downs = (own_ref[...], x_ref[:depth], z_ref[:depth], z_ref[depth:])

    def place(m, piece):
        z = (holder() ^ m) * (members // HOLDERS // 2) + piece // 2
        return pl.ds(pl.multiple_of(piece % 2 * (tokens // 2) + z * rows, rows), rows)

    eye = lax.broadcasted_iota(jnp.int32, (part, part), 0) == lax.broadcasted_iota(
        jnp.int32, (part, part), 1
    )
    output = None
    for m, (hidden_ref, down) in enumerate(zip(hidden_refs, downs)):
        product = dot_f32(hidden_ref[:depth], down, (((0,), (0,)), ((), ())))
        output = product if output is None else output + product
        terms = hidden_ref[depth:, :part].astype(f32)
        route = jnp.sum(terms[:HOLDERS], axis=0, keepdims=True)
        column = jnp.sum(jnp.where(eye, route, 0.0), axis=1, keepdims=True)
        column = jnp.broadcast_to(column, (part, LANES))
        for piece in range(part // rows):
            route_ref[place(m, piece)] = column[piece * rows : (piece + 1) * rows]
    features = (output * route_ref[:, :1]).astype(bf16)
    features_ref[...] = features
    wide = features.astype(f32)
    mean = jnp.sum(wide, axis=0, keepdims=True) / tokens
    column = jnp.sum(wide * mean, axis=1, keepdims=True)
    row = jnp.transpose(jnp.broadcast_to(column, (tokens, LANES)))[:1]
    gram = dot_f32(features, features, TRANSPOSED)
    centered = gram - column - row + jnp.sum(mean * mean)
    if gathered:
        whole_ref[...] = centered.astype(bf16)
        half = tokens // 2
        count = half // HOLDERS
        for m, centered_ref in enumerate(centered_refs):
            first = (holder() ^ m) * count
            for at, (row, left) in enumerate(((0, 0), (0, half), (half, half))):
                rows_there = pl.ds(pl.multiple_of(first + row, count), count)
                centered_ref[at * count : (at + 1) * count] = whole_ref[rows_there, left : left + half]
    else:
        (centered_ref,) = centered_refs
        centered = centered.astype(bf16)
        at = 0
        for i in range(tokens // TILE):
            for j in range(tokens // LANES):
                centered_ref[at * TILE : (at + 1) * TILE] = centered[
                    i * TILE : (i + 1) * TILE, j * LANES : (j + 1) * LANES
                ]
                at += 1
    for m, block_ref in enumerate(block_refs):
        for piece in range(part // rows):
            block_ref[piece * rows : (piece + 1) * rows] = features_ref[place(m, piece)]


def place_kernel(*refs):
    blocks, out_ref, sems = refs[:HOLDERS], refs[HOLDERS], refs[HOLDERS + 1]
    width = blocks[0].shape[1]
    copies = []
    for m, block in enumerate(blocks):
        columns = pl.ds(pl.multiple_of((holder() ^ m) * width, width), width)
        copies.append(pltpu.make_async_copy(block, out_ref.at[:, columns], sems.at[m]))
        copies[-1].start()
    for copy in copies:
        copy.wait()


def sum_kernel(*refs):
    total = refs[0][...].astype(f32)
    for ref in refs[1:-1]:
        total = total + ref[...].astype(f32)
    refs[-1][...] = total.astype(bf16)


def join_kernel(*refs):
    low_ref, high_ref, out_ref = refs[-3:]
    rows = low_ref.shape[0]
    out_ref[:rows] = low_ref[...]
    out_ref[rows:] = high_ref[...]


def table_of(flat_ref, experts, weighted):
    lane = lax.broadcasted_iota(jnp.int32, (experts, experts), 1)

    def one(expert, table):
        products = jnp.sum(weighted * flat_ref[pl.ds(expert, 1)], axis=1)
        return jnp.where(lane == expert, jnp.sum(products, axis=1, keepdims=True), table)

    return lax.fori_loop(0, experts, one, jnp.zeros((experts, experts), f32), unroll=experts <= 8)


def pair_kernel(distances, low_ref, high_ref, out_ref, flat_ref):
    experts, rows, _ = flat_ref.shape
    here = lax.axis_index("grp") * (lax.axis_size("tok") // HOLDERS) + lax.axis_index("tok") // HOLDERS
    for m in range(experts):
        ref, at = (low_ref, m) if m < experts // 2 else (high_ref, m - experts // 2)
        block = ref[at * rows : (at + 1) * rows].astype(f32)
        flat_ref[pl.ds(here ^ distances[m], 1)] = block[None]
    row = lax.broadcasted_iota(jnp.int32, flat_ref.shape, 1) // (rows // 3)
    flat = flat_ref[...]
    out_ref[...] = table_of(flat_ref, experts, jnp.where(row == 1, 2.0 * flat, flat))


def parts_kernel(parts_ref, out_ref, flat_ref):
    parts = parts_ref[...].astype(f32)
    total = parts[:, 0]
    for m in range(1, parts.shape[1]):
        total = total + parts[:, m]
    flat_ref[...] = total.astype(bf16).astype(f32)
    out_ref[...] = table_of(flat_ref, out_ref.shape[0], flat_ref[...])


def cka_kernel(*refs):
    tables, out_ref, kept_ref = refs[:-2], refs[-2], refs[-1]
    for m, table in enumerate(tables):
        kept_ref[pl.ds(holder() ^ m if m or len(tables) > 1 else 0, 1)] = table[...][None]
    totals = jnp.sum(kept_ref[...], axis=0)
    shape = totals.shape
    eye = lax.broadcasted_iota(jnp.int32, shape, 0) == lax.broadcasted_iota(jnp.int32, shape, 1)
    diagonal = jnp.where(eye, totals, 0.0)
    down = jnp.sum(diagonal, axis=1, keepdims=True)
    across = jnp.sum(diagonal, axis=0, keepdims=True)
    out_ref[...] = totals / jnp.sqrt(down * across)


def hold_kernel(*refs):
    pass


def held(arrays, after):
    return call(
        hold_kernel,
        [jax.ShapeDtypeStruct(a.shape, a.dtype) for a in arrays],
        [ANY] * (len(arrays) + 1),
        (*arrays, after),
        out_specs=[ANY] * len(arrays),
        aliases={i: i for i in range(len(arrays))},
    )


def shards(probe_states, norm_gain, gate_weight, up_weight, down_weight, route_weight):
    groups, members = lax.axis_size("grp"), lax.axis_size("tok")
    devices = groups * members
    experts = devices // HOLDERS
    rows, model = probe_states.shape
    tokens = rows * members
    depth = gate_weight.shape[0]
    part, token_part = model // HOLDERS, tokens // HOLDERS

    own, down_own, down_z, down_x = call(
        first_kernel,
        [jax.ShapeDtypeStruct((rows, model // 2), bf16)]
        + [jax.ShapeDtypeStruct((depth * n, part), bf16) for n in (1, 1, 2)],
        [HBM] * 3,
        [
            pltpu.with_memory_space_constraint(a, pltpu.HBM)
            for a in (probe_states, norm_gain[None, :], down_weight)
        ],
        scratch=[
            pltpu.VMEM((rows, model), bf16),
            pltpu.VMEM((1, model), f32),
            pltpu.SemaphoreType.DMA((2 + HOLDERS,)),
        ],
    )
    down_x = swapped(down_x, "tok", 1)
    pieces = [swapped(own, "tok", 2 * m) if m else own for m in range(members // 2)]
    near = call(
        stack_kernel,
        jax.ShapeDtypeStruct((tokens // 2, model // 2), bf16),
        [ANY] + [VMEM] * len(pieces),
        (down_x, *pieces),
    )
    down_z = call(
        onward_kernel,
        jax.ShapeDtypeStruct(down_x.shape, bf16),
        [ANY, VMEM, VMEM],
        (near, down_z, down_x),
    )
    far = swapped(near, "tok", 1)
    down_z = swapped(down_z, "tok", 2)
    hidden = call(
        hidden_kernel,
        jax.ShapeDtypeStruct((depth + TILE, tokens), bf16),
        [ANY] + [VMEM] * 7,
        (
            down_z,
            near,
            far,
            swapped(near, "grp", 1),
            swapped(far, "grp", 1),
            gate_weight,
            up_weight,
            route_weight,
        ),
    )
    hiddens = [swapped(hidden, "tok", m) if m else hidden for m in range(HOLDERS)]
    half = tokens // 2
    part_shape = (3 * half // HOLDERS, half)
    gathered = experts * part_shape[0] * part_shape[1] <= 1 << 20
    entries = tokens * tokens // LANES
    outs = [part_shape] * HOLDERS if gathered else [(entries, LANES)]
    outcome = call(
        lambda *refs: features_kernel(gathered, *refs),
        [jax.ShapeDtypeStruct((token_part, part), bf16)] * HOLDERS
        + [jax.ShapeDtypeStruct(shape, bf16) for shape in outs],
        [VMEM] * (HOLDERS + 3),
        (*hiddens, down_own, down_x, down_z),
        scratch=[
            pltpu.VMEM((tokens, LANES), f32),
            pltpu.VMEM((tokens, part), bf16),
            pltpu.VMEM((tokens, tokens), bf16),
        ],
    )
    blocks, centered = outcome[:HOLDERS], outcome[HOLDERS:]
    table_shape = jax.ShapeDtypeStruct((experts, experts), f32)
    if gathered:
        centered = [swapped(c, "tok", m) if m else c for m, c in enumerate(centered)]
        low = call(
            sum_kernel, jax.ShapeDtypeStruct(part_shape, bf16), [VMEM] * HOLDERS, centered
        )
        blocks = held(blocks, low)
        blocks = [swapped(b, "tok", m) if m else b for m, b in enumerate(blocks)]
        steps = [("tok", 1 << b) for b in range(2, members.bit_length() - 1)]
        steps += [("grp", 1 << b) for b in range(groups.bit_length() - 2, -1, -1)]
        distances = [0]
        for at, (axis, mask) in enumerate(steps):
            away = mask // HOLDERS if axis == "tok" else mask * (members // HOLDERS)
            distances += [d ^ away for d in distances]
            high = swapped(low, axis, mask)
            if at < len(steps) - 1:
                joined = jax.ShapeDtypeStruct((2 * low.shape[0], half), bf16)
                after = blocks if at == len(steps) - 2 else []
                low = call(
                    join_kernel, joined, [ANY] * len(after) + [VMEM] * 2, (*after, low, high)
                )
        table = call(
            lambda *refs: pair_kernel(distances, *refs),
            table_shape,
            [VMEM] * 2,
            (low, high),
            scratch=[pltpu.VMEM((experts, *part_shape), f32)],
        )
        tables = [swapped(table, "tok", m) if m else table for m in range(HOLDERS)]
    else:
        blocks = [swapped(b, "tok", m) if m else b for m, b in enumerate(blocks)]
        arrived = lax.all_to_all(
            centered[0], ("grp", "tok"), split_axis=0, concat_axis=0, tiled=True
        )
        table = call(
            parts_kernel,
            table_shape,
            [VMEM],
            (arrived.reshape(experts, HOLDERS, entries // devices, LANES),),
            scratch=[pltpu.VMEM((experts, entries // devices, LANES), f32)],
        )
        tables = [lax.psum(table, ("grp", "tok"))]
    cka = call(
        cka_kernel,
        table_shape,
        [VMEM] * len(tables),
        tables,
        scratch=[pltpu.VMEM((len(tables), experts, experts), f32)],
    )

    features = call(
        place_kernel,
        jax.ShapeDtypeStruct((token_part, model), bf16),
        [VMEM] * HOLDERS,
        blocks,
        out_specs=ANY,
        scratch=[pltpu.SemaphoreType.DMA((HOLDERS,))],
    )
    return (features, cka)


def solution(mesh):
    return jax.shard_map(
        shards,
        mesh=mesh,
        in_specs=(
            P("tok", None),
            P(),
            P(("grp", "tok"), None),
            P(("grp", "tok"), None),
            P(("grp", "tok"), None),
            P(("grp", "tok"), None),
        ),
        out_specs=(P(("grp", "tok"), None), P()),
        check_vma=False,
    )
```

```python
import jax
import jax.numpy as jnp
from jax import lax
from jax.experimental import pallas as pl
from jax.experimental.pallas import tpu as pltpu
from jax.sharding import PartitionSpec as P

HOLDERS = 4
LANES = 128
TILE = 16
BIG = 24 * 1024 * 1024
TRANSPOSED = (((1,), (1,)), ((), ()))
VMEM = pl.BlockSpec(memory_space=pltpu.VMEM)
ANY = pl.BlockSpec(memory_space=pl.ANY)
HBM = pl.BlockSpec(memory_space=pltpu.HBM)
bf16 = jnp.bfloat16
f32 = jnp.float32


def swapped(array, axis, mask):
    return lax.ppermute(array, axis, [(i, i ^ mask) for i in range(lax.axis_size(axis))])


def dot_f32(a, b, dims):
    return lax.dot_general(a, b, dims, preferred_element_type=f32)


def call(body, outs, in_specs, operands, out_specs=None, scratch=(), aliases={}):
    return pl.pallas_call(
        body,
        out_shape=outs,
        in_specs=in_specs,
        out_specs=jax.tree.map(lambda _: VMEM, outs) if out_specs is None else out_specs,
        scratch_shapes=list(scratch),
        compiler_params=pltpu.CompilerParams(vmem_limit_bytes=BIG),
        input_output_aliases=aliases,
    )(*operands)


def core():
    return lax.axis_index("grp") & 1


def holder():
    return lax.axis_index("tok") & (HOLDERS - 1)


def first_kernel(states_hbm, gain_hbm, down_hbm, out_ref, own_ref, z_ref, x_ref, states_ref, gain_ref, sems):
    depth, width = own_ref.shape
    blocks = (own_ref, x_ref.at[pl.ds(0, depth)], z_ref, x_ref.at[pl.ds(depth, depth)])
    copies = [
        pltpu.make_async_copy(states_hbm, states_ref, sems.at[0]),
        pltpu.make_async_copy(gain_hbm, gain_ref, sems.at[1]),
    ]
    for m, block in enumerate(blocks):
        columns = pl.ds(pl.multiple_of((holder() ^ m) * width, width), width)
        copies.append(pltpu.make_async_copy(down_hbm.at[:, columns], block, sems.at[2 + m]))
    for copy in copies:
        copy.start()
    for copy in copies[:2]:
        copy.wait()
    states = states_ref[...].astype(f32)
    scale = lax.rsqrt(jnp.mean(states * states, axis=1, keepdims=True) + 1e-06)
    width = out_ref.shape[1]
    own = pl.ds(pl.multiple_of(core() * width, width), width)
    out_ref[...] = (states_ref[:, own].astype(f32) * scale * gain_ref[:, own]).astype(bf16)
    for copy in copies[2:]:
        copy.wait()


def onward_kernel(after_ref, own_ref, got_ref, out_ref):
    depth = own_ref.shape[0]
    out_ref[:depth] = own_ref[...]
    out_ref[depth:] = got_ref[depth:]


def stack_kernel(after_ref, *refs):
    rows = refs[0].shape[0]
    z = lax.axis_index("tok") >> 1
    for m, piece in enumerate(refs[:-1]):
        refs[-1][pl.ds(pl.multiple_of((z ^ m) * rows, rows), rows)] = piece[...]


def hidden_kernel(after_ref, near_ref, far_ref, near2_ref, far2_ref, gate_ref, up_ref, route_ref, out_ref):
    count, width = near_ref.shape
    depth = gate_ref.shape[0]
    x = lax.axis_index("tok") & 1
    own = pl.ds(pl.multiple_of(core() * width, width), width)
    rest = pl.ds(pl.multiple_of((1 - core()) * width, width), width)
    for at, block, block2 in ((x, near_ref[...], near2_ref[...]), (1 - x, far_ref[...], far2_ref[...])):
        gate, upward = [
            dot_f32(ref[:, own], block, TRANSPOSED) + dot_f32(ref[:, rest], block2, TRANSPOSED)
            for ref in (gate_ref, up_ref)
        ]
        place = pl.ds(pl.multiple_of(at * count, count), count)
        out_ref[:depth, place] = (gate / (1.0 + jnp.exp(-gate)) * upward).astype(bf16)
    route = route_ref[...]
    high = route.astype(bf16).astype(f32)
    middle = (route - high).astype(bf16).astype(f32)
    low = route - high - middle
    part = route.shape[1]
    row = lax.broadcasted_iota(jnp.int32, (TILE, part), 0)
    terms = jnp.where(row == 0, high, jnp.where(row == 1, middle, jnp.where(row == 2, low, 0.0)))
    terms = jnp.concatenate([terms, jnp.zeros((TILE, 2 * count - part), f32)], 1)
    out_ref[depth:] = terms.astype(bf16)


def features_kernel(gathered, *refs):
    hidden_refs, (own_ref, x_ref, z_ref) = refs[:HOLDERS], refs[HOLDERS : HOLDERS + 3]
    kept_ref, z_ref2, x_ref2 = refs[HOLDERS + 3 : HOLDERS + 6]
    centered_refs, (route_ref, features_ref, whole_ref) = refs[HOLDERS + 6 : -3], refs[-3:]
    depth, tokens = own_ref.shape[0], hidden_refs[0].shape[1]
    part, members = tokens // HOLDERS, lax.axis_size("tok")
    rows = tokens // members
    downs = (own_ref[...], x_ref[:depth], z_ref[:depth], z_ref[depth:])

    def place(m, piece):
        z = (holder() ^ m) * (members // HOLDERS // 2) + piece // 2
        return pl.ds(pl.multiple_of(piece % 2 * (tokens // 2) + z * rows, rows), rows)

    eye = lax.broadcasted_iota(jnp.int32, (part, part), 0) == lax.broadcasted_iota(
        jnp.int32, (part, part), 1
    )
    output = None
    for m, (hidden_ref, down) in enumerate(zip(hidden_refs, downs)):
        product = dot_f32(hidden_ref[:depth], down, (((0,), (0,)), ((), ())))
        output = product if output is None else output + product
        terms = hidden_ref[depth:, :part].astype(f32)
        route = jnp.sum(terms[:HOLDERS], axis=0, keepdims=True)
        column = jnp.sum(jnp.where(eye, route, 0.0), axis=1, keepdims=True)
        column = jnp.broadcast_to(column, (part, LANES))
        for piece in range(part // rows):
            route_ref[place(m, piece)] = column[piece * rows : (piece + 1) * rows]
    features = (output * route_ref[:, :1]).astype(bf16)
    features_ref[...] = features
    wide = features.astype(f32)
    mean = jnp.sum(wide, axis=0, keepdims=True) / tokens
    column = jnp.sum(wide * mean, axis=1, keepdims=True)
    row = jnp.transpose(jnp.broadcast_to(column, (tokens, LANES)))[:1]
    gram = dot_f32(features, features, TRANSPOSED)
    centered = gram - column - row + jnp.sum(mean * mean)
    if gathered:
        whole_ref[...] = centered.astype(bf16)
        half = tokens // 2
        count = half // HOLDERS
        for m in range(HOLDERS):
            first = (holder() ^ m) * count
            for at, (row, left) in enumerate(((0, 0), (0, half), (half, half))):
                rows_there = pl.ds(pl.multiple_of(first + row, count), count)
                at += 3 * (m // 2)
                centered_refs[m % 2][at * count : (at + 1) * count] = whole_ref[
                    rows_there, left : left + half
                ]
    else:
        (centered_ref,) = centered_refs
        centered = centered.astype(bf16)
        at = 0
        for i in range(tokens // TILE):
            for j in range(tokens // LANES):
                centered_ref[at * TILE : (at + 1) * TILE] = centered[
                    i * TILE : (i + 1) * TILE, j * LANES : (j + 1) * LANES
                ]
                at += 1
    for block_ref, distances in ((kept_ref, (0,)), (z_ref2, (2,)), (x_ref2, (1, 3))):
        for at, m in enumerate(distances):
            for piece in range(part // rows):
                top = at * part + piece * rows
                block_ref[top : top + rows] = features_ref[place(m, piece)]


def place_kernel(kept_ref, x_ref, z_ref, out_ref, sems):
    rows, width = kept_ref.shape
    top, bottom = pl.ds(0, rows), pl.ds(rows, rows)
    blocks = (kept_ref, x_ref.at[top], z_ref.at[top], z_ref.at[bottom])
    copies = []
    for m, block in enumerate(blocks):
        columns = pl.ds(pl.multiple_of((holder() ^ m) * width, width), width)
        copies.append(pltpu.make_async_copy(block, out_ref.at[:, columns], sems.at[m]))
        copies[-1].start()
    for copy in copies:
        copy.wait()


def fold_kernel(own_ref, got_ref, kept_ref, sent_ref):
    rows = kept_ref.shape[0]
    total = own_ref[...].astype(f32) + got_ref[...].astype(f32)
    kept_ref[...] = total[:rows]
    sent_ref[...] = total[rows:]


def sum_kernel(own_ref, got_ref, out_ref):
    out_ref[...] = (own_ref[...] + got_ref[...]).astype(out_ref.dtype)


def join_kernel(low_ref, high_ref, out_ref):
    rows = low_ref.shape[0]
    out_ref[:rows] = low_ref[...]
    out_ref[rows:] = high_ref[...]


def table_of(flat_ref, experts, weighted):
    lane = lax.broadcasted_iota(jnp.int32, (experts, experts), 1)

    def one(expert, table):
        products = jnp.sum(weighted * flat_ref[pl.ds(expert, 1)], axis=1)
        return jnp.where(lane == expert, jnp.sum(products, axis=1, keepdims=True), table)

    return lax.fori_loop(0, experts, one, jnp.zeros((experts, experts), f32), unroll=experts <= 8)


def pair_kernel(distances, after_ref, low_ref, high_ref, out_ref, flat_ref):
    experts, rows, _ = flat_ref.shape
    here = lax.axis_index("grp") * (lax.axis_size("tok") // HOLDERS) + lax.axis_index("tok") // HOLDERS
    for m in range(experts):
        ref, at = (low_ref, m) if m < experts // 2 else (high_ref, m - experts // 2)
        block = ref[at * rows : (at + 1) * rows].astype(f32)
        flat_ref[pl.ds(here ^ distances[m], 1)] = block[None]
    row = lax.broadcasted_iota(jnp.int32, flat_ref.shape, 1) // (rows // 3)
    flat = flat_ref[...]
    out_ref[...] = table_of(flat_ref, experts, jnp.where(row == 1, 2.0 * flat, flat))


def parts_kernel(parts_ref, out_ref, flat_ref):
    parts = parts_ref[...].astype(f32)
    total = parts[:, 0]
    for m in range(1, parts.shape[1]):
        total = total + parts[:, m]
    flat_ref[...] = total.astype(bf16).astype(f32)
    out_ref[...] = table_of(flat_ref, out_ref.shape[0], flat_ref[...])


def cka_kernel(*refs):
    totals = refs[0][...]
    for ref in refs[1:-1]:
        totals = totals + ref[...]
    shape = totals.shape
    eye = lax.broadcasted_iota(jnp.int32, shape, 0) == lax.broadcasted_iota(jnp.int32, shape, 1)
    diagonal = jnp.where(eye, totals, 0.0)
    down = jnp.sum(diagonal, axis=1, keepdims=True)
    across = jnp.sum(diagonal, axis=0, keepdims=True)
    refs[-1][...] = totals / jnp.sqrt(down * across)


def hold_kernel(*refs):
    pass


def held(arrays, after):
    return call(
        hold_kernel,
        [jax.ShapeDtypeStruct(a.shape, a.dtype) for a in arrays],
        [ANY] * (len(arrays) + 1),
        (*arrays, after),
        out_specs=[ANY] * len(arrays),
        aliases={i: i for i in range(len(arrays))},
    )


def shards(probe_states, norm_gain, gate_weight, up_weight, down_weight, route_weight):
    groups, members = lax.axis_size("grp"), lax.axis_size("tok")
    devices = groups * members
    experts = devices // HOLDERS
    rows, model = probe_states.shape
    tokens = rows * members
    depth = gate_weight.shape[0]
    part, token_part = model // HOLDERS, tokens // HOLDERS

    own, down_own, down_z, down_x = call(
        first_kernel,
        [jax.ShapeDtypeStruct((rows, model // 2), bf16)]
        + [jax.ShapeDtypeStruct((depth * n, part), bf16) for n in (1, 1, 2)],
        [HBM] * 3,
        [
            pltpu.with_memory_space_constraint(a, pltpu.HBM)
            for a in (probe_states, norm_gain[None, :], down_weight)
        ],
        scratch=[
            pltpu.VMEM((rows, model), bf16),
            pltpu.VMEM((1, model), f32),
            pltpu.SemaphoreType.DMA((2 + HOLDERS,)),
        ],
    )
    down_x = swapped(down_x, "tok", 1)
    pieces = [swapped(own, "tok", 2 * m) if m else own for m in range(members // 2)]
    near = call(
        stack_kernel,
        jax.ShapeDtypeStruct((tokens // 2, model // 2), bf16),
        [ANY] + [VMEM] * len(pieces),
        (down_x, *pieces),
    )
    down_z = call(
        onward_kernel,
        jax.ShapeDtypeStruct(down_x.shape, bf16),
        [ANY, VMEM, VMEM],
        (near, down_z, down_x),
    )
    far = swapped(near, "tok", 1)
    down_z = swapped(down_z, "tok", 2)
    hidden = call(
        hidden_kernel,
        jax.ShapeDtypeStruct((depth + TILE, tokens), bf16),
        [ANY] + [VMEM] * 7,
        (
            down_z,
            near,
            far,
            swapped(near, "grp", 1),
            swapped(far, "grp", 1),
            gate_weight,
            up_weight,
            route_weight,
        ),
    )
    hiddens = [swapped(hidden, "tok", m) if m else hidden for m in range(HOLDERS)]
    half = tokens // 2
    part_shape = (3 * half // HOLDERS, half)
    gathered = experts * part_shape[0] * part_shape[1] <= 1 << 20
    entries = tokens * tokens // LANES
    both = (2 * part_shape[0], half)
    outs = [both] * 2 if gathered else [(entries, LANES)]
    kept, for_z, for_x, *centered = call(
        lambda *refs: features_kernel(gathered, *refs),
        [jax.ShapeDtypeStruct((token_part * n, part), bf16) for n in (1, 1, 2)]
        + [jax.ShapeDtypeStruct(shape, bf16) for shape in outs],
        [VMEM] * (HOLDERS + 3),
        (*hiddens, down_own, down_x, down_z),
        scratch=[
            pltpu.VMEM((tokens, LANES), f32),
            pltpu.VMEM((tokens, part), bf16),
            pltpu.VMEM((tokens, tokens), bf16),
        ],
    )

    def features_onward(got_x, after):
        out = jax.ShapeDtypeStruct(got_x.shape, bf16)
        return swapped(call(onward_kernel, out, [ANY, VMEM, VMEM], (after, for_z, got_x)), "tok", 2)

    table_shape = jax.ShapeDtypeStruct((experts, experts), f32)
    if gathered:
        ours, theirs = centered
        wide = jax.ShapeDtypeStruct(part_shape, f32)
        kept_part, sent_part = call(
            fold_kernel, [wide] * 2, [VMEM] * 2, (ours, swapped(theirs, "tok", 1))
        )
        low = call(
            sum_kernel,
            jax.ShapeDtypeStruct(part_shape, bf16),
            [VMEM] * 2,
            (kept_part, swapped(sent_part, "tok", 2)),
        )
        got_x = swapped(held([for_x], low)[0], "tok", 1)
        steps = [("tok", 1 << b) for b in range(2, members.bit_length() - 1)]
        steps += [("grp", 1 << b) for b in range(groups.bit_length() - 2, -1, -1)]
        distances = [0]
        for at, (axis, mask) in enumerate(steps):
            away = mask // HOLDERS if axis == "tok" else mask * (members // HOLDERS)
            distances += [d ^ away for d in distances]
            high = swapped(low, axis, mask)
            if at < len(steps) - 1:
                joined = jax.ShapeDtypeStruct((2 * low.shape[0], half), bf16)
                low = call(join_kernel, joined, [VMEM] * 2, (low, high))
                if at == 0:
                    got_z = features_onward(got_x, low)
        table = call(
            lambda *refs: pair_kernel(distances, *refs),
            table_shape,
            [ANY] + [VMEM] * 2,
            (got_z, low, high),
            scratch=[pltpu.VMEM((experts, *part_shape), f32)],
        )
        table = call(sum_kernel, table_shape, [VMEM] * 2, (table, swapped(table, "tok", 1)))
        tables = [table, swapped(table, "tok", 2)]
    else:
        got_x = swapped(for_x, "tok", 1)
        got_z = features_onward(got_x, kept)
        arrived = lax.all_to_all(
            centered[0], ("grp", "tok"), split_axis=0, concat_axis=0, tiled=True
        )
        table = call(
            parts_kernel,
            table_shape,
            [VMEM],
            (arrived.reshape(experts, HOLDERS, entries // devices, LANES),),
            scratch=[pltpu.VMEM((experts, entries // devices, LANES), f32)],
        )
        tables = [lax.psum(table, ("grp", "tok"))]
    cka = call(cka_kernel, table_shape, [VMEM] * len(tables), tables)

    features = call(
        place_kernel,
        jax.ShapeDtypeStruct((token_part, model), bf16),
        [VMEM] * 3,
        (kept, got_x, got_z),
        out_specs=ANY,
        scratch=[pltpu.SemaphoreType.DMA((HOLDERS,))],
    )
    return (features, cka)


def solution(mesh):
    return jax.shard_map(
        shards,
        mesh=mesh,
        in_specs=(
            P("tok", None),
            P(),
            P(("grp", "tok"), None),
            P(("grp", "tok"), None),
            P(("grp", "tok"), None),
            P(("grp", "tok"), None),
        ),
        out_specs=(P(("grp", "tok"), None), P()),
        check_vma=False,
    )
```

```python
import jax
import jax.numpy as jnp
from jax import lax
from jax.experimental import pallas as pl
from jax.experimental.pallas import tpu as pltpu
from jax.sharding import PartitionSpec as P

HOLDERS = 4
LANES = 128
TILE = 16
BIG = 24 * 1024 * 1024
TRANSPOSED = (((1,), (1,)), ((), ()))
VMEM = pl.BlockSpec(memory_space=pltpu.VMEM)
ANY = pl.BlockSpec(memory_space=pl.ANY)
HBM = pl.BlockSpec(memory_space=pltpu.HBM)
bf16 = jnp.bfloat16
f32 = jnp.float32


def swapped(array, axis, mask):
    return lax.ppermute(array, axis, [(i, i ^ mask) for i in range(lax.axis_size(axis))])


def dot_f32(a, b, dims):
    return lax.dot_general(a, b, dims, preferred_element_type=f32)


def call(body, outs, in_specs, operands, out_specs=None, scratch=(), aliases={}):
    return pl.pallas_call(
        body,
        out_shape=outs,
        in_specs=in_specs,
        out_specs=jax.tree.map(lambda _: VMEM, outs) if out_specs is None else out_specs,
        scratch_shapes=list(scratch),
        compiler_params=pltpu.CompilerParams(vmem_limit_bytes=BIG),
        input_output_aliases=aliases,
    )(*operands)


def core():
    return lax.axis_index("grp") & 1


def holder():
    return lax.axis_index("tok") & (HOLDERS - 1)


def first_kernel(states_hbm, gain_hbm, down_hbm, out_ref, own_ref, z_ref, x_ref, states_ref, gain_ref, sems):
    depth, width = own_ref.shape
    blocks = (own_ref, x_ref.at[pl.ds(0, depth)], z_ref, x_ref.at[pl.ds(depth, depth)])
    copies = [
        pltpu.make_async_copy(states_hbm, states_ref, sems.at[0]),
        pltpu.make_async_copy(gain_hbm, gain_ref, sems.at[1]),
    ]
    for m, block in enumerate(blocks):
        columns = pl.ds(pl.multiple_of((holder() ^ m) * width, width), width)
        copies.append(pltpu.make_async_copy(down_hbm.at[:, columns], block, sems.at[2 + m]))
    for copy in copies:
        copy.start()
    for copy in copies[:2]:
        copy.wait()
    states = states_ref[...].astype(f32)
    scale = lax.rsqrt(jnp.mean(states * states, axis=1, keepdims=True) + 1e-06)
    width = out_ref.shape[1]
    own = pl.ds(pl.multiple_of(core() * width, width), width)
    out_ref[...] = (states_ref[:, own].astype(f32) * scale * gain_ref[:, own]).astype(bf16)
    for copy in copies[2:]:
        copy.wait()


def onward_kernel(after_ref, own_ref, got_ref, out_ref):
    depth = own_ref.shape[0]
    out_ref[:depth] = own_ref[...]
    out_ref[depth:] = got_ref[depth:]


def stack_kernel(after_ref, *refs):
    rows = refs[0].shape[0]
    z = lax.axis_index("tok") >> 1
    for m, piece in enumerate(refs[:-1]):
        refs[-1][pl.ds(pl.multiple_of((z ^ m) * rows, rows), rows)] = piece[...]


def hidden_kernel(after_ref, near_ref, far_ref, near2_ref, far2_ref, gate_ref, up_ref, route_ref, out_ref):
    count, width = near_ref.shape
    depth = gate_ref.shape[0]
    x = lax.axis_index("tok") & 1
    own = pl.ds(pl.multiple_of(core() * width, width), width)
    rest = pl.ds(pl.multiple_of((1 - core()) * width, width), width)
    for at, block, block2 in ((x, near_ref[...], near2_ref[...]), (1 - x, far_ref[...], far2_ref[...])):
        gate, upward = [
            dot_f32(ref[:, own], block, TRANSPOSED) + dot_f32(ref[:, rest], block2, TRANSPOSED)
            for ref in (gate_ref, up_ref)
        ]
        place = pl.ds(pl.multiple_of(at * count, count), count)
        out_ref[:depth, place] = (gate / (1.0 + jnp.exp(-gate)) * upward).astype(bf16)
    route = route_ref[...]
    high = route.astype(bf16).astype(f32)
    middle = (route - high).astype(bf16).astype(f32)
    low = route - high - middle
    part = route.shape[1]
    row = lax.broadcasted_iota(jnp.int32, (TILE, part), 0)
    terms = jnp.where(row == 0, high, jnp.where(row == 1, middle, jnp.where(row == 2, low, 0.0)))
    terms = jnp.concatenate([terms, jnp.zeros((TILE, 2 * count - part), f32)], 1)
    out_ref[depth:] = terms.astype(bf16)


def features_kernel(shares, copies, *refs):
    hidden_refs, (own_ref, x_ref, z_ref) = refs[:HOLDERS], refs[HOLDERS : HOLDERS + 3]
    block_refs, centered_ref = refs[HOLDERS + 3 : 2 * HOLDERS + 3], refs[2 * HOLDERS + 3]
    route_ref, features_ref = refs[2 * HOLDERS + 4 :]
    depth, tokens = own_ref.shape[0], hidden_refs[0].shape[1]
    part, members = tokens // HOLDERS, lax.axis_size("tok")
    rows = tokens // members
    downs = (own_ref[...], x_ref[:depth], z_ref[:depth], z_ref[depth:])

    def place(m, piece):
        z = (holder() ^ m) * (members // HOLDERS // 2) + piece // 2
        return pl.ds(pl.multiple_of(piece % 2 * (tokens // 2) + z * rows, rows), rows)

    eye = lax.broadcasted_iota(jnp.int32, (part, part), 0) == lax.broadcasted_iota(
        jnp.int32, (part, part), 1
    )
    output = None
    for m, (hidden_ref, down) in enumerate(zip(hidden_refs, downs)):
        product = dot_f32(hidden_ref[:depth], down, (((0,), (0,)), ((), ())))
        output = product if output is None else output + product
        terms = hidden_ref[depth:, :part].astype(f32)
        route = jnp.sum(terms[:HOLDERS], axis=0, keepdims=True)
        column = jnp.sum(jnp.where(eye, route, 0.0), axis=1, keepdims=True)
        column = jnp.broadcast_to(column, (part, LANES))
        for piece in range(part // rows):
            route_ref[place(m, piece)] = column[piece * rows : (piece + 1) * rows]
    features = (output * route_ref[:, :1]).astype(bf16)
    features_ref[...] = features
    wide = features.astype(f32)
    mean = jnp.sum(wide, axis=0, keepdims=True) / tokens
    column = jnp.sum(wide * mean, axis=1, keepdims=True)
    row = jnp.transpose(jnp.broadcast_to(column, (tokens, LANES)))[:1]
    gram = dot_f32(features, features, TRANSPOSED)
    centered = (gram - column - row + jnp.sum(mean * mean)).astype(bf16)
    if copies > 1:
        count = tokens // (shares // members)
        for at in range(shares // members * copies):
            first = at // copies * count
            centered_ref[at * count : (at + 1) * count] = centered[first : first + count]
    else:
        at = 0
        for i in range(tokens // TILE):
            for j in range(tokens // LANES):
                centered_ref[at * TILE : (at + 1) * TILE] = centered[
                    i * TILE : (i + 1) * TILE, j * LANES : (j + 1) * LANES
                ]
                at += 1
    for m, block_ref in enumerate(block_refs):
        for piece in range(part // rows):
            block_ref[piece * rows : (piece + 1) * rows] = features_ref[place(m, piece)]


def place_kernel(*refs):
    blocks, out_ref, sems = refs[:HOLDERS], refs[HOLDERS], refs[HOLDERS + 1]
    width = blocks[0].shape[1]
    copies = []
    for m, block in enumerate(blocks):
        columns = pl.ds(pl.multiple_of((holder() ^ m) * width, width), width)
        copies.append(pltpu.make_async_copy(block, out_ref.at[:, columns], sems.at[m]))
        copies[-1].start()
    for copy in copies:
        copy.wait()


def pair_kernel(parts_ref, out_ref, flat_ref):
    copies, experts, _ = out_ref.shape
    parts = parts_ref[...].astype(f32)
    total = parts[:, 0]
    for holder in range(1, parts.shape[1]):
        total = total + parts[:, holder]
    flat_ref[...] = total.astype(bf16).astype(f32)
    lane = lax.broadcasted_iota(jnp.int32, (experts, experts), 1)

    def one(expert, table):
        products = jnp.sum(flat_ref[...] * flat_ref[pl.ds(expert, 1)], axis=1)
        return jnp.where(lane == expert, jnp.sum(products, axis=1, keepdims=True), table)

    table = lax.fori_loop(0, experts, one, jnp.zeros((experts, experts), f32), unroll=experts <= 8)
    for copy in range(copies):
        out_ref[copy] = table


def cka_kernel(tables_ref, out_ref):
    totals = jnp.sum(tables_ref[...], axis=0)
    shape = totals.shape
    eye = lax.broadcasted_iota(jnp.int32, shape, 0) == lax.broadcasted_iota(jnp.int32, shape, 1)
    kept = jnp.where(eye, totals, 0.0)
    down = jnp.sum(kept, axis=1, keepdims=True)
    across = jnp.sum(kept, axis=0, keepdims=True)
    out_ref[...] = totals / jnp.sqrt(down * across)


def shards(probe_states, norm_gain, gate_weight, up_weight, down_weight, route_weight):
    groups, members = lax.axis_size("grp"), lax.axis_size("tok")
    devices = groups * members
    experts = devices // HOLDERS
    rows, model = probe_states.shape
    tokens = rows * members
    depth = gate_weight.shape[0]
    part, token_part = model // HOLDERS, tokens // HOLDERS

    own, down_own, down_z, down_x = call(
        first_kernel,
        [jax.ShapeDtypeStruct((rows, model // 2), bf16)]
        + [jax.ShapeDtypeStruct((depth * n, part), bf16) for n in (1, 1, 2)],
        [HBM] * 3,
        [
            pltpu.with_memory_space_constraint(a, pltpu.HBM)
            for a in (probe_states, norm_gain[None, :], down_weight)
        ],
        scratch=[
            pltpu.VMEM((rows, model), bf16),
            pltpu.VMEM((1, model), f32),
            pltpu.SemaphoreType.DMA((2 + HOLDERS,)),
        ],
    )
    down_x = swapped(down_x, "tok", 1)
    pieces = [swapped(own, "tok", 2 * m) if m else own for m in range(members // 2)]
    near = call(
        stack_kernel,
        jax.ShapeDtypeStruct((tokens // 2, model // 2), bf16),
        [ANY] + [VMEM] * len(pieces),
        (down_x, *pieces),
    )
    down_z = call(
        onward_kernel,
        jax.ShapeDtypeStruct(down_x.shape, bf16),
        [ANY, VMEM, VMEM],
        (near, down_z, down_x),
    )
    far = swapped(near, "tok", 1)
    down_z = swapped(down_z, "tok", 2)
    hidden = call(
        hidden_kernel,
        jax.ShapeDtypeStruct((depth + TILE, tokens), bf16),
        [ANY] + [VMEM] * 7,
        (
            down_z,
            near,
            far,
            swapped(near, "grp", 1),
            swapped(far, "grp", 1),
            gate_weight,
            up_weight,
            route_weight,
        ),
    )
    hiddens = [swapped(hidden, "tok", m) if m else hidden for m in range(HOLDERS)]
    shared = devices * experts * experts <= 1 << 16 and tokens % (devices // 2 * TILE) == 0
    copies = 2 if shared else 1
    shares = devices // copies
    width = tokens if shared else LANES
    share_rows = tokens * tokens // shares // width
    *blocks, centered = call(
        lambda *refs: features_kernel(shares, copies, *refs),
        [jax.ShapeDtypeStruct((token_part, part), bf16)] * HOLDERS
        + [jax.ShapeDtypeStruct((devices * share_rows, width), bf16)],
        [VMEM] * (HOLDERS + 3),
        (*hiddens, down_own, down_x, down_z),
        scratch=[pltpu.VMEM((tokens, LANES), f32), pltpu.VMEM((tokens, part), bf16)],
    )
    arrived = lax.all_to_all(centered, ("grp", "tok"), split_axis=0, concat_axis=0, tiled=True)
    tables = call(
        pair_kernel,
        jax.ShapeDtypeStruct((shares if shared else 1, experts, experts), f32),
        [VMEM],
        (arrived.reshape(experts, HOLDERS, share_rows, width),),
        scratch=[pltpu.VMEM((experts, share_rows, width), f32)],
    )
    if shared:
        same = [
            [g * members + t for g in range(c, groups, copies) for t in range(members)]
            for c in range(copies)
        ]
        tables = lax.all_to_all(
            tables,
            ("grp", "tok"),
            split_axis=0,
            concat_axis=0,
            tiled=True,
            axis_index_groups=same,
        )
    else:
        tables = lax.psum(tables, ("grp", "tok"))
    cka = call(cka_kernel, jax.ShapeDtypeStruct((experts, experts), f32), [VMEM], (tables,))

    blocks = [swapped(b, "tok", m) if m else b for m, b in enumerate(blocks)]
    features = call(
        place_kernel,
        jax.ShapeDtypeStruct((token_part, model), bf16),
        [VMEM] * HOLDERS,
        blocks,
        out_specs=ANY,
        scratch=[pltpu.SemaphoreType.DMA((HOLDERS,))],
    )
    return (features, cka)


def solution(mesh):
    return jax.shard_map(
        shards,
        mesh=mesh,
        in_specs=(
            P("tok", None),
            P(),
            P(("grp", "tok"), None),
            P(("grp", "tok"), None),
            P(("grp", "tok"), None),
            P(("grp", "tok"), None),
        ),
        out_specs=(P(("grp", "tok"), None), P()),
        check_vma=False,
    )
```

```python
import jax
import jax.numpy as jnp
from jax import lax
from jax.experimental import pallas as pl
from jax.experimental.pallas import tpu as pltpu
from jax.sharding import PartitionSpec as P

HOLDERS = 4
LANES = 128
TILE = 16
BIG = 24 * 1024 * 1024
TRANSPOSED = (((1,), (1,)), ((), ()))
VMEM = pl.BlockSpec(memory_space=pltpu.VMEM)
ANY = pl.BlockSpec(memory_space=pl.ANY)
HBM = pl.BlockSpec(memory_space=pltpu.HBM)
bf16 = jnp.bfloat16
f32 = jnp.float32


def swapped(array, axis, mask):
    return lax.ppermute(array, axis, [(i, i ^ mask) for i in range(lax.axis_size(axis))])


def dot_f32(a, b, dims):
    return lax.dot_general(a, b, dims, preferred_element_type=f32)


def call(body, outs, in_specs, operands, out_specs=None, scratch=(), aliases={}):
    return pl.pallas_call(
        body,
        out_shape=outs,
        in_specs=in_specs,
        out_specs=jax.tree.map(lambda _: VMEM, outs) if out_specs is None else out_specs,
        scratch_shapes=list(scratch),
        compiler_params=pltpu.CompilerParams(vmem_limit_bytes=BIG),
        input_output_aliases=aliases,
    )(*operands)


def core():
    return lax.axis_index("grp") & 1


def holder():
    return lax.axis_index("tok") & (HOLDERS - 1)


def first_kernel(states_hbm, gain_hbm, down_hbm, out_ref, *refs):
    downs, (states_ref, gain_ref, sems) = refs[:HOLDERS], refs[HOLDERS:]
    copies = [
        pltpu.make_async_copy(states_hbm, states_ref, sems.at[0]),
        pltpu.make_async_copy(gain_hbm, gain_ref, sems.at[1]),
    ]
    width = downs[0].shape[1]
    for m, down_ref in enumerate(downs):
        columns = pl.ds(pl.multiple_of((holder() ^ m) * width, width), width)
        copies.append(pltpu.make_async_copy(down_hbm.at[:, columns], down_ref, sems.at[2 + m]))
    for copy in copies:
        copy.start()
    for copy in copies[:2]:
        copy.wait()
    states = states_ref[...].astype(f32)
    scale = lax.rsqrt(jnp.mean(states * states, axis=1, keepdims=True) + 1e-06)
    width = out_ref.shape[1]
    own = pl.ds(pl.multiple_of(core() * width, width), width)
    out_ref[...] = (states_ref[:, own].astype(f32) * scale * gain_ref[:, own]).astype(bf16)
    for copy in copies[2:]:
        copy.wait()


def hold_kernel(*refs):
    pass


def held(array, after):
    return call(
        hold_kernel,
        jax.ShapeDtypeStruct(array.shape, array.dtype),
        [ANY] * 2,
        (array, after),
        out_specs=ANY,
        aliases={0: 0},
    )


def stack_kernel(after_ref, after2_ref, *refs):
    rows = refs[0].shape[0]
    z = lax.axis_index("tok") >> 1
    for m, piece in enumerate(refs[:-1]):
        refs[-1][pl.ds(pl.multiple_of((z ^ m) * rows, rows), rows)] = piece[...]


def columns_of(half, width):
    return pl.ds(pl.multiple_of(half * width, width), width)


def gated(gate, upward):
    return (gate / (1.0 + jnp.exp(-gate)) * upward).astype(bf16)


def near_kernel(near_ref, near2_ref, far_ref, gate_ref, up_ref, route_ref, out_ref, gate_part_ref, up_part_ref):
    count, width = near_ref.shape
    depth = gate_ref.shape[0]
    own, rest = columns_of(core(), width), columns_of(1 - core(), width)
    near, near2, far = near_ref[...], near2_ref[...], far_ref[...]
    gate, upward = [
        dot_f32(ref[:, own], near, TRANSPOSED) + dot_f32(ref[:, rest], near2, TRANSPOSED)
        for ref in (gate_ref, up_ref)
    ]
    out_ref[:depth] = gated(gate, upward)
    route = route_ref[...]
    high = route.astype(bf16).astype(f32)
    middle = (route - high).astype(bf16).astype(f32)
    low = route - high - middle
    part = route.shape[1]
    row = lax.broadcasted_iota(jnp.int32, (TILE, part), 0)
    terms = jnp.where(row == 0, high, jnp.where(row == 1, middle, jnp.where(row == 2, low, 0.0)))
    terms = jnp.concatenate([terms, jnp.zeros((TILE, count - part), f32)], 1)
    out_ref[depth:] = terms.astype(bf16)
    gate_part_ref[...] = dot_f32(gate_ref[:, own], far, TRANSPOSED)
    up_part_ref[...] = dot_f32(up_ref[:, own], far, TRANSPOSED)


def far_kernel(far2_ref, gate_ref, up_ref, gate_part_ref, up_part_ref, out_ref):
    rest = columns_of(1 - core(), far2_ref.shape[1])
    far2 = far2_ref[...]
    gate, upward = [
        part_ref[...] + dot_f32(ref[:, rest], far2, TRANSPOSED)
        for ref, part_ref in ((gate_ref, gate_part_ref), (up_ref, up_part_ref))
    ]
    out_ref[...] = gated(gate, upward)


def features_kernel(*refs):
    near_refs, far_refs, down_refs = [refs[n * HOLDERS : (n + 1) * HOLDERS] for n in range(3)]
    block_refs, centered_ref = refs[3 * HOLDERS : 4 * HOLDERS], refs[4 * HOLDERS]
    route_ref, features_ref, whole_ref = refs[4 * HOLDERS + 1 :]
    depth, half = far_refs[0].shape
    tokens = 2 * half
    part, members = tokens // HOLDERS, lax.axis_size("tok")
    rows = tokens // members
    x = lax.axis_index("tok") & 1

    def place(m, piece):
        z = (holder() ^ m) * (members // HOLDERS // 2) + piece // 2
        return pl.ds(pl.multiple_of(piece % 2 * (tokens // 2) + z * rows, rows), rows)

    eye = lax.broadcasted_iota(jnp.int32, (part, part), 0) == lax.broadcasted_iota(
        jnp.int32, (part, part), 1
    )
    here = there = None
    for m in range(HOLDERS):
        near, far, down = near_refs[m][:depth], far_refs[m][...], down_refs[m][...]
        for_here, for_there = (far, near) if m & 1 else (near, far)
        for_here = dot_f32(for_here, down, (((0,), (0,)), ((), ())))
        for_there = dot_f32(for_there, down, (((0,), (0,)), ((), ())))
        here = for_here if m == 0 else here + for_here
        there = for_there if m == 0 else there + for_there
        terms = near_refs[m][depth:, :part].astype(f32)
        route = jnp.sum(terms[:HOLDERS], axis=0, keepdims=True)
        column = jnp.sum(jnp.where(eye, route, 0.0), axis=1, keepdims=True)
        column = jnp.broadcast_to(column, (part, LANES))
        for piece in range(part // rows):
            route_ref[place(m, piece)] = column[piece * rows : (piece + 1) * rows]
    for at, output in ((x, here), (1 - x, there)):
        at = pl.ds(pl.multiple_of(at * half, half), half)
        features_ref[at] = (output * route_ref[at][:, :1]).astype(bf16)
    features = features_ref[...]
    wide = features.astype(f32)
    mean = jnp.sum(wide, axis=0, keepdims=True) / tokens
    column = jnp.sum(wide * mean, axis=1, keepdims=True)
    row = jnp.transpose(jnp.broadcast_to(column, (tokens, LANES)))[:1]
    gram = dot_f32(features, features, TRANSPOSED)
    whole_ref[...] = (gram - column - row + jnp.sum(mean * mean)).astype(bf16)
    at = 0
    for i in range(tokens // TILE):
        for j in range(tokens // LANES):
            centered_ref[at * TILE : (at + 1) * TILE] = whole_ref[
                i * TILE : (i + 1) * TILE, j * LANES : (j + 1) * LANES
            ]
            at += 1
    for m, block_ref in enumerate(block_refs):
        for piece in range(part // rows):
            block_ref[piece * rows : (piece + 1) * rows] = features_ref[place(m, piece)]


def place_kernel(*refs):
    blocks, out_ref, sems = refs[:HOLDERS], refs[HOLDERS], refs[HOLDERS + 1]
    width = blocks[0].shape[1]
    copies = []
    for m, block in enumerate(blocks):
        columns = pl.ds(pl.multiple_of((holder() ^ m) * width, width), width)
        copies.append(pltpu.make_async_copy(block, out_ref.at[:, columns], sems.at[m]))
        copies[-1].start()
    for copy in copies:
        copy.wait()


def pair_kernel(parts_ref, out_ref, flat_ref):
    copies, experts, _ = out_ref.shape
    parts = parts_ref[...].astype(f32)
    total = parts[:, 0]
    for holder in range(1, parts.shape[1]):
        total = total + parts[:, holder]
    flat_ref[...] = total.astype(bf16).astype(f32)
    lane = lax.broadcasted_iota(jnp.int32, (experts, experts), 1)

    def one(expert, table):
        products = jnp.sum(flat_ref[...] * flat_ref[pl.ds(expert, 1)], axis=1)
        return jnp.where(lane == expert, jnp.sum(products, axis=1, keepdims=True), table)

    table = lax.fori_loop(0, experts, one, jnp.zeros((experts, experts), f32), unroll=experts <= 8)
    for copy in range(copies):
        out_ref[copy] = table


def cka_kernel(tables_ref, out_ref):
    totals = jnp.sum(tables_ref[...], axis=0)
    shape = totals.shape
    eye = lax.broadcasted_iota(jnp.int32, shape, 0) == lax.broadcasted_iota(jnp.int32, shape, 1)
    kept = jnp.where(eye, totals, 0.0)
    down = jnp.sum(kept, axis=1, keepdims=True)
    across = jnp.sum(kept, axis=0, keepdims=True)
    out_ref[...] = totals / jnp.sqrt(down * across)


def shards(probe_states, norm_gain, gate_weight, up_weight, down_weight, route_weight):
    groups, members = lax.axis_size("grp"), lax.axis_size("tok")
    devices = groups * members
    experts = devices // HOLDERS
    rows, model = probe_states.shape
    tokens = rows * members
    depth = gate_weight.shape[0]
    part, token_part = model // HOLDERS, tokens // HOLDERS

    own, *downs = call(
        first_kernel,
        [jax.ShapeDtypeStruct((rows, model // 2), bf16)]
        + [jax.ShapeDtypeStruct((depth, part), bf16)] * HOLDERS,
        [HBM] * 3,
        [
            pltpu.with_memory_space_constraint(a, pltpu.HBM)
            for a in (probe_states, norm_gain[None, :], down_weight)
        ],
        scratch=[
            pltpu.VMEM((rows, model), bf16),
            pltpu.VMEM((1, model), f32),
            pltpu.SemaphoreType.DMA((2 + HOLDERS,)),
        ],
    )
    down_x = swapped(downs[1], "tok", 1)
    pieces = [swapped(own, "tok", 2 * m) if m else own for m in range(members // 2)]
    down_z = swapped(downs[2], "tok", 2)
    near = call(
        stack_kernel,
        jax.ShapeDtypeStruct((tokens // 2, model // 2), bf16),
        [ANY] * 2 + [VMEM] * len(pieces),
        (down_x, down_z, *pieces),
    )
    far = swapped(near, "tok", 1)
    near2 = swapped(near, "grp", 1)
    down_xz = swapped(held(downs[3], near), "tok", 2)
    half_shape = jax.ShapeDtypeStruct((depth, tokens // 2), f32)
    near_hidden, gate_part, up_part = call(
        near_kernel,
        [jax.ShapeDtypeStruct((depth + TILE, tokens // 2), bf16), half_shape, half_shape],
        [VMEM] * 6,
        (near, near2, far, gate_weight, up_weight, route_weight),
    )
    near_hiddens = [swapped(near_hidden, "tok", m) if m else near_hidden for m in range(HOLDERS)]
    down_xz = swapped(held(down_xz, far), "tok", 1)
    far_hidden = call(
        far_kernel,
        jax.ShapeDtypeStruct((depth, tokens // 2), bf16),
        [VMEM] * 5,
        (swapped(far, "grp", 1), gate_weight, up_weight, gate_part, up_part),
    )
    far_hiddens = [swapped(far_hidden, "tok", m) if m else far_hidden for m in range(HOLDERS)]
    entries = tokens * tokens // LANES
    *blocks, centered = call(
        features_kernel,
        [jax.ShapeDtypeStruct((token_part, part), bf16)] * HOLDERS
        + [jax.ShapeDtypeStruct((entries, LANES), bf16)],
        [VMEM] * (3 * HOLDERS),
        (*near_hiddens, *far_hiddens, downs[0], down_x, down_z, down_xz),
        scratch=[
            pltpu.VMEM((tokens, LANES), f32),
            pltpu.VMEM((tokens, part), bf16),
            pltpu.VMEM((tokens, tokens), bf16),
        ],
    )
    arrived = lax.all_to_all(centered, ("grp", "tok"), split_axis=0, concat_axis=0, tiled=True)
    arrived = arrived.reshape(experts, HOLDERS, entries // devices, LANES)
    direct = devices * experts * experts <= 1 << 16
    tables = call(
        pair_kernel,
        jax.ShapeDtypeStruct((devices if direct else 1, experts, experts), f32),
        [VMEM],
        (arrived,),
        scratch=[pltpu.VMEM((experts, entries // devices, LANES), f32)],
    )
    if direct:
        tables = lax.all_to_all(tables, ("grp", "tok"), split_axis=0, concat_axis=0, tiled=True)
    else:
        tables = lax.psum(tables, ("grp", "tok"))
    cka = call(cka_kernel, jax.ShapeDtypeStruct((experts, experts), f32), [VMEM], (tables,))

    blocks = [swapped(b, "tok", m) if m else b for m, b in enumerate(blocks)]
    features = call(
        place_kernel,
        jax.ShapeDtypeStruct((token_part, model), bf16),
        [VMEM] * HOLDERS,
        blocks,
        out_specs=ANY,
        scratch=[pltpu.SemaphoreType.DMA((HOLDERS,))],
    )
    return (features, cka)


def solution(mesh):
    return jax.shard_map(
        shards,
        mesh=mesh,
        in_specs=(
            P("tok", None),
            P(),
            P(("grp", "tok"), None),
            P(("grp", "tok"), None),
            P(("grp", "tok"), None),
            P(("grp", "tok"), None),
        ),
        out_specs=(P(("grp", "tok"), None), P()),
        check_vma=False,
    )
```

```python
import jax
import jax.numpy as jnp
from jax import lax
from jax.experimental import pallas as pl
from jax.experimental.pallas import tpu as pltpu
from jax.sharding import PartitionSpec as P

HOLDERS = 4
LANES = 128
TILE = 16
BIG = 24 * 1024 * 1024
TRANSPOSED = (((1,), (1,)), ((), ()))
VMEM = pl.BlockSpec(memory_space=pltpu.VMEM)
ANY = pl.BlockSpec(memory_space=pl.ANY)
HBM = pl.BlockSpec(memory_space=pltpu.HBM)
bf16 = jnp.bfloat16
f32 = jnp.float32


def swapped(array, axis, mask):
    return lax.ppermute(array, axis, [(i, i ^ mask) for i in range(lax.axis_size(axis))])


def dot_f32(a, b, dims):
    return lax.dot_general(a, b, dims, preferred_element_type=f32)


def call(body, outs, in_specs, operands, out_specs=None, scratch=(), aliases={}):
    return pl.pallas_call(
        body,
        out_shape=outs,
        in_specs=in_specs,
        out_specs=jax.tree.map(lambda _: VMEM, outs) if out_specs is None else out_specs,
        scratch_shapes=list(scratch),
        compiler_params=pltpu.CompilerParams(vmem_limit_bytes=BIG),
        input_output_aliases=aliases,
    )(*operands)


def core():
    return lax.axis_index("grp") & 1


def holder():
    return lax.axis_index("tok") & (HOLDERS - 1)


def first_kernel(states_hbm, gain_hbm, down_hbm, route_hbm, out_ref, *refs):
    downs, (states_ref, gain_ref, route_ref, sems) = refs[:HOLDERS], refs[HOLDERS:]
    copies = [
        pltpu.make_async_copy(states_hbm, states_ref, sems.at[0]),
        pltpu.make_async_copy(gain_hbm, gain_ref, sems.at[1]),
        pltpu.make_async_copy(route_hbm, route_ref, sems.at[2]),
    ]
    depth, width = down_hbm.shape[0], downs[0].shape[1]
    for m, down_ref in enumerate(downs):
        columns = pl.ds(pl.multiple_of((holder() ^ m) * width, width), width)
        copies.append(
            pltpu.make_async_copy(
                down_hbm.at[:, columns], down_ref.at[pl.ds(0, depth)], sems.at[3 + m]
            )
        )
    for copy in copies:
        copy.start()
    for copy in copies[:3]:
        copy.wait()
    states = states_ref[...].astype(f32)
    scale = lax.rsqrt(jnp.mean(states * states, axis=1, keepdims=True) + 1e-06)
    width = out_ref.shape[1]
    own = pl.ds(pl.multiple_of(core() * width, width), width)
    out_ref[...] = (states_ref[:, own].astype(f32) * scale * gain_ref[:, own]).astype(bf16)
    route = route_ref[...]
    high = route.astype(bf16).astype(f32)
    middle = (route - high).astype(bf16).astype(f32)
    low = route - high - middle
    part = route.shape[1]
    row = lax.broadcasted_iota(jnp.int32, (TILE, part), 0)
    terms = jnp.where(row == 0, high, jnp.where(row == 1, middle, jnp.where(row == 2, low, 0.0)))
    terms = jnp.concatenate([terms, jnp.zeros((TILE, downs[0].shape[1] - part), f32)], 1)
    for down_ref in downs:
        down_ref[depth:] = terms.astype(bf16)
    for copy in copies[3:]:
        copy.wait()


def hold_kernel(*refs):
    pass


def held(array, after):
    return call(
        hold_kernel,
        jax.ShapeDtypeStruct(array.shape, array.dtype),
        [ANY] * 2,
        (array, after),
        out_specs=ANY,
        aliases={0: 0},
    )


def stack_kernel(after_ref, *refs):
    rows = refs[0].shape[0]
    z = lax.axis_index("tok") >> 1
    for m, piece in enumerate(refs[:-1]):
        refs[-1][pl.ds(pl.multiple_of((z ^ m) * rows, rows), rows)] = piece[...]


def columns_of(half, width):
    return pl.ds(pl.multiple_of(half * width, width), width)


def gated(gate, upward):
    return (gate / (1.0 + jnp.exp(-gate)) * upward).astype(bf16)


def near_kernel(near_ref, near2_ref, far_ref, gate_ref, up_ref, out_ref, gate_part_ref, up_part_ref):
    width = near_ref.shape[1]
    own, rest = columns_of(core(), width), columns_of(1 - core(), width)
    near, near2, far = near_ref[...], near2_ref[...], far_ref[...]
    gate, upward = [
        dot_f32(ref[:, own], near, TRANSPOSED) + dot_f32(ref[:, rest], near2, TRANSPOSED)
        for ref in (gate_ref, up_ref)
    ]
    out_ref[...] = gated(gate, upward)
    gate_part_ref[...] = dot_f32(gate_ref[:, own], far, TRANSPOSED)
    up_part_ref[...] = dot_f32(up_ref[:, own], far, TRANSPOSED)


def far_kernel(far2_ref, gate_ref, up_ref, near_hidden_ref, gate_part_ref, up_part_ref, out_ref):
    count, width = far2_ref.shape
    rest = columns_of(1 - core(), width)
    far2 = far2_ref[...]
    gate, upward = [
        part_ref[...] + dot_f32(ref[:, rest], far2, TRANSPOSED)
        for ref, part_ref in ((gate_ref, gate_part_ref), (up_ref, up_part_ref))
    ]
    x = lax.axis_index("tok") & 1
    out_ref[:, columns_of(x, count)] = near_hidden_ref[...]
    out_ref[:, columns_of(1 - x, count)] = gated(gate, upward)


def features_kernel(*refs):
    hidden_refs, down_refs = refs[:HOLDERS], refs[HOLDERS : 2 * HOLDERS]
    block_refs, shares_hbm = refs[2 * HOLDERS : 3 * HOLDERS], refs[3 * HOLDERS]
    route_ref, features_ref, whole_ref, shares_ref, sem = refs[3 * HOLDERS + 1 :]
    depth, tokens = hidden_refs[0].shape
    part, members = tokens // HOLDERS, lax.axis_size("tok")
    rows = tokens // members

    def place(m, piece):
        z = (holder() ^ m) * (members // HOLDERS // 2) + piece // 2
        return pl.ds(pl.multiple_of(piece % 2 * (tokens // 2) + z * rows, rows), rows)

    eye = lax.broadcasted_iota(jnp.int32, (part, part), 0) == lax.broadcasted_iota(
        jnp.int32, (part, part), 1
    )
    output = None
    for m, (hidden_ref, down_ref) in enumerate(zip(hidden_refs, down_refs)):
        product = dot_f32(hidden_ref[...], down_ref[:depth], (((0,), (0,)), ((), ())))
        output = product if output is None else output + product
        terms = down_ref[depth:, :part].astype(f32)
        route = jnp.sum(terms[:HOLDERS], axis=0, keepdims=True)
        column = jnp.sum(jnp.where(eye, route, 0.0), axis=1, keepdims=True)
        column = jnp.broadcast_to(column, (part, LANES))
        for piece in range(part // rows):
            route_ref[place(m, piece)] = column[piece * rows : (piece + 1) * rows]
    features = (output * route_ref[:, :1]).astype(bf16)
    features_ref[...] = features
    wide = features.astype(f32)
    mean = jnp.sum(wide, axis=0, keepdims=True) / tokens
    column = jnp.sum(wide * mean, axis=1, keepdims=True)
    row = jnp.transpose(jnp.broadcast_to(column, (tokens, LANES)))[:1]
    gram = dot_f32(features, features, TRANSPOSED)
    whole_ref[...] = (gram - column - row + jnp.sum(mean * mean)).astype(bf16)
    at = 0
    for i in range(tokens // TILE):
        for j in range(tokens // LANES):
            shares_ref[at * TILE : (at + 1) * TILE] = whole_ref[
                i * TILE : (i + 1) * TILE, j * LANES : (j + 1) * LANES
            ]
            at += 1
    copy = pltpu.make_async_copy(shares_ref, shares_hbm, sem)
    copy.start()
    for m, block_ref in enumerate(block_refs):
        for piece in range(part // rows):
            block_ref[piece * rows : (piece + 1) * rows] = features_ref[place(m, piece)]
    copy.wait()


def place_kernel(*refs):
    blocks, out_ref, sems = refs[:HOLDERS], refs[HOLDERS], refs[HOLDERS + 1]
    width = blocks[0].shape[1]
    copies = []
    for m, block in enumerate(blocks):
        columns = pl.ds(pl.multiple_of((holder() ^ m) * width, width), width)
        copies.append(pltpu.make_async_copy(block, out_ref.at[:, columns], sems.at[m]))
        copies[-1].start()
    for copy in copies:
        copy.wait()


def pair_kernel(parts_ref, out_ref, flat_ref):
    copies, experts, _ = out_ref.shape
    parts = parts_ref[...].astype(f32)
    total = parts[:, 0]
    for holder in range(1, parts.shape[1]):
        total = total + parts[:, holder]
    flat_ref[...] = total.astype(bf16).astype(f32)
    lane = lax.broadcasted_iota(jnp.int32, (experts, experts), 1)

    def one(expert, table):
        products = jnp.sum(flat_ref[...] * flat_ref[pl.ds(expert, 1)], axis=1)
        return jnp.where(lane == expert, jnp.sum(products, axis=1, keepdims=True), table)

    table = lax.fori_loop(0, experts, one, jnp.zeros((experts, experts), f32), unroll=experts <= 8)
    for copy in range(copies):
        out_ref[copy] = table


def cka_kernel(tables_ref, out_ref):
    totals = jnp.sum(tables_ref[...], axis=0)
    shape = totals.shape
    eye = lax.broadcasted_iota(jnp.int32, shape, 0) == lax.broadcasted_iota(jnp.int32, shape, 1)
    kept = jnp.where(eye, totals, 0.0)
    down = jnp.sum(kept, axis=1, keepdims=True)
    across = jnp.sum(kept, axis=0, keepdims=True)
    out_ref[...] = totals / jnp.sqrt(down * across)


def shards(probe_states, norm_gain, gate_weight, up_weight, down_weight, route_weight):
    groups, members = lax.axis_size("grp"), lax.axis_size("tok")
    devices = groups * members
    experts = devices // HOLDERS
    rows, model = probe_states.shape
    tokens = rows * members
    depth = gate_weight.shape[0]
    part, token_part = model // HOLDERS, tokens // HOLDERS

    own, *downs = call(
        first_kernel,
        [jax.ShapeDtypeStruct((rows, model // 2), bf16)]
        + [jax.ShapeDtypeStruct((depth + TILE, part), bf16)] * HOLDERS,
        [HBM] * 4,
        [
            pltpu.with_memory_space_constraint(a, pltpu.HBM)
            for a in (probe_states, norm_gain[None, :], down_weight, route_weight)
        ],
        scratch=[
            pltpu.VMEM((rows, model), bf16),
            pltpu.VMEM((1, model), f32),
            pltpu.VMEM(route_weight.shape, f32),
            pltpu.SemaphoreType.DMA((3 + HOLDERS,)),
        ],
    )
    down_x = swapped(downs[1], "tok", 1)
    pieces = [swapped(own, "tok", 2 * m) if m else own for m in range(members // 2)]
    near = call(
        stack_kernel,
        jax.ShapeDtypeStruct((tokens // 2, model // 2), bf16),
        [ANY] + [VMEM] * len(pieces),
        (down_x, *pieces),
    )
    far = swapped(near, "tok", 1)
    near2 = swapped(near, "grp", 1)
    down_xz = swapped(held(downs[3], near), "tok", 2)
    down_z = swapped(held(downs[2], near), "tok", 2)
    half_shape = (depth, tokens // 2)
    near_hidden, gate_part, up_part = call(
        near_kernel,
        [jax.ShapeDtypeStruct(half_shape, dtype) for dtype in (bf16, f32, f32)],
        [VMEM] * 5,
        (near, near2, far, gate_weight, up_weight),
    )
    down_xz = swapped(held(down_xz, far), "tok", 1)
    hidden = call(
        far_kernel,
        jax.ShapeDtypeStruct((depth, tokens), bf16),
        [VMEM] * 6,
        (swapped(far, "grp", 1), gate_weight, up_weight, near_hidden, gate_part, up_part),
    )
    hiddens = [swapped(hidden, "tok", m) if m else hidden for m in range(HOLDERS)]
    entries = tokens * tokens // LANES
    *blocks, centered = call(
        features_kernel,
        [jax.ShapeDtypeStruct((token_part, part), bf16)] * HOLDERS
        + [jax.ShapeDtypeStruct((entries, LANES), bf16)],
        [VMEM] * (2 * HOLDERS),
        (*hiddens, downs[0], down_x, down_z, down_xz),
        out_specs=[VMEM] * HOLDERS + [HBM],
        scratch=[
            pltpu.VMEM((tokens, LANES), f32),
            pltpu.VMEM((tokens, part), bf16),
            pltpu.VMEM((tokens, tokens), bf16),
            pltpu.VMEM((entries, LANES), bf16),
            pltpu.SemaphoreType.DMA,
        ],
    )
    arrived = lax.all_to_all(centered, ("grp", "tok"), split_axis=0, concat_axis=0, tiled=True)
    arrived = arrived.reshape(experts, HOLDERS, entries // devices, LANES)
    direct = devices * experts * experts <= 1 << 16
    tables = call(
        pair_kernel,
        jax.ShapeDtypeStruct((devices if direct else 1, experts, experts), f32),
        [VMEM],
        (arrived,),
        scratch=[pltpu.VMEM((experts, entries // devices, LANES), f32)],
    )
    if direct:
        tables = lax.all_to_all(tables, ("grp", "tok"), split_axis=0, concat_axis=0, tiled=True)
    else:
        tables = lax.psum(tables, ("grp", "tok"))
    cka = call(cka_kernel, jax.ShapeDtypeStruct((experts, experts), f32), [VMEM], (tables,))

    blocks = [swapped(b, "tok", m) if m else b for m, b in enumerate(blocks)]
    features = call(
        place_kernel,
        jax.ShapeDtypeStruct((token_part, model), bf16),
        [VMEM] * HOLDERS,
        blocks,
        out_specs=ANY,
        scratch=[pltpu.SemaphoreType.DMA((HOLDERS,))],
    )
    return (features, cka)


def solution(mesh):
    return jax.shard_map(
        shards,
        mesh=mesh,
        in_specs=(
            P("tok", None),
            P(),
            P(("grp", "tok"), None),
            P(("grp", "tok"), None),
            P(("grp", "tok"), None),
            P(("grp", "tok"), None),
        ),
        out_specs=(P(("grp", "tok"), None), P()),
        check_vma=False,
    )
```

```python
import jax
import jax.numpy as jnp
from jax import lax
from jax.experimental import pallas as pl
from jax.experimental.pallas import tpu as pltpu
from jax.sharding import PartitionSpec as P

HOLDERS = 4
LANES = 128
TILE = 16
BIG = 24 * 1024 * 1024
TRANSPOSED = (((1,), (1,)), ((), ()))
VMEM = pl.BlockSpec(memory_space=pltpu.VMEM)
ANY = pl.BlockSpec(memory_space=pl.ANY)
HBM = pl.BlockSpec(memory_space=pltpu.HBM)
bf16 = jnp.bfloat16
f32 = jnp.float32


def swapped(array, axis, mask):
    return lax.ppermute(array, axis, [(i, i ^ mask) for i in range(lax.axis_size(axis))])


def dot_f32(a, b, dims):
    return lax.dot_general(a, b, dims, preferred_element_type=f32)


def call(body, outs, in_specs, operands, out_specs=None, scratch=(), aliases={}):
    return pl.pallas_call(
        body,
        out_shape=outs,
        in_specs=in_specs,
        out_specs=jax.tree.map(lambda _: VMEM, outs) if out_specs is None else out_specs,
        scratch_shapes=list(scratch),
        compiler_params=pltpu.CompilerParams(vmem_limit_bytes=BIG),
        input_output_aliases=aliases,
    )(*operands)


def core():
    return lax.axis_index("grp") & 1


def holder():
    return lax.axis_index("tok") & (HOLDERS - 1)


def first_kernel(states_hbm, gain_hbm, down_hbm, route_hbm, out_ref, *refs):
    kept_ref, z_ref, x_ref, states_ref, gain_ref, route_ref, sems = refs
    depth, width = down_hbm.shape[0], kept_ref.shape[1]
    downs = (kept_ref, x_ref.at[pl.ds(0, depth + TILE)], z_ref, x_ref.at[pl.ds(depth + TILE, depth + TILE)])
    copies = [
        pltpu.make_async_copy(states_hbm, states_ref, sems.at[0]),
        pltpu.make_async_copy(gain_hbm, gain_ref, sems.at[1]),
        pltpu.make_async_copy(route_hbm, route_ref, sems.at[2]),
    ]
    for m, down_ref in enumerate(downs):
        columns = pl.ds(pl.multiple_of((holder() ^ m) * width, width), width)
        copies.append(
            pltpu.make_async_copy(
                down_hbm.at[:, columns], down_ref.at[pl.ds(0, depth)], sems.at[3 + m]
            )
        )
    for copy in copies:
        copy.start()
    for copy in copies[:3]:
        copy.wait()
    states = states_ref[...].astype(f32)
    scale = lax.rsqrt(jnp.mean(states * states, axis=1, keepdims=True) + 1e-06)
    width = out_ref.shape[1]
    own = pl.ds(pl.multiple_of(core() * width, width), width)
    out_ref[...] = (states_ref[:, own].astype(f32) * scale * gain_ref[:, own]).astype(bf16)
    route = route_ref[...]
    high = route.astype(bf16).astype(f32)
    middle = (route - high).astype(bf16).astype(f32)
    low = route - high - middle
    part = route.shape[1]
    row = lax.broadcasted_iota(jnp.int32, (TILE, part), 0)
    terms = jnp.where(row == 0, high, jnp.where(row == 1, middle, jnp.where(row == 2, low, 0.0)))
    terms = jnp.concatenate([terms, jnp.zeros((TILE, kept_ref.shape[1] - part), f32)], 1)
    for down_ref in downs:
        down_ref[pl.ds(depth, TILE)] = terms.astype(bf16)
    for copy in copies[3:]:
        copy.wait()


def onward_kernel(after_ref, own_ref, got_ref, out_ref):
    count = own_ref.shape[0]
    out_ref[:count] = own_ref[...]
    out_ref[count:] = got_ref[count:]


def stack_kernel(after_ref, *refs):
    rows = refs[0].shape[0]
    z = lax.axis_index("tok") >> 1
    for m, piece in enumerate(refs[:-1]):
        refs[-1][pl.ds(pl.multiple_of((z ^ m) * rows, rows), rows)] = piece[...]


def columns_of(half, width):
    return pl.ds(pl.multiple_of(half * width, width), width)


def gated(gate, upward):
    return (gate / (1.0 + jnp.exp(-gate)) * upward).astype(bf16)


def near_kernel(near_ref, near2_ref, far_ref, gate_ref, up_ref, out_ref, gate_part_ref, up_part_ref):
    width = near_ref.shape[1]
    own, rest = columns_of(core(), width), columns_of(1 - core(), width)
    near, near2, far = near_ref[...], near2_ref[...], far_ref[...]
    gate, upward = [
        dot_f32(ref[:, own], near, TRANSPOSED) + dot_f32(ref[:, rest], near2, TRANSPOSED)
        for ref in (gate_ref, up_ref)
    ]
    out_ref[...] = gated(gate, upward)
    gate_part_ref[...] = dot_f32(gate_ref[:, own], far, TRANSPOSED)
    up_part_ref[...] = dot_f32(up_ref[:, own], far, TRANSPOSED)


def far_kernel(after_ref, far2_ref, gate_ref, up_ref, near_hidden_ref, gate_part_ref, up_part_ref, out_ref):
    count, width = far2_ref.shape
    rest = columns_of(1 - core(), width)
    far2 = far2_ref[...]
    gate, upward = [
        part_ref[...] + dot_f32(ref[:, rest], far2, TRANSPOSED)
        for ref, part_ref in ((gate_ref, gate_part_ref), (up_ref, up_part_ref))
    ]
    x = lax.axis_index("tok") & 1
    out_ref[:, columns_of(x, count)] = near_hidden_ref[...]
    out_ref[:, columns_of(1 - x, count)] = gated(gate, upward)


def features_kernel(*refs):
    hidden_refs, (kept_ref, x_ref, z_ref) = refs[:HOLDERS], refs[HOLDERS : HOLDERS + 3]
    block_refs, shares_hbm = refs[HOLDERS + 3 : 2 * HOLDERS + 3], refs[2 * HOLDERS + 3]
    route_ref, features_ref, whole_ref, shares_ref, sem = refs[2 * HOLDERS + 4 :]
    depth, tokens = hidden_refs[0].shape
    count = kept_ref.shape[0]
    downs = (kept_ref[...], x_ref[:count], z_ref[:count], z_ref[count:])
    part, members = tokens // HOLDERS, lax.axis_size("tok")
    rows = tokens // members

    def place(m, piece):
        z = (holder() ^ m) * (members // HOLDERS // 2) + piece // 2
        return pl.ds(pl.multiple_of(piece % 2 * (tokens // 2) + z * rows, rows), rows)

    eye = lax.broadcasted_iota(jnp.int32, (part, part), 0) == lax.broadcasted_iota(
        jnp.int32, (part, part), 1
    )
    output = None
    for m, (hidden_ref, down) in enumerate(zip(hidden_refs, downs)):
        product = dot_f32(hidden_ref[...], down[:depth], (((0,), (0,)), ((), ())))
        output = product if output is None else output + product
        terms = down[depth:, :part].astype(f32)
        route = jnp.sum(terms[:HOLDERS], axis=0, keepdims=True)
        column = jnp.sum(jnp.where(eye, route, 0.0), axis=1, keepdims=True)
        column = jnp.broadcast_to(column, (part, LANES))
        for piece in range(part // rows):
            route_ref[place(m, piece)] = column[piece * rows : (piece + 1) * rows]
    features = (output * route_ref[:, :1]).astype(bf16)
    features_ref[...] = features
    wide = features.astype(f32)
    mean = jnp.sum(wide, axis=0, keepdims=True) / tokens
    column = jnp.sum(wide * mean, axis=1, keepdims=True)
    row = jnp.transpose(jnp.broadcast_to(column, (tokens, LANES)))[:1]
    gram = dot_f32(features, features, TRANSPOSED)
    whole_ref[...] = (gram - column - row + jnp.sum(mean * mean)).astype(bf16)
    at = 0
    for i in range(tokens // TILE):
        for j in range(tokens // LANES):
            shares_ref[at * TILE : (at + 1) * TILE] = whole_ref[
                i * TILE : (i + 1) * TILE, j * LANES : (j + 1) * LANES
            ]
            at += 1
    copy = pltpu.make_async_copy(shares_ref, shares_hbm, sem)
    copy.start()
    for m, block_ref in enumerate(block_refs):
        for piece in range(part // rows):
            block_ref[piece * rows : (piece + 1) * rows] = features_ref[place(m, piece)]
    copy.wait()


def place_kernel(*refs):
    blocks, out_ref, sems = refs[:HOLDERS], refs[HOLDERS], refs[HOLDERS + 1]
    width = blocks[0].shape[1]
    copies = []
    for m, block in enumerate(blocks):
        columns = pl.ds(pl.multiple_of((holder() ^ m) * width, width), width)
        copies.append(pltpu.make_async_copy(block, out_ref.at[:, columns], sems.at[m]))
        copies[-1].start()
    for copy in copies:
        copy.wait()


def pair_kernel(parts_ref, out_ref, flat_ref):
    copies, experts, _ = out_ref.shape
    parts = parts_ref[...].astype(f32)
    total = parts[:, 0]
    for holder in range(1, parts.shape[1]):
        total = total + parts[:, holder]
    flat_ref[...] = total.astype(bf16).astype(f32)
    lane = lax.broadcasted_iota(jnp.int32, (experts, experts), 1)

    def one(expert, table):
        products = jnp.sum(flat_ref[...] * flat_ref[pl.ds(expert, 1)], axis=1)
        return jnp.where(lane == expert, jnp.sum(products, axis=1, keepdims=True), table)

    table = lax.fori_loop(0, experts, one, jnp.zeros((experts, experts), f32), unroll=experts <= 8)
    for copy in range(copies):
        out_ref[copy] = table


def cka_kernel(tables_ref, out_ref):
    totals = jnp.sum(tables_ref[...], axis=0)
    shape = totals.shape
    eye = lax.broadcasted_iota(jnp.int32, shape, 0) == lax.broadcasted_iota(jnp.int32, shape, 1)
    kept = jnp.where(eye, totals, 0.0)
    down = jnp.sum(kept, axis=1, keepdims=True)
    across = jnp.sum(kept, axis=0, keepdims=True)
    out_ref[...] = totals / jnp.sqrt(down * across)


def shards(probe_states, norm_gain, gate_weight, up_weight, down_weight, route_weight):
    groups, members = lax.axis_size("grp"), lax.axis_size("tok")
    devices = groups * members
    experts = devices // HOLDERS
    rows, model = probe_states.shape
    tokens = rows * members
    depth = gate_weight.shape[0]
    part, token_part = model // HOLDERS, tokens // HOLDERS

    own, down_own, down_z, down_x = call(
        first_kernel,
        [jax.ShapeDtypeStruct((rows, model // 2), bf16)]
        + [jax.ShapeDtypeStruct(((depth + TILE) * n, part), bf16) for n in (1, 1, 2)],
        [HBM] * 4,
        [
            pltpu.with_memory_space_constraint(a, pltpu.HBM)
            for a in (probe_states, norm_gain[None, :], down_weight, route_weight)
        ],
        scratch=[
            pltpu.VMEM((rows, model), bf16),
            pltpu.VMEM((1, model), f32),
            pltpu.VMEM(route_weight.shape, f32),
            pltpu.SemaphoreType.DMA((3 + HOLDERS,)),
        ],
    )
    down_x = swapped(down_x, "tok", 1)
    pieces = [swapped(own, "tok", 2 * m) if m else own for m in range(members // 2)]
    near = call(
        stack_kernel,
        jax.ShapeDtypeStruct((tokens // 2, model // 2), bf16),
        [ANY] + [VMEM] * len(pieces),
        (down_x, *pieces),
    )
    far = swapped(near, "tok", 1)
    near2 = swapped(near, "grp", 1)
    down_z = call(
        onward_kernel,
        jax.ShapeDtypeStruct(down_x.shape, bf16),
        [ANY, VMEM, VMEM],
        (near, down_z, down_x),
    )
    down_z = swapped(down_z, "tok", 2)
    half_shape = (depth, tokens // 2)
    near_hidden, gate_part, up_part = call(
        near_kernel,
        [jax.ShapeDtypeStruct(half_shape, dtype) for dtype in (bf16, f32, f32)],
        [VMEM] * 5,
        (near, near2, far, gate_weight, up_weight),
    )
    hidden = call(
        far_kernel,
        jax.ShapeDtypeStruct((depth, tokens), bf16),
        [ANY] + [VMEM] * 6,
        (down_z, swapped(far, "grp", 1), gate_weight, up_weight, near_hidden, gate_part, up_part),
    )
    hiddens = [swapped(hidden, "tok", m) if m else hidden for m in range(HOLDERS)]
    entries = tokens * tokens // LANES
    *blocks, centered = call(
        features_kernel,
        [jax.ShapeDtypeStruct((token_part, part), bf16)] * HOLDERS
        + [jax.ShapeDtypeStruct((entries, LANES), bf16)],
        [VMEM] * (HOLDERS + 3),
        (*hiddens, down_own, down_x, down_z),
        out_specs=[VMEM] * HOLDERS + [HBM],
        scratch=[
            pltpu.VMEM((tokens, LANES), f32),
            pltpu.VMEM((tokens, part), bf16),
            pltpu.VMEM((tokens, tokens), bf16),
            pltpu.VMEM((entries, LANES), bf16),
            pltpu.SemaphoreType.DMA,
        ],
    )
    arrived = lax.all_to_all(centered, ("grp", "tok"), split_axis=0, concat_axis=0, tiled=True)
    arrived = arrived.reshape(experts, HOLDERS, entries // devices, LANES)
    direct = devices * experts * experts <= 1 << 16
    tables = call(
        pair_kernel,
        jax.ShapeDtypeStruct((devices if direct else 1, experts, experts), f32),
        [VMEM],
        (arrived,),
        scratch=[pltpu.VMEM((experts, entries // devices, LANES), f32)],
    )
    if direct:
        tables = lax.all_to_all(tables, ("grp", "tok"), split_axis=0, concat_axis=0, tiled=True)
    else:
        tables = lax.psum(tables, ("grp", "tok"))
    cka = call(cka_kernel, jax.ShapeDtypeStruct((experts, experts), f32), [VMEM], (tables,))

    blocks = [swapped(b, "tok", m) if m else b for m, b in enumerate(blocks)]
    features = call(
        place_kernel,
        jax.ShapeDtypeStruct((token_part, model), bf16),
        [VMEM] * HOLDERS,
        blocks,
        out_specs=ANY,
        scratch=[pltpu.SemaphoreType.DMA((HOLDERS,))],
    )
    return (features, cka)


def solution(mesh):
    return jax.shard_map(
        shards,
        mesh=mesh,
        in_specs=(
            P("tok", None),
            P(),
            P(("grp", "tok"), None),
            P(("grp", "tok"), None),
            P(("grp", "tok"), None),
            P(("grp", "tok"), None),
        ),
        out_specs=(P(("grp", "tok"), None), P()),
        check_vma=False,
    )
```

```python
import jax
import jax.numpy as jnp
from jax import lax
from jax.experimental import pallas as pl
from jax.experimental.pallas import tpu as pltpu
from jax.sharding import PartitionSpec as P

HOLDERS = 4
LANES = 128
TILE = 16
BIG = 24 * 1024 * 1024
TRANSPOSED = (((1,), (1,)), ((), ()))
VMEM = pl.BlockSpec(memory_space=pltpu.VMEM)
ANY = pl.BlockSpec(memory_space=pl.ANY)
HBM = pl.BlockSpec(memory_space=pltpu.HBM)
bf16 = jnp.bfloat16
f32 = jnp.float32


def swapped(array, axis, mask):
    return lax.ppermute(array, axis, [(i, i ^ mask) for i in range(lax.axis_size(axis))])


def dot_f32(a, b, dims):
    return lax.dot_general(a, b, dims, preferred_element_type=f32)


def call(body, outs, in_specs, operands, out_specs=None, scratch=(), aliases={}):
    return pl.pallas_call(
        body,
        out_shape=outs,
        in_specs=in_specs,
        out_specs=jax.tree.map(lambda _: VMEM, outs) if out_specs is None else out_specs,
        scratch_shapes=list(scratch),
        compiler_params=pltpu.CompilerParams(vmem_limit_bytes=BIG),
        input_output_aliases=aliases,
    )(*operands)


def core():
    return lax.axis_index("grp") & 1


def holder():
    return lax.axis_index("tok") & (HOLDERS - 1)


def columns_of(half, width):
    return pl.ds(pl.multiple_of(half * width, width), width)


def first_kernel(states_hbm, gain_hbm, down_hbm, route_hbm, out_ref, *refs):
    downs, (states_ref, gain_ref, route_ref, sems) = refs[:HOLDERS], refs[HOLDERS:]
    depth, width = down_hbm.shape[0], downs[0].shape[1]
    copies = [
        pltpu.make_async_copy(states_hbm, states_ref, sems.at[0]),
        pltpu.make_async_copy(gain_hbm, gain_ref, sems.at[1]),
        pltpu.make_async_copy(route_hbm, route_ref, sems.at[2]),
    ]
    for m, down_ref in enumerate(downs):
        columns = columns_of(holder() ^ m, width)
        copies.append(
            pltpu.make_async_copy(
                down_hbm.at[:, columns], down_ref.at[pl.ds(0, depth)], sems.at[3 + m]
            )
        )
    for copy in copies:
        copy.start()
    for copy in copies[:3]:
        copy.wait()
    states = states_ref[...].astype(f32)
    scale = lax.rsqrt(jnp.mean(states * states, axis=1, keepdims=True) + 1e-06)
    own = columns_of(core(), out_ref.shape[1])
    out_ref[...] = (states_ref[:, own].astype(f32) * scale * gain_ref[:, own]).astype(bf16)
    route = route_ref[...]
    high = route.astype(bf16).astype(f32)
    middle = (route - high).astype(bf16).astype(f32)
    low = route - high - middle
    part = route.shape[1]
    row = lax.broadcasted_iota(jnp.int32, (TILE, part), 0)
    terms = jnp.where(row == 0, high, jnp.where(row == 1, middle, jnp.where(row == 2, low, 0.0)))
    terms = jnp.concatenate([terms, jnp.zeros((TILE, width - part), f32)], 1)
    for down_ref in downs:
        down_ref[pl.ds(depth, TILE)] = terms.astype(bf16)
    for copy in copies[3:]:
        copy.wait()


def hold_kernel(*refs):
    pass


def held(array, after):
    return call(
        hold_kernel,
        jax.ShapeDtypeStruct(array.shape, array.dtype),
        [ANY] * 2,
        (array, after),
        out_specs=ANY,
        aliases={0: 0},
    )


def join_kernel(after_ref, first_ref, second_ref, out_ref):
    count = first_ref.shape[0]
    out_ref[:count] = first_ref[...]
    out_ref[count:] = second_ref[...]


def stack_kernel(after_ref, *refs):
    rows = refs[0].shape[0]
    z = lax.axis_index("tok") >> 1
    for m, piece in enumerate(refs[:-1]):
        refs[-1][pl.ds(pl.multiple_of((z ^ m) * rows, rows), rows)] = piece[...]


def gated(gate, upward):
    return (gate / (1.0 + jnp.exp(-gate)) * upward).astype(bf16)


def near_kernel(near_ref, near2_ref, far_ref, gate_ref, up_ref, out_ref, gate_part_ref, up_part_ref):
    width = near_ref.shape[1]
    own, rest = columns_of(core(), width), columns_of(1 - core(), width)
    near, near2, far = near_ref[...], near2_ref[...], far_ref[...]
    gate, upward = [
        dot_f32(ref[:, own], near, TRANSPOSED) + dot_f32(ref[:, rest], near2, TRANSPOSED)
        for ref in (gate_ref, up_ref)
    ]
    out_ref[...] = gated(gate, upward)
    gate_part_ref[...] = dot_f32(gate_ref[:, own], far, TRANSPOSED)
    up_part_ref[...] = dot_f32(up_ref[:, own], far, TRANSPOSED)


def far_kernel(after_ref, far2_ref, gate_ref, up_ref, near_hidden_ref, gate_part_ref, up_part_ref, out_ref):
    count, width = far2_ref.shape
    rest = columns_of(1 - core(), width)
    far2 = far2_ref[...]
    gate, upward = [
        part_ref[...] + dot_f32(ref[:, rest], far2, TRANSPOSED)
        for ref, part_ref in ((gate_ref, gate_part_ref), (up_ref, up_part_ref))
    ]
    x = lax.axis_index("tok") & 1
    out_ref[:, columns_of(x, count)] = near_hidden_ref[...]
    out_ref[:, columns_of(1 - x, count)] = gated(gate, upward)


def features_kernel(*refs):
    hidden_refs, (kept_ref, x_ref, z_ref) = refs[:HOLDERS], refs[HOLDERS : HOLDERS + 3]
    block_refs, shares_hbm = refs[HOLDERS + 3 : 2 * HOLDERS + 3], refs[2 * HOLDERS + 3]
    route_ref, features_ref, whole_ref, shares_ref, sem = refs[2 * HOLDERS + 4 :]
    depth, tokens = hidden_refs[0].shape
    count = kept_ref.shape[0]
    downs = (kept_ref[...], x_ref[...], z_ref[:count], z_ref[count:])
    part, members = tokens // HOLDERS, lax.axis_size("tok")
    rows = tokens // members

    def place(m, piece):
        z = (holder() ^ m) * (members // HOLDERS // 2) + piece // 2
        return pl.ds(pl.multiple_of(piece % 2 * (tokens // 2) + z * rows, rows), rows)

    eye = lax.broadcasted_iota(jnp.int32, (part, part), 0) == lax.broadcasted_iota(
        jnp.int32, (part, part), 1
    )
    output = None
    for m, (hidden_ref, down) in enumerate(zip(hidden_refs, downs)):
        product = dot_f32(hidden_ref[...], down[:depth], (((0,), (0,)), ((), ())))
        output = product if output is None else output + product
        terms = down[depth:, :part].astype(f32)
        route = jnp.sum(terms[:HOLDERS], axis=0, keepdims=True)
        column = jnp.sum(jnp.where(eye, route, 0.0), axis=1, keepdims=True)
        column = jnp.broadcast_to(column, (part, LANES))
        for piece in range(part // rows):
            route_ref[place(m, piece)] = column[piece * rows : (piece + 1) * rows]
    features = (output * route_ref[:, :1]).astype(bf16)
    features_ref[...] = features
    wide = features.astype(f32)
    mean = jnp.sum(wide, axis=0, keepdims=True) / tokens
    column = jnp.sum(wide * mean, axis=1, keepdims=True)
    row = jnp.transpose(jnp.broadcast_to(column, (tokens, LANES)))[:1]
    gram = dot_f32(features, features, TRANSPOSED)
    whole_ref[...] = (gram - column - row + jnp.sum(mean * mean)).astype(bf16)
    at = 0
    for i in range(tokens // TILE):
        for j in range(tokens // LANES):
            shares_ref[at * TILE : (at + 1) * TILE] = whole_ref[
                i * TILE : (i + 1) * TILE, j * LANES : (j + 1) * LANES
            ]
            at += 1
    copy = pltpu.make_async_copy(shares_ref, shares_hbm, sem)
    copy.start()
    for m, block_ref in enumerate(block_refs):
        for piece in range(part // rows):
            block_ref[piece * rows : (piece + 1) * rows] = features_ref[place(m, piece)]
    copy.wait()


def place_kernel(*refs):
    blocks, out_ref, sems = refs[:HOLDERS], refs[HOLDERS], refs[HOLDERS + 1]
    width = blocks[0].shape[1]
    copies = []
    for m, block in enumerate(blocks):
        columns = pl.ds(pl.multiple_of((holder() ^ m) * width, width), width)
        copies.append(pltpu.make_async_copy(block, out_ref.at[:, columns], sems.at[m]))
        copies[-1].start()
    for copy in copies:
        copy.wait()


def pair_kernel(parts_ref, out_ref, flat_ref):
    copies, experts, _ = out_ref.shape
    parts = parts_ref[...].astype(f32)
    total = parts[:, 0]
    for holder in range(1, parts.shape[1]):
        total = total + parts[:, holder]
    flat_ref[...] = total.astype(bf16).astype(f32)
    lane = lax.broadcasted_iota(jnp.int32, (experts, experts), 1)

    def one(expert, table):
        products = jnp.sum(flat_ref[...] * flat_ref[pl.ds(expert, 1)], axis=1)
        return jnp.where(lane == expert, jnp.sum(products, axis=1, keepdims=True), table)

    table = lax.fori_loop(0, experts, one, jnp.zeros((experts, experts), f32), unroll=experts <= 8)
    for copy in range(copies):
        out_ref[copy] = table


def cka_kernel(tables_ref, out_ref):
    totals = jnp.sum(tables_ref[...], axis=0)
    shape = totals.shape
    eye = lax.broadcasted_iota(jnp.int32, shape, 0) == lax.broadcasted_iota(jnp.int32, shape, 1)
    kept = jnp.where(eye, totals, 0.0)
    down = jnp.sum(kept, axis=1, keepdims=True)
    across = jnp.sum(kept, axis=0, keepdims=True)
    out_ref[...] = totals / jnp.sqrt(down * across)


def shards(probe_states, norm_gain, gate_weight, up_weight, down_weight, route_weight):
    groups, members = lax.axis_size("grp"), lax.axis_size("tok")
    devices = groups * members
    experts = devices // HOLDERS
    rows, model = probe_states.shape
    tokens = rows * members
    depth = gate_weight.shape[0]
    part, token_part = model // HOLDERS, tokens // HOLDERS

    own, down_own, down_x, down_z, down_xz = call(
        first_kernel,
        [jax.ShapeDtypeStruct((rows, model // 2), bf16)]
        + [jax.ShapeDtypeStruct((depth + TILE, part), bf16)] * HOLDERS,
        [HBM] * 4,
        [
            pltpu.with_memory_space_constraint(a, pltpu.HBM)
            for a in (probe_states, norm_gain[None, :], down_weight, route_weight)
        ],
        scratch=[
            pltpu.VMEM((rows, model), bf16),
            pltpu.VMEM((1, model), f32),
            pltpu.VMEM(route_weight.shape, f32),
            pltpu.SemaphoreType.DMA((3 + HOLDERS,)),
        ],
    )
    down_xz = swapped(down_xz, "tok", 1)
    pieces = [swapped(own, "tok", 2 * m) if m else own for m in range(members // 2)]
    near = call(
        stack_kernel,
        jax.ShapeDtypeStruct((tokens // 2, model // 2), bf16),
        [ANY] + [VMEM] * len(pieces),
        (down_xz, *pieces),
    )
    far = swapped(near, "tok", 1)
    near2 = swapped(near, "grp", 1)
    down_z = call(
        join_kernel,
        jax.ShapeDtypeStruct((2 * (depth + TILE), part), bf16),
        [ANY, VMEM, VMEM],
        (near, down_z, down_xz),
    )
    down_z = swapped(down_z, "tok", 2)
    down_x = swapped(held(down_x, far), "tok", 1)
    half_shape = (depth, tokens // 2)
    near_hidden, gate_part, up_part = call(
        near_kernel,
        [jax.ShapeDtypeStruct(half_shape, dtype) for dtype in (bf16, f32, f32)],
        [VMEM] * 5,
        (near, near2, far, gate_weight, up_weight),
    )
    hidden = call(
        far_kernel,
        jax.ShapeDtypeStruct((depth, tokens), bf16),
        [ANY] + [VMEM] * 6,
        (down_z, swapped(far, "grp", 1), gate_weight, up_weight, near_hidden, gate_part, up_part),
    )
    hiddens = [swapped(hidden, "tok", m) if m else hidden for m in range(HOLDERS)]
    entries = tokens * tokens // LANES
    *blocks, centered = call(
        features_kernel,
        [jax.ShapeDtypeStruct((token_part, part), bf16)] * HOLDERS
        + [jax.ShapeDtypeStruct((entries, LANES), bf16)],
        [VMEM] * (HOLDERS + 3),
        (*hiddens, down_own, down_x, down_z),
        out_specs=[VMEM] * HOLDERS + [HBM],
        scratch=[
            pltpu.VMEM((tokens, LANES), f32),
            pltpu.VMEM((tokens, part), bf16),
            pltpu.VMEM((tokens, tokens), bf16),
            pltpu.VMEM((entries, LANES), bf16),
            pltpu.SemaphoreType.DMA,
        ],
    )
    arrived = lax.all_to_all(centered, ("grp", "tok"), split_axis=0, concat_axis=0, tiled=True)
    arrived = arrived.reshape(experts, HOLDERS, entries // devices, LANES)
    direct = devices * experts * experts <= 1 << 16
    tables = call(
        pair_kernel,
        jax.ShapeDtypeStruct((devices if direct else 1, experts, experts), f32),
        [VMEM],
        (arrived,),
        scratch=[pltpu.VMEM((experts, entries // devices, LANES), f32)],
    )
    if direct:
        tables = lax.all_to_all(tables, ("grp", "tok"), split_axis=0, concat_axis=0, tiled=True)
    else:
        tables = lax.psum(tables, ("grp", "tok"))
    cka = call(cka_kernel, jax.ShapeDtypeStruct((experts, experts), f32), [VMEM], (tables,))

    blocks = [swapped(b, "tok", m) if m else b for m, b in enumerate(blocks)]
    features = call(
        place_kernel,
        jax.ShapeDtypeStruct((token_part, model), bf16),
        [VMEM] * HOLDERS,
        blocks,
        out_specs=ANY,
        scratch=[pltpu.SemaphoreType.DMA((HOLDERS,))],
    )
    return (features, cka)


def solution(mesh):
    return jax.shard_map(
        shards,
        mesh=mesh,
        in_specs=(
            P("tok", None),
            P(),
            P(("grp", "tok"), None),
            P(("grp", "tok"), None),
            P(("grp", "tok"), None),
            P(("grp", "tok"), None),
        ),
        out_specs=(P(("grp", "tok"), None), P()),
        check_vma=False,
    )
```

```python
import jax
import jax.numpy as jnp
from jax import lax
from jax.experimental import pallas as pl
from jax.experimental.pallas import tpu as pltpu
from jax.sharding import PartitionSpec as P

HOLDERS = 4
LANES = 128
TILE = 16
BIG = 24 * 1024 * 1024
TRANSPOSED = (((1,), (1,)), ((), ()))
VMEM = pl.BlockSpec(memory_space=pltpu.VMEM)
ANY = pl.BlockSpec(memory_space=pl.ANY)
HBM = pl.BlockSpec(memory_space=pltpu.HBM)
bf16 = jnp.bfloat16
f32 = jnp.float32


def swapped(array, axis, mask):
    return lax.ppermute(array, axis, [(i, i ^ mask) for i in range(lax.axis_size(axis))])


def dot_f32(a, b, dims):
    return lax.dot_general(a, b, dims, preferred_element_type=f32)


def call(body, outs, in_specs, operands, out_specs=None, scratch=(), aliases={}):
    return pl.pallas_call(
        body,
        out_shape=outs,
        in_specs=in_specs,
        out_specs=jax.tree.map(lambda _: VMEM, outs) if out_specs is None else out_specs,
        scratch_shapes=list(scratch),
        compiler_params=pltpu.CompilerParams(vmem_limit_bytes=BIG),
        input_output_aliases=aliases,
    )(*operands)


def core():
    return lax.axis_index("grp") & 1


def holder():
    return lax.axis_index("tok") & (HOLDERS - 1)


def columns_of(half, width):
    return pl.ds(pl.multiple_of(half * width, width), width)


def first_kernel(states_hbm, gain_hbm, down_hbm, route_hbm, out_ref, *refs):
    kept_ref, z_ref, early_ref, late_ref, states_ref, gain_ref, route_ref, sems = refs
    depth, width = down_hbm.shape[0], kept_ref.shape[1]
    count, late = depth + TILE, late_ref.shape[0] - TILE
    blocks = (
        (0, 0, depth, kept_ref.at[pl.ds(0, depth)]),
        (2, 0, depth, z_ref.at[pl.ds(0, depth)]),
        (3, 0, depth, early_ref.at[pl.ds(0, depth)]),
        (1, 0, depth - late, early_ref.at[pl.ds(count, depth - late)]),
        (1, depth - late, late, late_ref.at[pl.ds(0, late)]),
    )
    copies = [
        pltpu.make_async_copy(states_hbm, states_ref, sems.at[0]),
        pltpu.make_async_copy(gain_hbm, gain_ref, sems.at[1]),
        pltpu.make_async_copy(route_hbm, route_ref, sems.at[2]),
    ]
    for at, (m, top, size, block) in enumerate(blocks):
        source = down_hbm.at[pl.ds(top, size), columns_of(holder() ^ m, width)]
        copies.append(pltpu.make_async_copy(source, block, sems.at[3 + at]))
    for copy in copies:
        copy.start()
    for copy in copies[:3]:
        copy.wait()
    states = states_ref[...].astype(f32)
    scale = lax.rsqrt(jnp.mean(states * states, axis=1, keepdims=True) + 1e-06)
    own = columns_of(core(), out_ref.shape[1])
    out_ref[...] = (states_ref[:, own].astype(f32) * scale * gain_ref[:, own]).astype(bf16)
    route = route_ref[...]
    high = route.astype(bf16).astype(f32)
    middle = (route - high).astype(bf16).astype(f32)
    low = route - high - middle
    part = route.shape[1]
    row = lax.broadcasted_iota(jnp.int32, (TILE, part), 0)
    terms = jnp.where(row == 0, high, jnp.where(row == 1, middle, jnp.where(row == 2, low, 0.0)))
    terms = jnp.concatenate([terms, jnp.zeros((TILE, width - part), f32)], 1)
    for ref, top in ((kept_ref, depth), (z_ref, depth), (early_ref, depth), (late_ref, late)):
        ref[pl.ds(top, TILE)] = terms.astype(bf16)
    for copy in copies[3:]:
        copy.wait()


def hold_kernel(*refs):
    pass


def held(array, after):
    return call(
        hold_kernel,
        jax.ShapeDtypeStruct(array.shape, array.dtype),
        [ANY] * 2,
        (array, after),
        out_specs=ANY,
        aliases={0: 0},
    )


def join_kernel(after_ref, first_ref, second_ref, out_ref):
    count = first_ref.shape[0]
    out_ref[:count] = first_ref[...]
    out_ref[count:] = second_ref[:count]


def stack_kernel(after_ref, *refs):
    rows = refs[0].shape[0]
    z = lax.axis_index("tok") >> 1
    for m, piece in enumerate(refs[-2::-1]):
        refs[-1][pl.ds(pl.multiple_of((z ^ m) * rows, rows), rows)] = piece[...]


def gated(gate, upward):
    return (gate / (1.0 + jnp.exp(-gate)) * upward).astype(bf16)


def near_kernel(near_ref, near2_ref, far_ref, gate_ref, up_ref, out_ref, gate_part_ref, up_part_ref):
    width = near_ref.shape[1]
    own, rest = columns_of(core(), width), columns_of(1 - core(), width)
    near, near2, far = near_ref[...], near2_ref[...], far_ref[...]
    gate, upward = [
        dot_f32(ref[:, own], near, TRANSPOSED) + dot_f32(ref[:, rest], near2, TRANSPOSED)
        for ref in (gate_ref, up_ref)
    ]
    out_ref[...] = gated(gate, upward)
    gate_part_ref[...] = dot_f32(gate_ref[:, own], far, TRANSPOSED)
    up_part_ref[...] = dot_f32(up_ref[:, own], far, TRANSPOSED)


def far_kernel(after_ref, far2_ref, gate_ref, up_ref, near_hidden_ref, gate_part_ref, up_part_ref, out_ref):
    count, width = far2_ref.shape
    rest = columns_of(1 - core(), width)
    far2 = far2_ref[...]
    gate, upward = [
        part_ref[...] + dot_f32(ref[:, rest], far2, TRANSPOSED)
        for ref, part_ref in ((gate_ref, gate_part_ref), (up_ref, up_part_ref))
    ]
    x = lax.axis_index("tok") & 1
    out_ref[:, columns_of(x, count)] = near_hidden_ref[...]
    out_ref[:, columns_of(1 - x, count)] = gated(gate, upward)


def features_kernel(*refs):
    hidden_refs, (kept_ref, z_ref, early_ref, late_ref) = refs[:HOLDERS], refs[HOLDERS : 2 * HOLDERS]
    block_refs, shares_hbm = refs[2 * HOLDERS : 3 * HOLDERS], refs[3 * HOLDERS]
    route_ref, features_ref, whole_ref, shares_ref, sem = refs[3 * HOLDERS + 1 :]
    depth, tokens = hidden_refs[0].shape
    count = kept_ref.shape[0]
    x_block = jnp.concatenate([early_ref[count:], late_ref[...]])
    downs = (kept_ref[...], x_block, z_ref[:count], z_ref[count:])
    part, members = tokens // HOLDERS, lax.axis_size("tok")
    rows = tokens // members

    def place(m, piece):
        z = (holder() ^ m) * (members // HOLDERS // 2) + piece // 2
        return pl.ds(pl.multiple_of(piece % 2 * (tokens // 2) + z * rows, rows), rows)

    eye = lax.broadcasted_iota(jnp.int32, (part, part), 0) == lax.broadcasted_iota(
        jnp.int32, (part, part), 1
    )
    output = None
    for m, (hidden_ref, down) in enumerate(zip(hidden_refs, downs)):
        product = dot_f32(hidden_ref[...], down[:depth], (((0,), (0,)), ((), ())))
        output = product if output is None else output + product
        terms = down[depth:, :part].astype(f32)
        route = jnp.sum(terms[:HOLDERS], axis=0, keepdims=True)
        column = jnp.sum(jnp.where(eye, route, 0.0), axis=1, keepdims=True)
        column = jnp.broadcast_to(column, (part, LANES))
        for piece in range(part // rows):
            route_ref[place(m, piece)] = column[piece * rows : (piece + 1) * rows]
    features = (output * route_ref[:, :1]).astype(bf16)
    features_ref[...] = features
    wide = features.astype(f32)
    mean = jnp.sum(wide, axis=0, keepdims=True) / tokens
    column = jnp.sum(wide * mean, axis=1, keepdims=True)
    row = jnp.transpose(jnp.broadcast_to(column, (tokens, LANES)))[:1]
    gram = dot_f32(features, features, TRANSPOSED)
    whole_ref[...] = (gram - column - row + jnp.sum(mean * mean)).astype(bf16)
    at = 0
    for i in range(tokens // TILE):
        for j in range(tokens // LANES):
            shares_ref[at * TILE : (at + 1) * TILE] = whole_ref[
                i * TILE : (i + 1) * TILE, j * LANES : (j + 1) * LANES
            ]
            at += 1
    copy = pltpu.make_async_copy(shares_ref, shares_hbm, sem)
    copy.start()
    for m, block_ref in enumerate(block_refs):
        for piece in range(part // rows):
            block_ref[piece * rows : (piece + 1) * rows] = features_ref[place(m, piece)]
    copy.wait()


def place_kernel(*refs):
    blocks, out_ref, sems = refs[:HOLDERS], refs[HOLDERS], refs[HOLDERS + 1]
    width = blocks[0].shape[1]
    copies = []
    for m, block in enumerate(blocks):
        columns = pl.ds(pl.multiple_of((holder() ^ m) * width, width), width)
        copies.append(pltpu.make_async_copy(block, out_ref.at[:, columns], sems.at[m]))
        copies[-1].start()
    for copy in copies:
        copy.wait()


def pair_kernel(parts_ref, out_ref, flat_ref):
    copies, experts, _ = out_ref.shape
    parts = parts_ref[...].astype(f32)
    total = parts[:, 0]
    for holder in range(1, parts.shape[1]):
        total = total + parts[:, holder]
    flat_ref[...] = total.astype(bf16).astype(f32)
    lane = lax.broadcasted_iota(jnp.int32, (experts, experts), 1)

    def one(expert, table):
        products = jnp.sum(flat_ref[...] * flat_ref[pl.ds(expert, 1)], axis=1)
        return jnp.where(lane == expert, jnp.sum(products, axis=1, keepdims=True), table)

    table = lax.fori_loop(0, experts, one, jnp.zeros((experts, experts), f32), unroll=experts <= 8)
    for copy in range(copies):
        out_ref[copy] = table


def cka_kernel(tables_ref, out_ref):
    totals = jnp.sum(tables_ref[...], axis=0)
    shape = totals.shape
    eye = lax.broadcasted_iota(jnp.int32, shape, 0) == lax.broadcasted_iota(jnp.int32, shape, 1)
    kept = jnp.where(eye, totals, 0.0)
    down = jnp.sum(kept, axis=1, keepdims=True)
    across = jnp.sum(kept, axis=0, keepdims=True)
    out_ref[...] = totals / jnp.sqrt(down * across)


def shards(probe_states, norm_gain, gate_weight, up_weight, down_weight, route_weight):
    groups, members = lax.axis_size("grp"), lax.axis_size("tok")
    devices = groups * members
    experts = devices // HOLDERS
    rows, model = probe_states.shape
    tokens = rows * members
    depth = gate_weight.shape[0]
    part, token_part = model // HOLDERS, tokens // HOLDERS

    count = depth + TILE
    late = depth // 2 // TILE * TILE + TILE
    own, down_own, down_z, down_early, down_late = call(
        first_kernel,
        [jax.ShapeDtypeStruct((rows, model // 2), bf16)]
        + [jax.ShapeDtypeStruct((n, part), bf16) for n in (count, count, 2 * count - late, late)],
        [HBM] * 4,
        [
            pltpu.with_memory_space_constraint(a, pltpu.HBM)
            for a in (probe_states, norm_gain[None, :], down_weight, route_weight)
        ],
        scratch=[
            pltpu.VMEM((rows, model), bf16),
            pltpu.VMEM((1, model), f32),
            pltpu.VMEM(route_weight.shape, f32),
            pltpu.SemaphoreType.DMA((8,)),
        ],
    )
    down_early = swapped(down_early, "tok", 1)
    pieces = [swapped(own, "tok", 2 * m) for m in range(members // 2 - 1, 0, -1)] + [own]
    near = call(
        stack_kernel,
        jax.ShapeDtypeStruct((tokens // 2, model // 2), bf16),
        [ANY] + [VMEM] * len(pieces),
        (down_early, *pieces),
    )
    far = swapped(near, "tok", 1)
    near2 = swapped(near, "grp", 1)
    down_z = call(
        join_kernel,
        jax.ShapeDtypeStruct((2 * count, part), bf16),
        [ANY, VMEM, VMEM],
        (near, down_z, down_early),
    )
    down_z = swapped(down_z, "tok", 2)
    down_late = swapped(held(down_late, far), "tok", 1)
    half_shape = (depth, tokens // 2)
    near_hidden, gate_part, up_part = call(
        near_kernel,
        [jax.ShapeDtypeStruct(half_shape, dtype) for dtype in (bf16, f32, f32)],
        [VMEM] * 5,
        (near, near2, far, gate_weight, up_weight),
    )
    hidden = call(
        far_kernel,
        jax.ShapeDtypeStruct((depth, tokens), bf16),
        [ANY] + [VMEM] * 6,
        (down_z, swapped(far, "grp", 1), gate_weight, up_weight, near_hidden, gate_part, up_part),
    )
    hiddens = [swapped(hidden, "tok", m) if m else hidden for m in range(HOLDERS)]
    entries = tokens * tokens // LANES
    *blocks, centered = call(
        features_kernel,
        [jax.ShapeDtypeStruct((token_part, part), bf16)] * HOLDERS
        + [jax.ShapeDtypeStruct((entries, LANES), bf16)],
        [VMEM] * (2 * HOLDERS),
        (*hiddens, down_own, down_z, down_early, down_late),
        out_specs=[VMEM] * HOLDERS + [HBM],
        scratch=[
            pltpu.VMEM((tokens, LANES), f32),
            pltpu.VMEM((tokens, part), bf16),
            pltpu.VMEM((tokens, tokens), bf16),
            pltpu.VMEM((entries, LANES), bf16),
            pltpu.SemaphoreType.DMA,
        ],
    )
    arrived = lax.all_to_all(centered, ("grp", "tok"), split_axis=0, concat_axis=0, tiled=True)
    arrived = arrived.reshape(experts, HOLDERS, entries // devices, LANES)
    direct = devices * experts * experts <= 1 << 16
    tables = call(
        pair_kernel,
        jax.ShapeDtypeStruct((devices if direct else 1, experts, experts), f32),
        [VMEM],
        (arrived,),
        scratch=[pltpu.VMEM((experts, entries // devices, LANES), f32)],
    )
    if direct:
        tables = lax.all_to_all(tables, ("grp", "tok"), split_axis=0, concat_axis=0, tiled=True)
    else:
        tables = lax.psum(tables, ("grp", "tok"))
    cka = call(cka_kernel, jax.ShapeDtypeStruct((experts, experts), f32), [VMEM], (tables,))

    blocks = [swapped(b, "tok", m) if m else b for m, b in enumerate(blocks)]
    features = call(
        place_kernel,
        jax.ShapeDtypeStruct((token_part, model), bf16),
        [VMEM] * HOLDERS,
        blocks,
        out_specs=ANY,
        scratch=[pltpu.SemaphoreType.DMA((HOLDERS,))],
    )
    return (features, cka)


def solution(mesh):
    return jax.shard_map(
        shards,
        mesh=mesh,
        in_specs=(
            P("tok", None),
            P(),
            P(("grp", "tok"), None),
            P(("grp", "tok"), None),
            P(("grp", "tok"), None),
            P(("grp", "tok"), None),
        ),
        out_specs=(P(("grp", "tok"), None), P()),
        check_vma=False,
    )
```

```python
import jax
import jax.numpy as jnp
from jax import lax
from jax.experimental import pallas as pl
from jax.experimental.pallas import tpu as pltpu
from jax.sharding import PartitionSpec as P

HOLDERS = 4
LANES = 128
TILE = 16
BIG = 24 * 1024 * 1024
TRANSPOSED = (((1,), (1,)), ((), ()))
VMEM = pl.BlockSpec(memory_space=pltpu.VMEM)
ANY = pl.BlockSpec(memory_space=pl.ANY)
HBM = pl.BlockSpec(memory_space=pltpu.HBM)
bf16 = jnp.bfloat16
f32 = jnp.float32


def swapped(array, axis, mask):
    return lax.ppermute(array, axis, [(i, i ^ mask) for i in range(lax.axis_size(axis))])


def dot_f32(a, b, dims):
    return lax.dot_general(a, b, dims, preferred_element_type=f32)


def call(body, outs, in_specs, operands, out_specs=None, scratch=(), aliases={}):
    return pl.pallas_call(
        body,
        out_shape=outs,
        in_specs=in_specs,
        out_specs=jax.tree.map(lambda _: VMEM, outs) if out_specs is None else out_specs,
        scratch_shapes=list(scratch),
        compiler_params=pltpu.CompilerParams(vmem_limit_bytes=BIG),
        input_output_aliases=aliases,
    )(*operands)


def core():
    return lax.axis_index("grp") & 1


def holder():
    return lax.axis_index("tok") & (HOLDERS - 1)


def columns_of(half, width):
    return pl.ds(pl.multiple_of(half * width, width), width)


def first_kernel(states_hbm, gain_hbm, down_hbm, route_hbm, out_ref, *refs):
    downs, (states_ref, gain_ref, route_ref, sems) = refs[:HOLDERS], refs[HOLDERS:]
    depth, width = down_hbm.shape[0], downs[0].shape[1]
    copies = [
        pltpu.make_async_copy(states_hbm, states_ref, sems.at[0]),
        pltpu.make_async_copy(gain_hbm, gain_ref, sems.at[1]),
        pltpu.make_async_copy(route_hbm, route_ref, sems.at[2]),
    ]
    for m, down_ref in enumerate(downs):
        columns = columns_of(holder() ^ m, width)
        copies.append(
            pltpu.make_async_copy(
                down_hbm.at[:, columns], down_ref.at[pl.ds(0, depth)], sems.at[3 + m]
            )
        )
    for copy in copies:
        copy.start()
    for copy in copies[:3]:
        copy.wait()
    states = states_ref[...].astype(f32)
    scale = lax.rsqrt(jnp.mean(states * states, axis=1, keepdims=True) + 1e-06)
    own = columns_of(core(), out_ref.shape[1])
    out_ref[...] = (states_ref[:, own].astype(f32) * scale * gain_ref[:, own]).astype(bf16)
    route = route_ref[...]
    high = route.astype(bf16).astype(f32)
    middle = (route - high).astype(bf16).astype(f32)
    low = route - high - middle
    part = route.shape[1]
    row = lax.broadcasted_iota(jnp.int32, (TILE, part), 0)
    terms = jnp.where(row == 0, high, jnp.where(row == 1, middle, jnp.where(row == 2, low, 0.0)))
    terms = jnp.concatenate([terms, jnp.zeros((TILE, width - part), f32)], 1)
    for down_ref in downs:
        down_ref[pl.ds(depth, TILE)] = terms.astype(bf16)
    for copy in copies[3:]:
        copy.wait()


def hold_kernel(*refs):
    pass


def held(array, after):
    return call(
        hold_kernel,
        jax.ShapeDtypeStruct(array.shape, array.dtype),
        [ANY] * 2,
        (array, after),
        out_specs=ANY,
        aliases={0: 0},
    )


def join_kernel(after_ref, first_ref, second_ref, out_ref):
    count = first_ref.shape[0]
    out_ref[:count] = first_ref[...]
    out_ref[count:] = second_ref[...]


def stack_kernel(after_ref, *refs):
    rows = refs[0].shape[0]
    z = lax.axis_index("tok") >> 1
    for m, piece in enumerate(refs[-2::-1]):
        refs[-1][pl.ds(pl.multiple_of((z ^ m) * rows, rows), rows)] = piece[...]


def gated(gate, upward):
    return (gate / (1.0 + jnp.exp(-gate)) * upward).astype(bf16)


def near_kernel(near_ref, near2_ref, far_ref, gate_ref, up_ref, out_ref, gate_part_ref, up_part_ref):
    width = near_ref.shape[1]
    own, rest = columns_of(core(), width), columns_of(1 - core(), width)
    near, near2, far = near_ref[...], near2_ref[...], far_ref[...]
    gate, upward = [
        dot_f32(ref[:, own], near, TRANSPOSED) + dot_f32(ref[:, rest], near2, TRANSPOSED)
        for ref in (gate_ref, up_ref)
    ]
    out_ref[...] = gated(gate, upward)
    gate_part_ref[...] = dot_f32(gate_ref[:, own], far, TRANSPOSED)
    up_part_ref[...] = dot_f32(up_ref[:, own], far, TRANSPOSED)


def far_kernel(after_ref, far2_ref, gate_ref, up_ref, near_hidden_ref, gate_part_ref, up_part_ref, out_ref):
    count, width = far2_ref.shape
    rest = columns_of(1 - core(), width)
    far2 = far2_ref[...]
    gate, upward = [
        part_ref[...] + dot_f32(ref[:, rest], far2, TRANSPOSED)
        for ref, part_ref in ((gate_ref, gate_part_ref), (up_ref, up_part_ref))
    ]
    x = lax.axis_index("tok") & 1
    out_ref[:, columns_of(x, count)] = near_hidden_ref[...]
    out_ref[:, columns_of(1 - x, count)] = gated(gate, upward)


def features_kernel(*refs):
    hidden_refs, (kept_ref, x_ref, z_ref) = refs[:HOLDERS], refs[HOLDERS : HOLDERS + 3]
    block_refs, shares_hbm = refs[HOLDERS + 3 : 2 * HOLDERS + 3], refs[2 * HOLDERS + 3]
    route_ref, features_ref, whole_ref, shares_ref, sem = refs[2 * HOLDERS + 4 :]
    depth, tokens = hidden_refs[0].shape
    count = kept_ref.shape[0]
    downs = (kept_ref[...], x_ref[...], z_ref[:count], z_ref[count:])
    part, members = tokens // HOLDERS, lax.axis_size("tok")
    rows = tokens // members

    def place(m, piece):
        z = (holder() ^ m) * (members // HOLDERS // 2) + piece // 2
        return pl.ds(pl.multiple_of(piece % 2 * (tokens // 2) + z * rows, rows), rows)

    eye = lax.broadcasted_iota(jnp.int32, (part, part), 0) == lax.broadcasted_iota(
        jnp.int32, (part, part), 1
    )
    output = None
    for m, (hidden_ref, down) in enumerate(zip(hidden_refs, downs)):
        product = dot_f32(hidden_ref[...], down[:depth], (((0,), (0,)), ((), ())))
        output = product if output is None else output + product
        terms = down[depth:, :part].astype(f32)
        route = jnp.sum(terms[:HOLDERS], axis=0, keepdims=True)
        column = jnp.sum(jnp.where(eye, route, 0.0), axis=1, keepdims=True)
        column = jnp.broadcast_to(column, (part, LANES))
        for piece in range(part // rows):
            route_ref[place(m, piece)] = column[piece * rows : (piece + 1) * rows]
    features = (output * route_ref[:, :1]).astype(bf16)
    features_ref[...] = features
    wide = features.astype(f32)
    mean = jnp.sum(wide, axis=0, keepdims=True) / tokens
    column = jnp.sum(wide * mean, axis=1, keepdims=True)
    row = jnp.transpose(jnp.broadcast_to(column, (tokens, LANES)))[:1]
    gram = dot_f32(features, features, TRANSPOSED)
    whole_ref[...] = (gram - column - row + jnp.sum(mean * mean)).astype(bf16)
    at = 0
    for i in range(tokens // TILE):
        for j in range(tokens // LANES):
            shares_ref[at * TILE : (at + 1) * TILE] = whole_ref[
                i * TILE : (i + 1) * TILE, j * LANES : (j + 1) * LANES
            ]
            at += 1
    copy = pltpu.make_async_copy(shares_ref, shares_hbm, sem)
    copy.start()
    for m, block_ref in enumerate(block_refs):
        for piece in range(part // rows):
            block_ref[piece * rows : (piece + 1) * rows] = features_ref[place(m, piece)]
    copy.wait()


def pair_kernel(*refs):
    parts_ref, out_ref, flat_ref = refs[HOLDERS:]
    copies, experts, _ = out_ref.shape
    parts = parts_ref[...].astype(f32)
    total = parts[:, 0]
    for holder in range(1, parts.shape[1]):
        total = total + parts[:, holder]
    flat_ref[...] = total.astype(bf16).astype(f32)
    lane = lax.broadcasted_iota(jnp.int32, (experts, experts), 1)

    def one(expert, table):
        products = jnp.sum(flat_ref[...] * flat_ref[pl.ds(expert, 1)], axis=1)
        return jnp.where(lane == expert, jnp.sum(products, axis=1, keepdims=True), table)

    table = lax.fori_loop(0, experts, one, jnp.zeros((experts, experts), f32), unroll=experts <= 8)
    for copy in range(copies):
        out_ref[copy] = table


def last_kernel(tables_ref, *refs):
    blocks, (features_ref, out_ref, sems) = refs[:HOLDERS], refs[HOLDERS:]
    width = blocks[0].shape[1]
    copies = []
    for m, block in enumerate(blocks):
        columns = columns_of(holder() ^ m, width)
        copies.append(pltpu.make_async_copy(block, features_ref.at[:, columns], sems.at[m]))
        copies[-1].start()
    totals = jnp.sum(tables_ref[...], axis=0)
    shape = totals.shape
    eye = lax.broadcasted_iota(jnp.int32, shape, 0) == lax.broadcasted_iota(jnp.int32, shape, 1)
    kept = jnp.where(eye, totals, 0.0)
    down = jnp.sum(kept, axis=1, keepdims=True)
    across = jnp.sum(kept, axis=0, keepdims=True)
    out_ref[...] = totals / jnp.sqrt(down * across)
    for copy in copies:
        copy.wait()


def shards(probe_states, norm_gain, gate_weight, up_weight, down_weight, route_weight):
    groups, members = lax.axis_size("grp"), lax.axis_size("tok")
    devices = groups * members
    experts = devices // HOLDERS
    rows, model = probe_states.shape
    tokens = rows * members
    depth = gate_weight.shape[0]
    part, token_part = model // HOLDERS, tokens // HOLDERS

    own, down_own, down_x, down_z, down_xz = call(
        first_kernel,
        [jax.ShapeDtypeStruct((rows, model // 2), bf16)]
        + [jax.ShapeDtypeStruct((depth + TILE, part), bf16)] * HOLDERS,
        [HBM] * 4,
        [
            pltpu.with_memory_space_constraint(a, pltpu.HBM)
            for a in (probe_states, norm_gain[None, :], down_weight, route_weight)
        ],
        scratch=[
            pltpu.VMEM((rows, model), bf16),
            pltpu.VMEM((1, model), f32),
            pltpu.VMEM(route_weight.shape, f32),
            pltpu.SemaphoreType.DMA((3 + HOLDERS,)),
        ],
    )
    down_xz = swapped(down_xz, "tok", 1)
    pieces = [swapped(own, "tok", 2 * m) for m in range(members // 2 - 1, 0, -1)] + [own]
    near = call(
        stack_kernel,
        jax.ShapeDtypeStruct((tokens // 2, model // 2), bf16),
        [ANY] + [VMEM] * len(pieces),
        (down_xz, *pieces),
    )
    far = swapped(near, "tok", 1)
    near2 = swapped(near, "grp", 1)
    down_z = call(
        join_kernel,
        jax.ShapeDtypeStruct((2 * (depth + TILE), part), bf16),
        [ANY, VMEM, VMEM],
        (near, down_z, down_xz),
    )
    down_z = swapped(down_z, "tok", 2)
    down_x = swapped(held(down_x, far), "tok", 1)
    half_shape = (depth, tokens // 2)
    near_hidden, gate_part, up_part = call(
        near_kernel,
        [jax.ShapeDtypeStruct(half_shape, dtype) for dtype in (bf16, f32, f32)],
        [VMEM] * 5,
        (near, near2, far, gate_weight, up_weight),
    )
    hidden = call(
        far_kernel,
        jax.ShapeDtypeStruct((depth, tokens), bf16),
        [ANY] + [VMEM] * 6,
        (down_z, swapped(far, "grp", 1), gate_weight, up_weight, near_hidden, gate_part, up_part),
    )
    hiddens = [swapped(hidden, "tok", m) if m else hidden for m in range(HOLDERS)]
    entries = tokens * tokens // LANES
    *blocks, centered = call(
        features_kernel,
        [jax.ShapeDtypeStruct((token_part, part), bf16)] * HOLDERS
        + [jax.ShapeDtypeStruct((entries, LANES), bf16)],
        [VMEM] * (HOLDERS + 3),
        (*hiddens, down_own, down_x, down_z),
        out_specs=[VMEM] * HOLDERS + [HBM],
        scratch=[
            pltpu.VMEM((tokens, LANES), f32),
            pltpu.VMEM((tokens, part), bf16),
            pltpu.VMEM((tokens, tokens), bf16),
            pltpu.VMEM((entries, LANES), bf16),
            pltpu.SemaphoreType.DMA,
        ],
    )
    arrived = lax.all_to_all(centered, ("grp", "tok"), split_axis=0, concat_axis=0, tiled=True)
    arrived = arrived.reshape(experts, HOLDERS, entries // devices, LANES)
    blocks = [swapped(b, "tok", m) if m else b for m, b in enumerate(blocks)]
    direct = devices * experts * experts <= 1 << 16
    tables = call(
        pair_kernel,
        jax.ShapeDtypeStruct((devices if direct else 1, experts, experts), f32),
        [ANY] * HOLDERS + [VMEM],
        (*blocks, arrived),
        scratch=[pltpu.VMEM((experts, entries // devices, LANES), f32)],
    )
    if direct:
        tables = lax.all_to_all(tables, ("grp", "tok"), split_axis=0, concat_axis=0, tiled=True)
    else:
        tables = lax.psum(tables, ("grp", "tok"))
    return call(
        last_kernel,
        (
            jax.ShapeDtypeStruct((token_part, model), bf16),
            jax.ShapeDtypeStruct((experts, experts), f32),
        ),
        [VMEM] * (HOLDERS + 1),
        (tables, *blocks),
        out_specs=(HBM, VMEM),
        scratch=[pltpu.SemaphoreType.DMA((HOLDERS,))],
    )


def solution(mesh):
    return jax.shard_map(
        shards,
        mesh=mesh,
        in_specs=(
            P("tok", None),
            P(),
            P(("grp", "tok"), None),
            P(("grp", "tok"), None),
            P(("grp", "tok"), None),
            P(("grp", "tok"), None),
        ),
        out_specs=(P(("grp", "tok"), None), P()),
        check_vma=False,
    )
```

```python
import jax
import jax.numpy as jnp
from jax import lax
from jax.experimental import pallas as pl
from jax.experimental.pallas import tpu as pltpu
from jax.sharding import PartitionSpec as P

HOLDERS = 4
LANES = 128
TILE = 16
BIG = 24 * 1024 * 1024
TRANSPOSED = (((1,), (1,)), ((), ()))
VMEM = pl.BlockSpec(memory_space=pltpu.VMEM)
ANY = pl.BlockSpec(memory_space=pl.ANY)
HBM = pl.BlockSpec(memory_space=pltpu.HBM)
bf16 = jnp.bfloat16
f32 = jnp.float32


def swapped(array, axis, mask):
    return lax.ppermute(array, axis, [(i, i ^ mask) for i in range(lax.axis_size(axis))])


def dot_f32(a, b, dims):
    return lax.dot_general(a, b, dims, preferred_element_type=f32)


def call(body, outs, in_specs, operands, out_specs=None, scratch=(), aliases={}):
    return pl.pallas_call(
        body,
        out_shape=outs,
        in_specs=in_specs,
        out_specs=jax.tree.map(lambda _: VMEM, outs) if out_specs is None else out_specs,
        scratch_shapes=list(scratch),
        compiler_params=pltpu.CompilerParams(vmem_limit_bytes=BIG),
        input_output_aliases=aliases,
    )(*operands)


def core():
    return lax.axis_index("grp") & 1


def holder():
    return lax.axis_index("tok") & (HOLDERS - 1)


def columns_of(half, width):
    return pl.ds(pl.multiple_of(half * width, width), width)


def first_kernel(states_hbm, gain_hbm, down_hbm, route_hbm, out_ref, *refs):
    with_z_ref, kept_ref, z_ref, early_ref, late_ref = refs[:5]
    states_ref, gain_ref, route_ref, sems = refs[5:]
    depth, width = down_hbm.shape[0], kept_ref.shape[1]
    rows, count = states_ref.shape[0], depth + TILE
    beside, first_x = with_z_ref.shape[0] - rows, early_ref.shape[0] - count
    left, right = with_z_ref.at[pl.ds(rows, beside), pl.ds(0, width)], with_z_ref.at[
        pl.ds(rows, beside), pl.ds(width, width)
    ]
    blocks = (
        (0, 0, depth, kept_ref.at[pl.ds(0, depth)]),
        (2, 0, beside, left),
        (2, beside, beside, right),
        (2, 2 * beside, depth - 2 * beside, z_ref.at[pl.ds(0, depth - 2 * beside)]),
        (3, 0, depth, early_ref.at[pl.ds(0, depth)]),
        (1, 0, first_x, early_ref.at[pl.ds(count, first_x)]),
        (1, first_x, depth - first_x, late_ref.at[pl.ds(0, depth - first_x)]),
    )
    copies = [
        pltpu.make_async_copy(states_hbm, states_ref, sems.at[0]),
        pltpu.make_async_copy(gain_hbm, gain_ref, sems.at[1]),
        pltpu.make_async_copy(route_hbm, route_ref, sems.at[2]),
    ]
    for at, (m, top, size, block) in enumerate(blocks):
        source = down_hbm.at[pl.ds(top, size), columns_of(holder() ^ m, width)]
        copies.append(pltpu.make_async_copy(source, block, sems.at[3 + at]))
    for copy in copies:
        copy.start()
    for copy in copies[:3]:
        copy.wait()
    states = states_ref[...].astype(f32)
    scale = lax.rsqrt(jnp.mean(states * states, axis=1, keepdims=True) + 1e-06)
    own = columns_of(core(), out_ref.shape[1])
    normed = (states_ref[:, own].astype(f32) * scale * gain_ref[:, own]).astype(bf16)
    out_ref[...] = normed
    with_z_ref[:rows] = normed
    route = route_ref[...]
    high = route.astype(bf16).astype(f32)
    middle = (route - high).astype(bf16).astype(f32)
    low = route - high - middle
    part = route.shape[1]
    row = lax.broadcasted_iota(jnp.int32, (TILE, part), 0)
    terms = jnp.where(row == 0, high, jnp.where(row == 1, middle, jnp.where(row == 2, low, 0.0)))
    terms = jnp.concatenate([terms, jnp.zeros((TILE, width - part), f32)], 1)
    for ref, top in (
        (kept_ref, depth),
        (z_ref, depth - 2 * beside),
        (early_ref, depth),
        (late_ref, depth - first_x),
    ):
        ref[top : top + TILE] = terms.astype(bf16)
    for copy in copies[3:]:
        copy.wait()


def hold_kernel(*refs):
    pass


def held(array, after):
    return call(
        hold_kernel,
        jax.ShapeDtypeStruct(array.shape, array.dtype),
        [ANY] * 2,
        (array, after),
        out_specs=ANY,
        aliases={0: 0},
    )


def join_kernel(after_ref, first_ref, second_ref, out_ref):
    count = first_ref.shape[0]
    out_ref[:count] = first_ref[...]
    out_ref[count:] = second_ref[: out_ref.shape[0] - count]


def stack_kernel(after_ref, *refs):
    rows = refs[-2].shape[0]
    z = lax.axis_index("tok") >> 1
    for m, piece in enumerate(refs[-2::-1]):
        refs[-1][pl.ds(pl.multiple_of((z ^ m) * rows, rows), rows)] = piece[:rows]


def gated(gate, upward):
    return (gate / (1.0 + jnp.exp(-gate)) * upward).astype(bf16)


def near_kernel(near_ref, near2_ref, far_ref, gate_ref, up_ref, out_ref, gate_part_ref, up_part_ref):
    width = near_ref.shape[1]
    own, rest = columns_of(core(), width), columns_of(1 - core(), width)
    near, near2, far = near_ref[...], near2_ref[...], far_ref[...]
    gate, upward = [
        dot_f32(ref[:, own], near, TRANSPOSED) + dot_f32(ref[:, rest], near2, TRANSPOSED)
        for ref in (gate_ref, up_ref)
    ]
    out_ref[...] = gated(gate, upward)
    gate_part_ref[...] = dot_f32(gate_ref[:, own], far, TRANSPOSED)
    up_part_ref[...] = dot_f32(up_ref[:, own], far, TRANSPOSED)


def far_kernel(after_ref, far2_ref, gate_ref, up_ref, near_hidden_ref, gate_part_ref, up_part_ref, out_ref):
    count, width = far2_ref.shape
    rest = columns_of(1 - core(), width)
    far2 = far2_ref[...]
    gate, upward = [
        part_ref[...] + dot_f32(ref[:, rest], far2, TRANSPOSED)
        for ref, part_ref in ((gate_ref, gate_part_ref), (up_ref, up_part_ref))
    ]
    x = lax.axis_index("tok") & 1
    out_ref[:, columns_of(x, count)] = near_hidden_ref[...]
    out_ref[:, columns_of(1 - x, count)] = gated(gate, upward)


def features_kernel(*refs):
    hidden_refs, (kept_ref, with_z_ref, z_ref, early_ref, late_ref) = refs[:HOLDERS], refs[HOLDERS:][:5]
    block_refs, shares_hbm = refs[HOLDERS + 5 : 2 * HOLDERS + 5], refs[2 * HOLDERS + 5]
    route_ref, features_ref, whole_ref, shares_ref, sem = refs[2 * HOLDERS + 6 :]
    depth, tokens = hidden_refs[0].shape
    part, members = tokens // HOLDERS, lax.axis_size("tok")
    rows = tokens // members
    count, width = kept_ref.shape
    beside = (2 * count - z_ref.shape[0]) // 2
    x_block = jnp.concatenate([early_ref[count:], late_ref[...]])
    z_block = jnp.concatenate(
        [with_z_ref[rows:, :width], with_z_ref[rows:, width:], z_ref[: count - 2 * beside]]
    )
    downs = (kept_ref[...], x_block, z_block, z_ref[count - 2 * beside :])

    def place(m, piece):
        z = (holder() ^ m) * (members // HOLDERS // 2) + piece // 2
        return pl.ds(pl.multiple_of(piece % 2 * (tokens // 2) + z * rows, rows), rows)

    eye = lax.broadcasted_iota(jnp.int32, (part, part), 0) == lax.broadcasted_iota(
        jnp.int32, (part, part), 1
    )
    output = None
    for m, (hidden_ref, down) in enumerate(zip(hidden_refs, downs)):
        product = dot_f32(hidden_ref[...], down[:depth], (((0,), (0,)), ((), ())))
        output = product if output is None else output + product
        terms = down[depth:, :part].astype(f32)
        route = jnp.sum(terms[:HOLDERS], axis=0, keepdims=True)
        column = jnp.sum(jnp.where(eye, route, 0.0), axis=1, keepdims=True)
        column = jnp.broadcast_to(column, (part, LANES))
        for piece in range(part // rows):
            route_ref[place(m, piece)] = column[piece * rows : (piece + 1) * rows]
    features = (output * route_ref[:, :1]).astype(bf16)
    features_ref[...] = features
    wide = features.astype(f32)
    mean = jnp.sum(wide, axis=0, keepdims=True) / tokens
    column = jnp.sum(wide * mean, axis=1, keepdims=True)
    row = jnp.transpose(jnp.broadcast_to(column, (tokens, LANES)))[:1]
    gram = dot_f32(features, features, TRANSPOSED)
    whole_ref[...] = (gram - column - row + jnp.sum(mean * mean)).astype(bf16)
    at = 0
    for i in range(tokens // TILE):
        for j in range(tokens // LANES):
            shares_ref[at * TILE : (at + 1) * TILE] = whole_ref[
                i * TILE : (i + 1) * TILE, j * LANES : (j + 1) * LANES
            ]
            at += 1
    copy = pltpu.make_async_copy(shares_ref, shares_hbm, sem)
    copy.start()
    for m, block_ref in enumerate(block_refs):
        for piece in range(part // rows):
            block_ref[piece * rows : (piece + 1) * rows] = features_ref[place(m, piece)]
    copy.wait()


def place_kernel(*refs):
    blocks, out_ref, sems = refs[:HOLDERS], refs[HOLDERS], refs[HOLDERS + 1]
    width = blocks[0].shape[1]
    copies = []
    for m, block in enumerate(blocks):
        columns = pl.ds(pl.multiple_of((holder() ^ m) * width, width), width)
        copies.append(pltpu.make_async_copy(block, out_ref.at[:, columns], sems.at[m]))
        copies[-1].start()
    for copy in copies:
        copy.wait()


def pair_kernel(parts_ref, out_ref, flat_ref):
    copies, experts, _ = out_ref.shape
    parts = parts_ref[...].astype(f32)
    total = parts[:, 0]
    for holder in range(1, parts.shape[1]):
        total = total + parts[:, holder]
    flat_ref[...] = total.astype(bf16).astype(f32)
    lane = lax.broadcasted_iota(jnp.int32, (experts, experts), 1)

    def one(expert, table):
        products = jnp.sum(flat_ref[...] * flat_ref[pl.ds(expert, 1)], axis=1)
        return jnp.where(lane == expert, jnp.sum(products, axis=1, keepdims=True), table)

    table = lax.fori_loop(0, experts, one, jnp.zeros((experts, experts), f32), unroll=experts <= 8)
    for copy in range(copies):
        out_ref[copy] = table


def cka_kernel(tables_ref, out_ref):
    totals = jnp.sum(tables_ref[...], axis=0)
    shape = totals.shape
    eye = lax.broadcasted_iota(jnp.int32, shape, 0) == lax.broadcasted_iota(jnp.int32, shape, 1)
    kept = jnp.where(eye, totals, 0.0)
    down = jnp.sum(kept, axis=1, keepdims=True)
    across = jnp.sum(kept, axis=0, keepdims=True)
    out_ref[...] = totals / jnp.sqrt(down * across)


def shards(probe_states, norm_gain, gate_weight, up_weight, down_weight, route_weight):
    groups, members = lax.axis_size("grp"), lax.axis_size("tok")
    devices = groups * members
    experts = devices // HOLDERS
    rows, model = probe_states.shape
    tokens = rows * members
    depth = gate_weight.shape[0]
    part, token_part = model // HOLDERS, tokens // HOLDERS

    count = depth + TILE
    beside, first_x = depth // 4 // TILE * TILE, depth // 4 // TILE * TILE
    own, with_z, down_own, down_z, down_early, down_late = call(
        first_kernel,
        [jax.ShapeDtypeStruct((n, model // 2), bf16) for n in (rows, rows + beside)]
        + [
            jax.ShapeDtypeStruct((n, part), bf16)
            for n in (count, count - 2 * beside, count + first_x, count - first_x)
        ],
        [HBM] * 4,
        [
            pltpu.with_memory_space_constraint(a, pltpu.HBM)
            for a in (probe_states, norm_gain[None, :], down_weight, route_weight)
        ],
        scratch=[
            pltpu.VMEM((rows, model), bf16),
            pltpu.VMEM((1, model), f32),
            pltpu.VMEM(route_weight.shape, f32),
            pltpu.SemaphoreType.DMA((10,)),
        ],
    )
    down_early = swapped(down_early, "tok", 1)
    with_z = swapped(with_z, "tok", 2)
    pieces = [swapped(own, "tok", 2 * m) for m in range(members // 2 - 1, 1, -1)] + [with_z, own]
    near = call(
        stack_kernel,
        jax.ShapeDtypeStruct((tokens // 2, model // 2), bf16),
        [ANY] + [VMEM] * len(pieces),
        (down_early, *pieces),
    )
    far = swapped(near, "tok", 1)
    near2 = swapped(near, "grp", 1)
    down_z = call(
        join_kernel,
        jax.ShapeDtypeStruct((2 * (count - beside), part), bf16),
        [ANY, VMEM, VMEM],
        (near, down_z, down_early),
    )
    down_z = swapped(down_z, "tok", 2)
    down_late = swapped(held(down_late, far), "tok", 1)
    half_shape = (depth, tokens // 2)
    near_hidden, gate_part, up_part = call(
        near_kernel,
        [jax.ShapeDtypeStruct(half_shape, dtype) for dtype in (bf16, f32, f32)],
        [VMEM] * 5,
        (near, near2, far, gate_weight, up_weight),
    )
    hidden = call(
        far_kernel,
        jax.ShapeDtypeStruct((depth, tokens), bf16),
        [ANY] + [VMEM] * 6,
        (down_z, swapped(far, "grp", 1), gate_weight, up_weight, near_hidden, gate_part, up_part),
    )
    hiddens = [swapped(hidden, "tok", m) if m else hidden for m in range(HOLDERS)]
    entries = tokens * tokens // LANES
    *blocks, centered = call(
        features_kernel,
        [jax.ShapeDtypeStruct((token_part, part), bf16)] * HOLDERS
        + [jax.ShapeDtypeStruct((entries, LANES), bf16)],
        [VMEM] * (HOLDERS + 5),
        (*hiddens, down_own, with_z, down_z, down_early, down_late),
        out_specs=[VMEM] * HOLDERS + [HBM],
        scratch=[
            pltpu.VMEM((tokens, LANES), f32),
            pltpu.VMEM((tokens, part), bf16),
            pltpu.VMEM((tokens, tokens), bf16),
            pltpu.VMEM((entries, LANES), bf16),
            pltpu.SemaphoreType.DMA,
        ],
    )
    arrived = lax.all_to_all(centered, ("grp", "tok"), split_axis=0, concat_axis=0, tiled=True)
    arrived = arrived.reshape(experts, HOLDERS, entries // devices, LANES)
    direct = devices * experts * experts <= 1 << 16
    tables = call(
        pair_kernel,
        jax.ShapeDtypeStruct((devices if direct else 1, experts, experts), f32),
        [VMEM],
        (arrived,),
        scratch=[pltpu.VMEM((experts, entries // devices, LANES), f32)],
    )
    if direct:
        tables = lax.all_to_all(tables, ("grp", "tok"), split_axis=0, concat_axis=0, tiled=True)
    else:
        tables = lax.psum(tables, ("grp", "tok"))
    cka = call(cka_kernel, jax.ShapeDtypeStruct((experts, experts), f32), [VMEM], (tables,))

    blocks = [swapped(b, "tok", m) if m else b for m, b in enumerate(blocks)]
    features = call(
        place_kernel,
        jax.ShapeDtypeStruct((token_part, model), bf16),
        [VMEM] * HOLDERS,
        blocks,
        out_specs=ANY,
        scratch=[pltpu.SemaphoreType.DMA((HOLDERS,))],
    )
    return (features, cka)


def solution(mesh):
    return jax.shard_map(
        shards,
        mesh=mesh,
        in_specs=(
            P("tok", None),
            P(),
            P(("grp", "tok"), None),
            P(("grp", "tok"), None),
            P(("grp", "tok"), None),
            P(("grp", "tok"), None),
        ),
        out_specs=(P(("grp", "tok"), None), P()),
        check_vma=False,
    )
```

```python
import jax
import jax.numpy as jnp
from jax import lax
from jax.experimental import pallas as pl
from jax.experimental.pallas import tpu as pltpu
from jax.sharding import PartitionSpec as P

HOLDERS = 4
LANES = 128
TILE = 16
BIG = 24 * 1024 * 1024
TRANSPOSED = (((1,), (1,)), ((), ()))
VMEM = pl.BlockSpec(memory_space=pltpu.VMEM)
ANY = pl.BlockSpec(memory_space=pl.ANY)
HBM = pl.BlockSpec(memory_space=pltpu.HBM)
bf16 = jnp.bfloat16
f32 = jnp.float32


def swapped(array, axis, mask):
    return lax.ppermute(array, axis, [(i, i ^ mask) for i in range(lax.axis_size(axis))])


def dot_f32(a, b, dims):
    return lax.dot_general(a, b, dims, preferred_element_type=f32)


def call(body, outs, in_specs, operands, out_specs=None, scratch=(), aliases={}):
    return pl.pallas_call(
        body,
        out_shape=outs,
        in_specs=in_specs,
        out_specs=jax.tree.map(lambda _: VMEM, outs) if out_specs is None else out_specs,
        scratch_shapes=list(scratch),
        compiler_params=pltpu.CompilerParams(vmem_limit_bytes=BIG),
        input_output_aliases=aliases,
    )(*operands)


def core():
    return lax.axis_index("grp") & 1


def holder():
    return lax.axis_index("tok") & (HOLDERS - 1)


def columns_of(half, width):
    return pl.ds(pl.multiple_of(half * width, width), width)


def first_kernel(states_hbm, gain_hbm, down_hbm, route_hbm, out_ref, *refs):
    with_z_ref, kept_ref, z_ref, early_ref, late_ref = refs[:5]
    states_ref, gain_ref, route_ref, sems = refs[5:]
    depth, width = down_hbm.shape[0], kept_ref.shape[1]
    rows, count = states_ref.shape[0], depth + TILE
    beside, first_x = with_z_ref.shape[0] - rows, early_ref.shape[0] - count
    left, right = with_z_ref.at[pl.ds(rows, beside), pl.ds(0, width)], with_z_ref.at[
        pl.ds(rows, beside), pl.ds(width, width)
    ]
    blocks = (
        (0, 0, depth, kept_ref.at[pl.ds(0, depth)]),
        (2, 0, beside, left),
        (2, beside, beside, right),
        (2, 2 * beside, depth - 2 * beside, z_ref.at[pl.ds(0, depth - 2 * beside)]),
        (3, 0, depth, early_ref.at[pl.ds(0, depth)]),
        (1, 0, first_x, early_ref.at[pl.ds(count, first_x)]),
        (1, first_x, depth - first_x, late_ref.at[pl.ds(0, depth - first_x)]),
    )
    copies = [
        pltpu.make_async_copy(states_hbm, states_ref, sems.at[0]),
        pltpu.make_async_copy(gain_hbm, gain_ref, sems.at[1]),
        pltpu.make_async_copy(route_hbm, route_ref, sems.at[2]),
    ]
    for at, (m, top, size, block) in enumerate(blocks):
        source = down_hbm.at[pl.ds(top, size), columns_of(holder() ^ m, width)]
        copies.append(pltpu.make_async_copy(source, block, sems.at[3 + at]))
    for copy in copies:
        copy.start()
    for copy in copies[:3]:
        copy.wait()
    states = states_ref[...].astype(f32)
    scale = lax.rsqrt(jnp.mean(states * states, axis=1, keepdims=True) + 1e-06)
    own = columns_of(core(), out_ref.shape[1])
    normed = (states_ref[:, own].astype(f32) * scale * gain_ref[:, own]).astype(bf16)
    out_ref[...] = normed
    with_z_ref[:rows] = normed
    route = route_ref[...]
    high = route.astype(bf16).astype(f32)
    middle = (route - high).astype(bf16).astype(f32)
    low = route - high - middle
    part = route.shape[1]
    row = lax.broadcasted_iota(jnp.int32, (TILE, part), 0)
    terms = jnp.where(row == 0, high, jnp.where(row == 1, middle, jnp.where(row == 2, low, 0.0)))
    terms = jnp.concatenate([terms, jnp.zeros((TILE, width - part), f32)], 1)
    for ref, top in (
        (kept_ref, depth),
        (z_ref, depth - 2 * beside),
        (early_ref, depth),
        (late_ref, depth - first_x),
    ):
        ref[top : top + TILE] = terms.astype(bf16)
    for copy in copies[3:]:
        copy.wait()


def hold_kernel(*refs):
    pass


def held(array, after):
    return call(
        hold_kernel,
        jax.ShapeDtypeStruct(array.shape, array.dtype),
        [ANY] * 2,
        (array, after),
        out_specs=ANY,
        aliases={0: 0},
    )


def join_kernel(after_ref, first_ref, second_ref, out_ref):
    count = first_ref.shape[0]
    out_ref[:count] = first_ref[...]
    out_ref[count:] = second_ref[: out_ref.shape[0] - count]


def stack_kernel(after_ref, *refs):
    rows = refs[-2].shape[0]
    z = lax.axis_index("tok") >> 1
    for m, piece in enumerate(refs[-2::-1]):
        refs[-1][pl.ds(pl.multiple_of((z ^ m) * rows, rows), rows)] = piece[:rows]


def gated(gate, upward):
    return (gate / (1.0 + jnp.exp(-gate)) * upward).astype(bf16)


def near_kernel(near_ref, near2_ref, far_ref, gate_ref, up_ref, out_ref, gate_part_ref, up_part_ref):
    width = near_ref.shape[1]
    own, rest = columns_of(core(), width), columns_of(1 - core(), width)
    near, near2, far = near_ref[...], near2_ref[...], far_ref[...]
    gate, upward = [
        dot_f32(ref[:, own], near, TRANSPOSED) + dot_f32(ref[:, rest], near2, TRANSPOSED)
        for ref in (gate_ref, up_ref)
    ]
    out_ref[...] = gated(gate, upward)
    gate_part_ref[...] = dot_f32(gate_ref[:, own], far, TRANSPOSED)
    up_part_ref[...] = dot_f32(up_ref[:, own], far, TRANSPOSED)


def far_kernel(after_ref, far2_ref, gate_ref, up_ref, near_hidden_ref, gate_part_ref, up_part_ref, out_ref):
    count, width = far2_ref.shape
    rest = columns_of(1 - core(), width)
    far2 = far2_ref[...]
    gate, upward = [
        part_ref[...] + dot_f32(ref[:, rest], far2, TRANSPOSED)
        for ref, part_ref in ((gate_ref, gate_part_ref), (up_ref, up_part_ref))
    ]
    x = lax.axis_index("tok") & 1
    out_ref[:, columns_of(x, count)] = near_hidden_ref[...]
    out_ref[:, columns_of(1 - x, count)] = gated(gate, upward)


def features_kernel(*refs):
    hidden_refs, (kept_ref, with_z_ref, z_ref, early_ref, late_ref) = refs[:HOLDERS], refs[HOLDERS:][:5]
    block_refs, shares_hbm = refs[HOLDERS + 5 : 2 * HOLDERS + 5], refs[2 * HOLDERS + 5]
    route_ref, features_ref, whole_ref, shares_ref, sem = refs[2 * HOLDERS + 6 :]
    depth, tokens = hidden_refs[0].shape
    part, members = tokens // HOLDERS, lax.axis_size("tok")
    rows = tokens // members
    count, width = kept_ref.shape
    beside = (2 * count - z_ref.shape[0]) // 2
    x_block = jnp.concatenate([early_ref[count:], late_ref[...]])
    z_block = jnp.concatenate(
        [with_z_ref[rows:, :width], with_z_ref[rows:, width:], z_ref[: count - 2 * beside]]
    )
    downs = (kept_ref[...], x_block, z_block, z_ref[count - 2 * beside :])

    def place(m, piece):
        z = (holder() ^ m) * (members // HOLDERS // 2) + piece // 2
        return pl.ds(pl.multiple_of(piece % 2 * (tokens // 2) + z * rows, rows), rows)

    eye = lax.broadcasted_iota(jnp.int32, (part, part), 0) == lax.broadcasted_iota(
        jnp.int32, (part, part), 1
    )
    output = None
    for m, (hidden_ref, down) in enumerate(zip(hidden_refs, downs)):
        product = dot_f32(hidden_ref[...], down[:depth], (((0,), (0,)), ((), ())))
        output = product if output is None else output + product
        terms = down[depth:, :part].astype(f32)
        route = jnp.sum(terms[:HOLDERS], axis=0, keepdims=True)
        column = jnp.sum(jnp.where(eye, route, 0.0), axis=1, keepdims=True)
        column = jnp.broadcast_to(column, (part, LANES))
        for piece in range(part // rows):
            route_ref[place(m, piece)] = column[piece * rows : (piece + 1) * rows]
    features = (output * route_ref[:, :1]).astype(bf16)
    features_ref[...] = features
    wide = features.astype(f32)
    mean = jnp.sum(wide, axis=0, keepdims=True) / tokens
    column = jnp.sum(wide * mean, axis=1, keepdims=True)
    row = jnp.transpose(jnp.broadcast_to(column, (tokens, LANES)))[:1]
    gram = dot_f32(features, features, TRANSPOSED)
    whole_ref[...] = (gram - column - row + jnp.sum(mean * mean)).astype(bf16)
    at = 0
    for i in range(tokens // TILE):
        for j in range(tokens // LANES):
            shares_ref[at * TILE : (at + 1) * TILE] = whole_ref[
                i * TILE : (i + 1) * TILE, j * LANES : (j + 1) * LANES
            ]
            at += 1
    copy = pltpu.make_async_copy(shares_ref, shares_hbm, sem)
    copy.start()
    for m, block_ref in enumerate(block_refs):
        for piece in range(part // rows):
            block_ref[piece * rows : (piece + 1) * rows] = features_ref[place(m, piece)]
    copy.wait()


def place_kernel(*refs):
    blocks, out_ref, sems = refs[:HOLDERS], refs[HOLDERS], refs[HOLDERS + 1]
    width = blocks[0].shape[1]
    copies = []
    for m, block in enumerate(blocks):
        columns = pl.ds(pl.multiple_of((holder() ^ m) * width, width), width)
        copies.append(pltpu.make_async_copy(block, out_ref.at[:, columns], sems.at[m]))
        copies[-1].start()
    for copy in copies:
        copy.wait()


def pair_kernel(parts_ref, out_ref, flat_ref):
    copies, experts, _ = out_ref.shape
    parts = parts_ref[...].astype(f32)
    total = parts[:, 0]
    for holder in range(1, parts.shape[1]):
        total = total + parts[:, holder]
    flat_ref[...] = total.astype(bf16).astype(f32)
    lane = lax.broadcasted_iota(jnp.int32, (experts, experts), 1)

    def one(expert, table):
        products = jnp.sum(flat_ref[...] * flat_ref[pl.ds(expert, 1)], axis=1)
        return jnp.where(lane == expert, jnp.sum(products, axis=1, keepdims=True), table)

    table = lax.fori_loop(0, experts, one, jnp.zeros((experts, experts), f32), unroll=experts <= 8)
    for copy in range(copies):
        out_ref[copy] = table


def cka_kernel(tables_ref, out_ref):
    totals = jnp.sum(tables_ref[...], axis=0)
    shape = totals.shape
    eye = lax.broadcasted_iota(jnp.int32, shape, 0) == lax.broadcasted_iota(jnp.int32, shape, 1)
    kept = jnp.where(eye, totals, 0.0)
    down = jnp.sum(kept, axis=1, keepdims=True)
    across = jnp.sum(kept, axis=0, keepdims=True)
    out_ref[...] = totals / jnp.sqrt(down * across)


def shards(probe_states, norm_gain, gate_weight, up_weight, down_weight, route_weight):
    groups, members = lax.axis_size("grp"), lax.axis_size("tok")
    devices = groups * members
    experts = devices // HOLDERS
    rows, model = probe_states.shape
    tokens = rows * members
    depth = gate_weight.shape[0]
    part, token_part = model // HOLDERS, tokens // HOLDERS

    count = depth + TILE
    beside, first_x = depth // 4 // TILE * TILE, depth // 2 // TILE * TILE
    own, with_z, down_own, down_z, down_early, down_late = call(
        first_kernel,
        [jax.ShapeDtypeStruct((n, model // 2), bf16) for n in (rows, rows + beside)]
        + [
            jax.ShapeDtypeStruct((n, part), bf16)
            for n in (count, count - 2 * beside, count + first_x, count - first_x)
        ],
        [HBM] * 4,
        [
            pltpu.with_memory_space_constraint(a, pltpu.HBM)
            for a in (probe_states, norm_gain[None, :], down_weight, route_weight)
        ],
        scratch=[
            pltpu.VMEM((rows, model), bf16),
            pltpu.VMEM((1, model), f32),
            pltpu.VMEM(route_weight.shape, f32),
            pltpu.SemaphoreType.DMA((10,)),
        ],
    )
    down_early = swapped(down_early, "tok", 1)
    with_z = swapped(with_z, "tok", 2)
    pieces = [swapped(own, "tok", 2 * m) for m in range(members // 2 - 1, 1, -1)] + [with_z, own]
    near = call(
        stack_kernel,
        jax.ShapeDtypeStruct((tokens // 2, model // 2), bf16),
        [ANY] + [VMEM] * len(pieces),
        (down_early, *pieces),
    )
    far = swapped(near, "tok", 1)
    near2 = swapped(near, "grp", 1)
    down_z = call(
        join_kernel,
        jax.ShapeDtypeStruct((2 * (count - beside), part), bf16),
        [ANY, VMEM, VMEM],
        (near, down_z, down_early),
    )
    down_z = swapped(down_z, "tok", 2)
    down_late = swapped(held(down_late, far), "tok", 1)
    half_shape = (depth, tokens // 2)
    near_hidden, gate_part, up_part = call(
        near_kernel,
        [jax.ShapeDtypeStruct(half_shape, dtype) for dtype in (bf16, f32, f32)],
        [VMEM] * 5,
        (near, near2, far, gate_weight, up_weight),
    )
    hidden = call(
        far_kernel,
        jax.ShapeDtypeStruct((depth, tokens), bf16),
        [ANY] + [VMEM] * 6,
        (down_z, swapped(far, "grp", 1), gate_weight, up_weight, near_hidden, gate_part, up_part),
    )
    hiddens = [swapped(hidden, "tok", m) if m else hidden for m in range(HOLDERS)]
    entries = tokens * tokens // LANES
    *blocks, centered = call(
        features_kernel,
        [jax.ShapeDtypeStruct((token_part, part), bf16)] * HOLDERS
        + [jax.ShapeDtypeStruct((entries, LANES), bf16)],
        [VMEM] * (HOLDERS + 5),
        (*hiddens, down_own, with_z, down_z, down_early, down_late),
        out_specs=[VMEM] * HOLDERS + [HBM],
        scratch=[
            pltpu.VMEM((tokens, LANES), f32),
            pltpu.VMEM((tokens, part), bf16),
            pltpu.VMEM((tokens, tokens), bf16),
            pltpu.VMEM((entries, LANES), bf16),
            pltpu.SemaphoreType.DMA,
        ],
    )
    arrived = lax.all_to_all(centered, ("grp", "tok"), split_axis=0, concat_axis=0, tiled=True)
    arrived = arrived.reshape(experts, HOLDERS, entries // devices, LANES)
    direct = devices * experts * experts <= 1 << 16
    tables = call(
        pair_kernel,
        jax.ShapeDtypeStruct((devices if direct else 1, experts, experts), f32),
        [VMEM],
        (arrived,),
        scratch=[pltpu.VMEM((experts, entries // devices, LANES), f32)],
    )
    if direct:
        tables = lax.all_to_all(tables, ("grp", "tok"), split_axis=0, concat_axis=0, tiled=True)
    else:
        tables = lax.psum(tables, ("grp", "tok"))
    cka = call(cka_kernel, jax.ShapeDtypeStruct((experts, experts), f32), [VMEM], (tables,))

    blocks = [swapped(b, "tok", m) if m else b for m, b in enumerate(blocks)]
    features = call(
        place_kernel,
        jax.ShapeDtypeStruct((token_part, model), bf16),
        [VMEM] * HOLDERS,
        blocks,
        out_specs=ANY,
        scratch=[pltpu.SemaphoreType.DMA((HOLDERS,))],
    )
    return (features, cka)


def solution(mesh):
    return jax.shard_map(
        shards,
        mesh=mesh,
        in_specs=(
            P("tok", None),
            P(),
            P(("grp", "tok"), None),
            P(("grp", "tok"), None),
            P(("grp", "tok"), None),
            P(("grp", "tok"), None),
        ),
        out_specs=(P(("grp", "tok"), None), P()),
        check_vma=False,
    )
```

```python
import jax
import jax.numpy as jnp
from jax import lax
from jax.experimental import pallas as pl
from jax.experimental.pallas import tpu as pltpu
from jax.sharding import PartitionSpec as P

HOLDERS = 4
LANES = 128
TILE = 16
BIG = 24 * 1024 * 1024
TRANSPOSED = (((1,), (1,)), ((), ()))
VMEM = pl.BlockSpec(memory_space=pltpu.VMEM)
ANY = pl.BlockSpec(memory_space=pl.ANY)
HBM = pl.BlockSpec(memory_space=pltpu.HBM)
bf16 = jnp.bfloat16
f32 = jnp.float32


def swapped(array, axis, mask):
    return lax.ppermute(array, axis, [(i, i ^ mask) for i in range(lax.axis_size(axis))])


def dot_f32(a, b, dims):
    return lax.dot_general(a, b, dims, preferred_element_type=f32)


def call(body, outs, in_specs, operands, out_specs=None, scratch=(), aliases={}):
    return pl.pallas_call(
        body,
        out_shape=outs,
        in_specs=in_specs,
        out_specs=jax.tree.map(lambda _: VMEM, outs) if out_specs is None else out_specs,
        scratch_shapes=list(scratch),
        compiler_params=pltpu.CompilerParams(vmem_limit_bytes=BIG),
        input_output_aliases=aliases,
    )(*operands)


def core():
    return lax.axis_index("grp") & 1


def holder():
    return lax.axis_index("tok") & (HOLDERS - 1)


def columns_of(half, width):
    return pl.ds(pl.multiple_of(half * width, width), width)


def first_kernel(states_hbm, gain_hbm, down_hbm, route_hbm, out_ref, *refs):
    with_z_ref, kept_ref, z_ref, early_ref, late_ref = refs[:5]
    states_ref, gain_ref, route_ref, sems = refs[5:]
    depth, width = down_hbm.shape[0], kept_ref.shape[1]
    rows, count = states_ref.shape[0], depth + TILE
    beside, first_x = with_z_ref.shape[0] - rows, early_ref.shape[0] - count
    left, right = with_z_ref.at[pl.ds(rows, beside), pl.ds(0, width)], with_z_ref.at[
        pl.ds(rows, beside), pl.ds(width, width)
    ]
    blocks = (
        (0, 0, depth, kept_ref.at[pl.ds(0, depth)]),
        (2, 0, beside, left),
        (2, beside, beside, right),
        (2, 2 * beside, depth - 2 * beside, z_ref.at[pl.ds(0, depth - 2 * beside)]),
        (3, 0, depth, early_ref.at[pl.ds(0, depth)]),
        (1, 0, first_x, early_ref.at[pl.ds(count, first_x)]),
        (1, first_x, depth - first_x, late_ref.at[pl.ds(0, depth - first_x)]),
    )
    copies = [
        pltpu.make_async_copy(states_hbm, states_ref, sems.at[0]),
        pltpu.make_async_copy(gain_hbm, gain_ref, sems.at[1]),
        pltpu.make_async_copy(route_hbm, route_ref, sems.at[2]),
    ]
    for at, (m, top, size, block) in enumerate(blocks):
        source = down_hbm.at[pl.ds(top, size), columns_of(holder() ^ m, width)]
        copies.append(pltpu.make_async_copy(source, block, sems.at[3 + at]))
    for copy in copies:
        copy.start()
    for copy in copies[:3]:
        copy.wait()
    states = states_ref[...].astype(f32)
    scale = lax.rsqrt(jnp.mean(states * states, axis=1, keepdims=True) + 1e-06)
    own = columns_of(core(), out_ref.shape[1])
    normed = (states_ref[:, own].astype(f32) * scale * gain_ref[:, own]).astype(bf16)
    out_ref[...] = normed
    with_z_ref[:rows] = normed
    route = route_ref[...]
    high = route.astype(bf16).astype(f32)
    middle = (route - high).astype(bf16).astype(f32)
    low = route - high - middle
    part = route.shape[1]
    row = lax.broadcasted_iota(jnp.int32, (TILE, part), 0)
    terms = jnp.where(row == 0, high, jnp.where(row == 1, middle, jnp.where(row == 2, low, 0.0)))
    terms = jnp.concatenate([terms, jnp.zeros((TILE, width - part), f32)], 1)
    for ref, top in (
        (kept_ref, depth),
        (z_ref, depth - 2 * beside),
        (early_ref, depth),
        (late_ref, depth - first_x),
    ):
        ref[top : top + TILE] = terms.astype(bf16)
    for copy in copies[3:]:
        copy.wait()


def hold_kernel(*refs):
    pass


def held(array, after):
    return call(
        hold_kernel,
        jax.ShapeDtypeStruct(array.shape, array.dtype),
        [ANY] * 2,
        (array, after),
        out_specs=ANY,
        aliases={0: 0},
    )


def join_kernel(after_ref, first_ref, second_ref, out_ref):
    count = first_ref.shape[0]
    out_ref[:count] = first_ref[...]
    out_ref[count:] = second_ref[: out_ref.shape[0] - count]


def to_place(out_ref, m, piece):
    rows = piece.shape[0]
    place = (lax.axis_index("tok") >> 1) ^ m
    out_ref[pl.ds(pl.multiple_of(place * rows, rows), rows)] = piece


def near_stack_kernel(after_ref, *refs):
    pieces, (near_ref, others_ref) = refs[:-3], refs[-2:]
    count = len(pieces)
    rows = near_ref.shape[0] // count
    for at, ref in enumerate(pieces):
        m = count - 1 - at
        piece = ref[:rows]
        to_place(near_ref, m, piece)
        if m:
            others_ref[(m - 1) * rows : m * rows] = piece


def far_stack_kernel(own_ref, others_ref, out_ref):
    rows = own_ref.shape[0]
    to_place(out_ref, 0, own_ref[...])
    for m in range(1, out_ref.shape[0] // rows):
        to_place(out_ref, m, others_ref[(m - 1) * rows : m * rows])


def gated(gate, upward):
    return (gate / (1.0 + jnp.exp(-gate)) * upward).astype(bf16)


def near_kernel(near_ref, near2_ref, far_ref, gate_ref, up_ref, out_ref, gate_part_ref, up_part_ref):
    width = near_ref.shape[1]
    own, rest = columns_of(core(), width), columns_of(1 - core(), width)
    near, near2, far = near_ref[...], near2_ref[...], far_ref[...]
    gate, upward = [
        dot_f32(ref[:, own], near, TRANSPOSED) + dot_f32(ref[:, rest], near2, TRANSPOSED)
        for ref in (gate_ref, up_ref)
    ]
    out_ref[...] = gated(gate, upward)
    gate_part_ref[...] = dot_f32(gate_ref[:, own], far, TRANSPOSED)
    up_part_ref[...] = dot_f32(up_ref[:, own], far, TRANSPOSED)


def far_kernel(after_ref, far2_ref, gate_ref, up_ref, near_hidden_ref, gate_part_ref, up_part_ref, out_ref):
    count, width = far2_ref.shape
    rest = columns_of(1 - core(), width)
    far2 = far2_ref[...]
    gate, upward = [
        part_ref[...] + dot_f32(ref[:, rest], far2, TRANSPOSED)
        for ref, part_ref in ((gate_ref, gate_part_ref), (up_ref, up_part_ref))
    ]
    x = lax.axis_index("tok") & 1
    out_ref[:, columns_of(x, count)] = near_hidden_ref[...]
    out_ref[:, columns_of(1 - x, count)] = gated(gate, upward)


def features_kernel(*refs):
    hidden_refs, (kept_ref, with_z_ref, z_ref, early_ref, late_ref) = refs[:HOLDERS], refs[HOLDERS:][:5]
    block_refs, shares_hbm = refs[HOLDERS + 5 : 2 * HOLDERS + 5], refs[2 * HOLDERS + 5]
    route_ref, features_ref, whole_ref, shares_ref, sem = refs[2 * HOLDERS + 6 :]
    depth, tokens = hidden_refs[0].shape
    part, members = tokens // HOLDERS, lax.axis_size("tok")
    rows = tokens // members
    count, width = kept_ref.shape
    beside = (2 * count - z_ref.shape[0]) // 2
    x_block = jnp.concatenate([early_ref[count:], late_ref[...]])
    z_block = jnp.concatenate(
        [with_z_ref[rows:, :width], with_z_ref[rows:, width:], z_ref[: count - 2 * beside]]
    )
    downs = (kept_ref[...], x_block, z_block, z_ref[count - 2 * beside :])

    def place(m, piece):
        z = (holder() ^ m) * (members // HOLDERS // 2) + piece // 2
        return pl.ds(pl.multiple_of(piece % 2 * (tokens // 2) + z * rows, rows), rows)

    eye = lax.broadcasted_iota(jnp.int32, (part, part), 0) == lax.broadcasted_iota(
        jnp.int32, (part, part), 1
    )
    output = None
    for m, (hidden_ref, down) in enumerate(zip(hidden_refs, downs)):
        product = dot_f32(hidden_ref[...], down[:depth], (((0,), (0,)), ((), ())))
        output = product if output is None else output + product
        terms = down[depth:, :part].astype(f32)
        route = jnp.sum(terms[:HOLDERS], axis=0, keepdims=True)
        column = jnp.sum(jnp.where(eye, route, 0.0), axis=1, keepdims=True)
        column = jnp.broadcast_to(column, (part, LANES))
        for piece in range(part // rows):
            route_ref[place(m, piece)] = column[piece * rows : (piece + 1) * rows]
    features = (output * route_ref[:, :1]).astype(bf16)
    features_ref[...] = features
    wide = features.astype(f32)
    mean = jnp.sum(wide, axis=0, keepdims=True) / tokens
    column = jnp.sum(wide * mean, axis=1, keepdims=True)
    row = jnp.transpose(jnp.broadcast_to(column, (tokens, LANES)))[:1]
    gram = dot_f32(features, features, TRANSPOSED)
    whole_ref[...] = (gram - column - row + jnp.sum(mean * mean)).astype(bf16)
    at = 0
    for i in range(tokens // TILE):
        for j in range(tokens // LANES):
            shares_ref[at * TILE : (at + 1) * TILE] = whole_ref[
                i * TILE : (i + 1) * TILE, j * LANES : (j + 1) * LANES
            ]
            at += 1
    copy = pltpu.make_async_copy(shares_ref, shares_hbm, sem)
    copy.start()
    for m, block_ref in enumerate(block_refs):
        for piece in range(part // rows):
            block_ref[piece * rows : (piece + 1) * rows] = features_ref[place(m, piece)]
    copy.wait()


def place_kernel(*refs):
    blocks, out_ref, sems = refs[:HOLDERS], refs[HOLDERS], refs[HOLDERS + 1]
    width = blocks[0].shape[1]
    copies = []
    for m, block in enumerate(blocks):
        columns = pl.ds(pl.multiple_of((holder() ^ m) * width, width), width)
        copies.append(pltpu.make_async_copy(block, out_ref.at[:, columns], sems.at[m]))
        copies[-1].start()
    for copy in copies:
        copy.wait()


def pair_kernel(parts_ref, out_ref, flat_ref):
    copies, experts, _ = out_ref.shape
    parts = parts_ref[...].astype(f32)
    total = parts[:, 0]
    for holder in range(1, parts.shape[1]):
        total = total + parts[:, holder]
    flat_ref[...] = total.astype(bf16).astype(f32)
    lane = lax.broadcasted_iota(jnp.int32, (experts, experts), 1)

    def one(expert, table):
        products = jnp.sum(flat_ref[...] * flat_ref[pl.ds(expert, 1)], axis=1)
        return jnp.where(lane == expert, jnp.sum(products, axis=1, keepdims=True), table)

    table = lax.fori_loop(0, experts, one, jnp.zeros((experts, experts), f32), unroll=experts <= 8)
    for copy in range(copies):
        out_ref[copy] = table


def cka_kernel(tables_ref, out_ref):
    totals = jnp.sum(tables_ref[...], axis=0)
    shape = totals.shape
    eye = lax.broadcasted_iota(jnp.int32, shape, 0) == lax.broadcasted_iota(jnp.int32, shape, 1)
    kept = jnp.where(eye, totals, 0.0)
    down = jnp.sum(kept, axis=1, keepdims=True)
    across = jnp.sum(kept, axis=0, keepdims=True)
    out_ref[...] = totals / jnp.sqrt(down * across)


def shards(probe_states, norm_gain, gate_weight, up_weight, down_weight, route_weight):
    groups, members = lax.axis_size("grp"), lax.axis_size("tok")
    devices = groups * members
    experts = devices // HOLDERS
    rows, model = probe_states.shape
    tokens = rows * members
    depth = gate_weight.shape[0]
    part, token_part = model // HOLDERS, tokens // HOLDERS

    count = depth + TILE
    beside, first_x = depth // 4 // TILE * TILE, depth // 4 // TILE * TILE
    own, with_z, down_own, down_z, down_early, down_late = call(
        first_kernel,
        [jax.ShapeDtypeStruct((n, model // 2), bf16) for n in (rows, rows + beside)]
        + [
            jax.ShapeDtypeStruct((n, part), bf16)
            for n in (count, count - 2 * beside, count + first_x, count - first_x)
        ],
        [HBM] * 4,
        [
            pltpu.with_memory_space_constraint(a, pltpu.HBM)
            for a in (probe_states, norm_gain[None, :], down_weight, route_weight)
        ],
        scratch=[
            pltpu.VMEM((rows, model), bf16),
            pltpu.VMEM((1, model), f32),
            pltpu.VMEM(route_weight.shape, f32),
            pltpu.SemaphoreType.DMA((10,)),
        ],
    )
    down_early = swapped(down_early, "tok", 1)
    with_z = swapped(with_z, "tok", 2)
    pieces = [swapped(own, "tok", 2 * m) for m in range(members // 2 - 1, 1, -1)] + [with_z, own]
    half_width = model // 2
    near_shape = jax.ShapeDtypeStruct((tokens // 2, half_width), bf16)
    far_own = swapped(held(own, pieces[0]), "tok", 1)
    near, others = call(
        near_stack_kernel,
        [near_shape, jax.ShapeDtypeStruct((tokens // 2 - rows, half_width), bf16)],
        [ANY] + [VMEM] * len(pieces) + [ANY],
        (down_early, *pieces, far_own),
    )
    far = call(
        far_stack_kernel, near_shape, [VMEM] * 2, (far_own, swapped(others, "tok", 1))
    )
    near2 = swapped(near, "grp", 1)
    down_z = call(
        join_kernel,
        jax.ShapeDtypeStruct((2 * (count - beside), part), bf16),
        [ANY, VMEM, VMEM],
        (near, down_z, down_early),
    )
    down_z = swapped(down_z, "tok", 2)
    down_late = swapped(held(down_late, far), "tok", 1)
    half_shape = (depth, tokens // 2)
    near_hidden, gate_part, up_part = call(
        near_kernel,
        [jax.ShapeDtypeStruct(half_shape, dtype) for dtype in (bf16, f32, f32)],
        [VMEM] * 5,
        (near, near2, far, gate_weight, up_weight),
    )
    hidden = call(
        far_kernel,
        jax.ShapeDtypeStruct((depth, tokens), bf16),
        [ANY] + [VMEM] * 6,
        (down_z, swapped(far, "grp", 1), gate_weight, up_weight, near_hidden, gate_part, up_part),
    )
    hiddens = [swapped(hidden, "tok", m) if m else hidden for m in range(HOLDERS)]
    entries = tokens * tokens // LANES
    *blocks, centered = call(
        features_kernel,
        [jax.ShapeDtypeStruct((token_part, part), bf16)] * HOLDERS
        + [jax.ShapeDtypeStruct((entries, LANES), bf16)],
        [VMEM] * (HOLDERS + 5),
        (*hiddens, down_own, with_z, down_z, down_early, down_late),
        out_specs=[VMEM] * HOLDERS + [HBM],
        scratch=[
            pltpu.VMEM((tokens, LANES), f32),
            pltpu.VMEM((tokens, part), bf16),
            pltpu.VMEM((tokens, tokens), bf16),
            pltpu.VMEM((entries, LANES), bf16),
            pltpu.SemaphoreType.DMA,
        ],
    )
    arrived = lax.all_to_all(centered, ("grp", "tok"), split_axis=0, concat_axis=0, tiled=True)
    arrived = arrived.reshape(experts, HOLDERS, entries // devices, LANES)
    direct = devices * experts * experts <= 1 << 16
    tables = call(
        pair_kernel,
        jax.ShapeDtypeStruct((devices if direct else 1, experts, experts), f32),
        [VMEM],
        (arrived,),
        scratch=[pltpu.VMEM((experts, entries // devices, LANES), f32)],
    )
    if direct:
        tables = lax.all_to_all(tables, ("grp", "tok"), split_axis=0, concat_axis=0, tiled=True)
    else:
        tables = lax.psum(tables, ("grp", "tok"))
    cka = call(cka_kernel, jax.ShapeDtypeStruct((experts, experts), f32), [VMEM], (tables,))

    blocks = [swapped(b, "tok", m) if m else b for m, b in enumerate(blocks)]
    features = call(
        place_kernel,
        jax.ShapeDtypeStruct((token_part, model), bf16),
        [VMEM] * HOLDERS,
        blocks,
        out_specs=ANY,
        scratch=[pltpu.SemaphoreType.DMA((HOLDERS,))],
    )
    return (features, cka)


def solution(mesh):
    return jax.shard_map(
        shards,
        mesh=mesh,
        in_specs=(
            P("tok", None),
            P(),
            P(("grp", "tok"), None),
            P(("grp", "tok"), None),
            P(("grp", "tok"), None),
            P(("grp", "tok"), None),
        ),
        out_specs=(P(("grp", "tok"), None), P()),
        check_vma=False,
    )
```

```python
import jax
import jax.numpy as jnp
from jax import lax
from jax.experimental import pallas as pl
from jax.experimental.pallas import tpu as pltpu
from jax.sharding import PartitionSpec as P

HOLDERS = 4
LANES = 128
TILE = 16
BIG = 24 * 1024 * 1024
TRANSPOSED = (((1,), (1,)), ((), ()))
VMEM = pl.BlockSpec(memory_space=pltpu.VMEM)
ANY = pl.BlockSpec(memory_space=pl.ANY)
HBM = pl.BlockSpec(memory_space=pltpu.HBM)
bf16 = jnp.bfloat16
f32 = jnp.float32


def swapped(array, axis, mask):
    return lax.ppermute(array, axis, [(i, i ^ mask) for i in range(lax.axis_size(axis))])


def dot_f32(a, b, dims):
    return lax.dot_general(a, b, dims, preferred_element_type=f32)


def call(body, outs, in_specs, operands, out_specs=None, scratch=(), aliases={}):
    return pl.pallas_call(
        body,
        out_shape=outs,
        in_specs=in_specs,
        out_specs=jax.tree.map(lambda _: VMEM, outs) if out_specs is None else out_specs,
        scratch_shapes=list(scratch),
        compiler_params=pltpu.CompilerParams(vmem_limit_bytes=BIG),
        input_output_aliases=aliases,
    )(*operands)


def core():
    return lax.axis_index("grp") & 1


def holder():
    return lax.axis_index("tok") & (HOLDERS - 1)


def columns_of(half, width):
    return pl.ds(pl.multiple_of(half * width, width), width)


def first_kernel(states_hbm, gain_hbm, down_hbm, route_hbm, out_ref, *refs):
    with_z_ref, kept_ref, z_ref, early_ref, late_ref = refs[:5]
    states_ref, gain_ref, route_ref, sems = refs[5:]
    depth, width = down_hbm.shape[0], kept_ref.shape[1]
    rows, count = states_ref.shape[0], depth + TILE
    beside, first_x = with_z_ref.shape[0] - rows, early_ref.shape[0] - count
    left, right = with_z_ref.at[pl.ds(rows, beside), pl.ds(0, width)], with_z_ref.at[
        pl.ds(rows, beside), pl.ds(width, width)
    ]
    blocks = (
        (0, 0, depth, kept_ref.at[pl.ds(0, depth)]),
        (2, 0, beside, left),
        (2, beside, beside, right),
        (2, 2 * beside, depth - 2 * beside, z_ref.at[pl.ds(0, depth - 2 * beside)]),
        (3, 0, depth, early_ref.at[pl.ds(0, depth)]),
        (1, 0, first_x, early_ref.at[pl.ds(count, first_x)]),
        (1, first_x, depth - first_x, late_ref.at[pl.ds(0, depth - first_x)]),
    )
    copies = [
        pltpu.make_async_copy(states_hbm, states_ref, sems.at[0]),
        pltpu.make_async_copy(gain_hbm, gain_ref, sems.at[1]),
        pltpu.make_async_copy(route_hbm, route_ref, sems.at[2]),
    ]
    for at, (m, top, size, block) in enumerate(blocks):
        source = down_hbm.at[pl.ds(top, size), columns_of(holder() ^ m, width)]
        copies.append(pltpu.make_async_copy(source, block, sems.at[3 + at]))
    for copy in copies:
        copy.start()
    for copy in copies[:3]:
        copy.wait()
    states = states_ref[...].astype(f32)
    scale = lax.rsqrt(jnp.mean(states * states, axis=1, keepdims=True) + 1e-06)
    own = columns_of(core(), out_ref.shape[1])
    normed = (states_ref[:, own].astype(f32) * scale * gain_ref[:, own]).astype(bf16)
    out_ref[...] = normed
    with_z_ref[:rows] = normed
    route = route_ref[...]
    high = route.astype(bf16).astype(f32)
    middle = (route - high).astype(bf16).astype(f32)
    low = route - high - middle
    part = route.shape[1]
    row = lax.broadcasted_iota(jnp.int32, (TILE, part), 0)
    terms = jnp.where(row == 0, high, jnp.where(row == 1, middle, jnp.where(row == 2, low, 0.0)))
    terms = jnp.concatenate([terms, jnp.zeros((TILE, width - part), f32)], 1)
    for ref, top in (
        (kept_ref, depth),
        (z_ref, depth - 2 * beside),
        (early_ref, depth),
        (late_ref, depth - first_x),
    ):
        ref[top : top + TILE] = terms.astype(bf16)
    for copy in copies[3:]:
        copy.wait()


def hold_kernel(*refs):
    pass


def held(array, after):
    return call(
        hold_kernel,
        jax.ShapeDtypeStruct(array.shape, array.dtype),
        [ANY] * 2,
        (array, after),
        out_specs=ANY,
        aliases={0: 0},
    )


def join_kernel(after_ref, first_ref, second_ref, out_ref):
    count = first_ref.shape[0]
    out_ref[:count] = first_ref[...]
    out_ref[count:] = second_ref[: out_ref.shape[0] - count]


def stack_kernel(after_ref, *refs):
    rows = refs[-2].shape[0]
    z = lax.axis_index("tok") >> 1
    for m, piece in enumerate(refs[-2::-1]):
        refs[-1][pl.ds(pl.multiple_of((z ^ m) * rows, rows), rows)] = piece[:rows]


def gated(gate, upward):
    return (gate / (1.0 + jnp.exp(-gate)) * upward).astype(bf16)


def near_kernel(near_ref, near2_ref, far_ref, gate_ref, up_ref, out_ref, gate_part_ref, up_part_ref):
    width = near_ref.shape[1]
    own, rest = columns_of(core(), width), columns_of(1 - core(), width)
    near, near2, far = near_ref[...], near2_ref[...], far_ref[...]
    gate, upward = [
        dot_f32(ref[:, own], near, TRANSPOSED) + dot_f32(ref[:, rest], near2, TRANSPOSED)
        for ref in (gate_ref, up_ref)
    ]
    out_ref[...] = gated(gate, upward)
    gate_part_ref[...] = dot_f32(gate_ref[:, own], far, TRANSPOSED)
    up_part_ref[...] = dot_f32(up_ref[:, own], far, TRANSPOSED)


def far_kernel(after_ref, far2_ref, gate_ref, up_ref, near_hidden_ref, gate_part_ref, up_part_ref, out_ref):
    count, width = far2_ref.shape
    rest = columns_of(1 - core(), width)
    far2 = far2_ref[...]
    gate, upward = [
        part_ref[...] + dot_f32(ref[:, rest], far2, TRANSPOSED)
        for ref, part_ref in ((gate_ref, gate_part_ref), (up_ref, up_part_ref))
    ]
    x = lax.axis_index("tok") & 1
    out_ref[:, columns_of(x, count)] = near_hidden_ref[...]
    out_ref[:, columns_of(1 - x, count)] = gated(gate, upward)


def features_kernel(*refs):
    hidden_refs, (kept_ref, with_z_ref, z_ref, early_ref, late_ref) = refs[:HOLDERS], refs[HOLDERS:][:5]
    block_refs, shares_hbm = refs[HOLDERS + 5 : 2 * HOLDERS + 5], refs[2 * HOLDERS + 5]
    route_ref, features_ref, whole_ref, shares_ref, sem = refs[2 * HOLDERS + 6 :]
    depth, tokens = hidden_refs[0].shape
    part, members = tokens // HOLDERS, lax.axis_size("tok")
    rows = tokens // members
    count, width = kept_ref.shape
    beside = (2 * count - z_ref.shape[0]) // 2
    x_block = jnp.concatenate([early_ref[count:], late_ref[...]])
    z_block = jnp.concatenate(
        [with_z_ref[rows:, :width], with_z_ref[rows:, width:], z_ref[: count - 2 * beside]]
    )
    downs = (kept_ref[...], x_block, z_block, z_ref[count - 2 * beside :])

    def place(m, piece):
        z = (holder() ^ m) * (members // HOLDERS // 2) + piece // 2
        return pl.ds(pl.multiple_of(piece % 2 * (tokens // 2) + z * rows, rows), rows)

    eye = lax.broadcasted_iota(jnp.int32, (part, part), 0) == lax.broadcasted_iota(
        jnp.int32, (part, part), 1
    )
    output = None
    for m, (hidden_ref, down) in enumerate(zip(hidden_refs, downs)):
        product = dot_f32(hidden_ref[...], down[:depth], (((0,), (0,)), ((), ())))
        output = product if output is None else output + product
        terms = down[depth:, :part].astype(f32)
        route = jnp.sum(terms[:HOLDERS], axis=0, keepdims=True)
        column = jnp.sum(jnp.where(eye, route, 0.0), axis=1, keepdims=True)
        column = jnp.broadcast_to(column, (part, LANES))
        for piece in range(part // rows):
            route_ref[place(m, piece)] = column[piece * rows : (piece + 1) * rows]
    features = (output * route_ref[:, :1]).astype(bf16)
    features_ref[...] = features
    wide = features.astype(f32)
    mean = jnp.sum(wide, axis=0, keepdims=True) / tokens
    column = jnp.sum(wide * mean, axis=1, keepdims=True)
    row = jnp.transpose(jnp.broadcast_to(column, (tokens, LANES)))[:1]
    gram = dot_f32(features, features, TRANSPOSED)
    whole_ref[...] = (gram - column - row + jnp.sum(mean * mean)).astype(bf16)
    at = 0
    for i in range(tokens // TILE):
        for j in range(tokens // LANES):
            shares_ref[at * TILE : (at + 1) * TILE] = whole_ref[
                i * TILE : (i + 1) * TILE, j * LANES : (j + 1) * LANES
            ]
            at += 1
    copy = pltpu.make_async_copy(shares_ref, shares_hbm, sem)
    copy.start()
    for m, block_ref in enumerate(block_refs):
        for piece in range(part // rows):
            block_ref[piece * rows : (piece + 1) * rows] = features_ref[place(m, piece)]
    copy.wait()


def place_kernel(*refs):
    blocks, out_ref, sems = refs[:HOLDERS], refs[HOLDERS], refs[HOLDERS + 1]
    width = blocks[0].shape[1]
    copies = []
    for m, block in enumerate(blocks):
        columns = pl.ds(pl.multiple_of((holder() ^ m) * width, width), width)
        copies.append(pltpu.make_async_copy(block, out_ref.at[:, columns], sems.at[m]))
        copies[-1].start()
    for copy in copies:
        copy.wait()


def pair_kernel(parts_ref, out_ref, flat_ref):
    experts = flat_ref.shape[0]
    parts = parts_ref[...].astype(f32)
    total = parts[:, 0]
    for m in range(1, parts.shape[1]):
        total = total + parts[:, m]
    flat_ref[...] = total.astype(bf16).astype(f32)
    in_row = out_ref.shape[1] == 1
    shape = (experts, out_ref.shape[2])
    row = lax.broadcasted_iota(jnp.int32, shape, 0)
    lane = lax.broadcasted_iota(jnp.int32, shape, 1)

    def one(expert, table):
        products = jnp.sum(flat_ref[...] * flat_ref[pl.ds(expert, 1)], axis=1)
        here = lane == expert * experts + row if in_row else lane == expert
        return jnp.where(here, jnp.sum(products, axis=1, keepdims=True), table)

    table = lax.fori_loop(0, experts, one, jnp.zeros(shape, f32), unroll=experts <= 8)
    if in_row:
        table = jnp.sum(table, axis=0, keepdims=True)
    out_ref[...] = jnp.broadcast_to(table[None], out_ref.shape)


def cka_kernel(tables_ref, out_ref):
    totals = jnp.sum(tables_ref[...], axis=0)
    shape = out_ref.shape
    row = lax.broadcasted_iota(jnp.int32, shape, 0)
    lane = lax.broadcasted_iota(jnp.int32, shape, 1)
    if totals.shape != shape:
        experts = shape[0]
        wide = (experts, totals.shape[1])
        spread = jnp.broadcast_to(totals, wide)
        at = lax.broadcasted_iota(jnp.int32, wide, 1) - experts * lax.broadcasted_iota(
            jnp.int32, wide, 0
        )
        totals = jnp.zeros(shape, f32)
        for column in range(experts):
            values = jnp.sum(jnp.where(at == column, spread, 0.0), axis=1, keepdims=True)
            totals = jnp.where(lane == column, values, totals)
    kept = jnp.where(row == lane, totals, 0.0)
    down = jnp.sum(kept, axis=1, keepdims=True)
    across = jnp.sum(kept, axis=0, keepdims=True)
    out_ref[...] = totals / jnp.sqrt(down * across)


def shards(probe_states, norm_gain, gate_weight, up_weight, down_weight, route_weight):
    groups, members = lax.axis_size("grp"), lax.axis_size("tok")
    devices = groups * members
    experts = devices // HOLDERS
    rows, model = probe_states.shape
    tokens = rows * members
    depth = gate_weight.shape[0]
    part, token_part = model // HOLDERS, tokens // HOLDERS

    count = depth + TILE
    beside, first_x = depth // 6 // TILE * TILE, depth // 2 // TILE * TILE
    own, with_z, down_own, down_z, down_early, down_late = call(
        first_kernel,
        [jax.ShapeDtypeStruct((n, model // 2), bf16) for n in (rows, rows + beside)]
        + [
            jax.ShapeDtypeStruct((n, part), bf16)
            for n in (count, count - 2 * beside, count + first_x, count - first_x)
        ],
        [HBM] * 4,
        [
            pltpu.with_memory_space_constraint(a, pltpu.HBM)
            for a in (probe_states, norm_gain[None, :], down_weight, route_weight)
        ],
        scratch=[
            pltpu.VMEM((rows, model), bf16),
            pltpu.VMEM((1, model), f32),
            pltpu.VMEM(route_weight.shape, f32),
            pltpu.SemaphoreType.DMA((10,)),
        ],
    )
    down_early = swapped(down_early, "tok", 1)
    with_z = swapped(with_z, "tok", 2)
    pieces = [swapped(own, "tok", 2 * m) for m in range(members // 2 - 1, 1, -1)] + [with_z, own]
    near = call(
        stack_kernel,
        jax.ShapeDtypeStruct((tokens // 2, model // 2), bf16),
        [ANY] + [VMEM] * len(pieces),
        (down_early, *pieces),
    )
    far = swapped(near, "tok", 1)
    near2 = swapped(near, "grp", 1)
    down_z = call(
        join_kernel,
        jax.ShapeDtypeStruct((2 * (count - beside), part), bf16),
        [ANY, VMEM, VMEM],
        (near, down_z, down_early),
    )
    down_z = swapped(down_z, "tok", 2)
    down_late = swapped(held(down_late, far), "tok", 1)
    half_shape = (depth, tokens // 2)
    near_hidden, gate_part, up_part = call(
        near_kernel,
        [jax.ShapeDtypeStruct(half_shape, dtype) for dtype in (bf16, f32, f32)],
        [VMEM] * 5,
        (near, near2, far, gate_weight, up_weight),
    )
    hidden = call(
        far_kernel,
        jax.ShapeDtypeStruct((depth, tokens), bf16),
        [ANY] + [VMEM] * 6,
        (down_z, swapped(far, "grp", 1), gate_weight, up_weight, near_hidden, gate_part, up_part),
    )
    hiddens = [swapped(hidden, "tok", m) if m else hidden for m in range(HOLDERS)]
    entries = tokens * tokens // LANES
    *blocks, centered = call(
        features_kernel,
        [jax.ShapeDtypeStruct((token_part, part), bf16)] * HOLDERS
        + [jax.ShapeDtypeStruct((entries, LANES), bf16)],
        [VMEM] * (HOLDERS + 5),
        (*hiddens, down_own, with_z, down_z, down_early, down_late),
        out_specs=[VMEM] * HOLDERS + [HBM],
        scratch=[
            pltpu.VMEM((tokens, LANES), f32),
            pltpu.VMEM((tokens, part), bf16),
            pltpu.VMEM((tokens, tokens), bf16),
            pltpu.VMEM((entries, LANES), bf16),
            pltpu.SemaphoreType.DMA,
        ],
    )
    arrived = lax.all_to_all(centered, ("grp", "tok"), split_axis=0, concat_axis=0, tiled=True)
    arrived = arrived.reshape(experts, HOLDERS, entries // devices, LANES)
    direct = experts * experts <= LANES
    tables = call(
        pair_kernel,
        jax.ShapeDtypeStruct((devices, 1, LANES) if direct else (1, experts, experts), f32),
        [VMEM],
        (arrived,),
        scratch=[pltpu.VMEM((experts, entries // devices, LANES), f32)],
    )
    if direct:
        tables = lax.all_to_all(tables, ("grp", "tok"), split_axis=0, concat_axis=0, tiled=True)
    else:
        tables = lax.psum(tables, ("grp", "tok"))
    cka = call(cka_kernel, jax.ShapeDtypeStruct((experts, experts), f32), [VMEM], (tables,))

    blocks = [swapped(b, "tok", m) if m else b for m, b in enumerate(blocks)]
    features = call(
        place_kernel,
        jax.ShapeDtypeStruct((token_part, model), bf16),
        [VMEM] * HOLDERS,
        blocks,
        out_specs=ANY,
        scratch=[pltpu.SemaphoreType.DMA((HOLDERS,))],
    )
    return (features, cka)


def solution(mesh):
    return jax.shard_map(
        shards,
        mesh=mesh,
        in_specs=(
            P("tok", None),
            P(),
            P(("grp", "tok"), None),
            P(("grp", "tok"), None),
            P(("grp", "tok"), None),
            P(("grp", "tok"), None),
        ),
        out_specs=(P(("grp", "tok"), None), P()),
        check_vma=False,
    )
```

```python
import jax
import jax.numpy as jnp
from jax import lax
from jax.experimental import pallas as pl
from jax.experimental.pallas import tpu as pltpu
from jax.sharding import PartitionSpec as P

HOLDERS = 4
LANES = 128
TILE = 16
BIG = 24 * 1024 * 1024
TRANSPOSED = (((1,), (1,)), ((), ()))
VMEM = pl.BlockSpec(memory_space=pltpu.VMEM)
ANY = pl.BlockSpec(memory_space=pl.ANY)
HBM = pl.BlockSpec(memory_space=pltpu.HBM)
bf16 = jnp.bfloat16
f32 = jnp.float32


def swapped(array, axis, mask):
    return lax.ppermute(array, axis, [(i, i ^ mask) for i in range(lax.axis_size(axis))])


def dot_f32(a, b, dims):
    return lax.dot_general(a, b, dims, preferred_element_type=f32)


def call(body, outs, in_specs, operands, out_specs=None, scratch=(), aliases={}):
    return pl.pallas_call(
        body,
        out_shape=outs,
        in_specs=in_specs,
        out_specs=jax.tree.map(lambda _: VMEM, outs) if out_specs is None else out_specs,
        scratch_shapes=list(scratch),
        compiler_params=pltpu.CompilerParams(vmem_limit_bytes=BIG),
        input_output_aliases=aliases,
    )(*operands)


def core():
    return lax.axis_index("grp") & 1


def holder():
    return lax.axis_index("tok") & (HOLDERS - 1)


def columns_of(half, width):
    return pl.ds(pl.multiple_of(half * width, width), width)


def first_kernel(states_hbm, gain_hbm, down_hbm, route_hbm, out_ref, *refs):
    with_z_ref, kept_ref, z_ref, early_ref, late_ref = refs[:5]
    states_ref, gain_ref, route_ref, sems = refs[5:]
    depth, width = down_hbm.shape[0], kept_ref.shape[1]
    rows, count = states_ref.shape[0], depth + TILE
    beside, first_x = with_z_ref.shape[0] - rows, early_ref.shape[0] - count
    left, right = with_z_ref.at[pl.ds(rows, beside), pl.ds(0, width)], with_z_ref.at[
        pl.ds(rows, beside), pl.ds(width, width)
    ]
    blocks = (
        (0, 0, depth, kept_ref.at[pl.ds(0, depth)]),
        (2, 0, beside, left),
        (2, beside, beside, right),
        (2, 2 * beside, depth - 2 * beside, z_ref.at[pl.ds(0, depth - 2 * beside)]),
        (3, 0, depth, early_ref.at[pl.ds(0, depth)]),
        (1, 0, first_x, early_ref.at[pl.ds(count, first_x)]),
        (1, first_x, depth - first_x, late_ref.at[pl.ds(0, depth - first_x)]),
    )
    copies = [
        pltpu.make_async_copy(states_hbm, states_ref, sems.at[0]),
        pltpu.make_async_copy(gain_hbm, gain_ref, sems.at[1]),
        pltpu.make_async_copy(route_hbm, route_ref, sems.at[2]),
    ]
    for at, (m, top, size, block) in enumerate(blocks):
        source = down_hbm.at[pl.ds(top, size), columns_of(holder() ^ m, width)]
        copies.append(pltpu.make_async_copy(source, block, sems.at[3 + at]))
    for copy in copies:
        copy.start()
    for copy in copies[:3]:
        copy.wait()
    states = states_ref[...].astype(f32)
    scale = lax.rsqrt(jnp.mean(states * states, axis=1, keepdims=True) + 1e-06)
    own = columns_of(core(), out_ref.shape[1])
    normed = (states_ref[:, own].astype(f32) * scale * gain_ref[:, own]).astype(bf16)
    out_ref[...] = normed
    with_z_ref[:rows] = normed
    route = route_ref[...]
    high = route.astype(bf16).astype(f32)
    middle = (route - high).astype(bf16).astype(f32)
    low = route - high - middle
    part = route.shape[1]
    row = lax.broadcasted_iota(jnp.int32, (TILE, part), 0)
    terms = jnp.where(row == 0, high, jnp.where(row == 1, middle, jnp.where(row == 2, low, 0.0)))
    terms = jnp.concatenate([terms, jnp.zeros((TILE, width - part), f32)], 1)
    for ref, top in (
        (kept_ref, depth),
        (z_ref, depth - 2 * beside),
        (early_ref, depth),
        (late_ref, depth - first_x),
    ):
        ref[top : top + TILE] = terms.astype(bf16)
    for copy in copies[3:]:
        copy.wait()


def hold_kernel(*refs):
    pass


def held(array, after):
    return call(
        hold_kernel,
        jax.ShapeDtypeStruct(array.shape, array.dtype),
        [ANY] * 2,
        (array, after),
        out_specs=ANY,
        aliases={0: 0},
    )


def join_kernel(after_ref, first_ref, second_ref, out_ref):
    count = first_ref.shape[0]
    out_ref[:count] = first_ref[...]
    out_ref[count:] = second_ref[: out_ref.shape[0] - count]


def stack_kernel(after_ref, *refs):
    rows = refs[-2].shape[0]
    z = lax.axis_index("tok") >> 1
    for m, piece in enumerate(refs[-2::-1]):
        refs[-1][pl.ds(pl.multiple_of((z ^ m) * rows, rows), rows)] = piece[:rows]


def gated(gate, upward):
    return (gate / (1.0 + jnp.exp(-gate)) * upward).astype(bf16)


def near_kernel(near_ref, near2_ref, far_ref, gate_ref, up_ref, out_ref, gate_part_ref, up_part_ref):
    width = near_ref.shape[1]
    own, rest = columns_of(core(), width), columns_of(1 - core(), width)
    near, near2, far = near_ref[...], near2_ref[...], far_ref[...]
    gate, upward = [
        dot_f32(ref[:, own], near, TRANSPOSED) + dot_f32(ref[:, rest], near2, TRANSPOSED)
        for ref in (gate_ref, up_ref)
    ]
    out_ref[...] = gated(gate, upward)
    gate_part_ref[...] = dot_f32(gate_ref[:, own], far, TRANSPOSED)
    up_part_ref[...] = dot_f32(up_ref[:, own], far, TRANSPOSED)


def far_kernel(after_ref, far2_ref, gate_ref, up_ref, near_hidden_ref, gate_part_ref, up_part_ref, out_ref):
    count, width = far2_ref.shape
    rest = columns_of(1 - core(), width)
    far2 = far2_ref[...]
    gate, upward = [
        part_ref[...] + dot_f32(ref[:, rest], far2, TRANSPOSED)
        for ref, part_ref in ((gate_ref, gate_part_ref), (up_ref, up_part_ref))
    ]
    x = lax.axis_index("tok") & 1
    out_ref[:, columns_of(x, count)] = near_hidden_ref[...]
    out_ref[:, columns_of(1 - x, count)] = gated(gate, upward)


def features_kernel(*refs):
    hidden_refs, (kept_ref, with_z_ref, z_ref, early_ref, late_ref) = refs[:HOLDERS], refs[HOLDERS:][:5]
    block_refs, shares_hbm = refs[HOLDERS + 5 : 2 * HOLDERS + 5], refs[2 * HOLDERS + 5]
    route_ref, features_ref, whole_ref, shares_ref, sem = refs[2 * HOLDERS + 6 :]
    depth, tokens = hidden_refs[0].shape
    part, members = tokens // HOLDERS, lax.axis_size("tok")
    rows = tokens // members
    count, width = kept_ref.shape
    beside = (2 * count - z_ref.shape[0]) // 2
    x_block = jnp.concatenate([early_ref[count:], late_ref[...]])
    z_block = jnp.concatenate(
        [with_z_ref[rows:, :width], with_z_ref[rows:, width:], z_ref[: count - 2 * beside]]
    )
    downs = (kept_ref[...], x_block, z_block, z_ref[count - 2 * beside :])

    def place(m, piece):
        z = (holder() ^ m) * (members // HOLDERS // 2) + piece // 2
        return pl.ds(pl.multiple_of(piece % 2 * (tokens // 2) + z * rows, rows), rows)

    eye = lax.broadcasted_iota(jnp.int32, (part, part), 0) == lax.broadcasted_iota(
        jnp.int32, (part, part), 1
    )
    output = None
    for m, (hidden_ref, down) in enumerate(zip(hidden_refs, downs)):
        product = dot_f32(hidden_ref[...], down[:depth], (((0,), (0,)), ((), ())))
        output = product if output is None else output + product
        terms = down[depth:, :part].astype(f32)
        route = jnp.sum(terms[:HOLDERS], axis=0, keepdims=True)
        column = jnp.sum(jnp.where(eye, route, 0.0), axis=1, keepdims=True)
        column = jnp.broadcast_to(column, (part, LANES))
        for piece in range(part // rows):
            route_ref[place(m, piece)] = column[piece * rows : (piece + 1) * rows]
    features = (output * route_ref[:, :1]).astype(bf16)
    features_ref[...] = features
    wide = features.astype(f32)
    mean = jnp.sum(wide, axis=0, keepdims=True) / tokens
    column = jnp.sum(wide * mean, axis=1, keepdims=True)
    row = jnp.transpose(jnp.broadcast_to(column, (tokens, LANES)))[:1]
    gram = dot_f32(features, features, TRANSPOSED)
    whole_ref[...] = (gram - column - row + jnp.sum(mean * mean)).astype(bf16)
    at = 0
    for i in range(tokens // TILE):
        for j in range(tokens // LANES):
            shares_ref[at * TILE : (at + 1) * TILE] = whole_ref[
                i * TILE : (i + 1) * TILE, j * LANES : (j + 1) * LANES
            ]
            at += 1
    copy = pltpu.make_async_copy(shares_ref, shares_hbm, sem)
    copy.start()
    for m, block_ref in enumerate(block_refs):
        for piece in range(part // rows):
            block_ref[piece * rows : (piece + 1) * rows] = features_ref[place(m, piece)]
    copy.wait()


def place_kernel(*refs):
    blocks, out_ref, sems = refs[:HOLDERS], refs[HOLDERS], refs[HOLDERS + 1]
    width = blocks[0].shape[1]
    copies = []
    for m, block in enumerate(blocks):
        columns = pl.ds(pl.multiple_of((holder() ^ m) * width, width), width)
        copies.append(pltpu.make_async_copy(block, out_ref.at[:, columns], sems.at[m]))
        copies[-1].start()
    for copy in copies:
        copy.wait()


def pair_kernel(parts_ref, out_ref, flat_ref):
    experts = flat_ref.shape[0]
    parts = parts_ref[...].astype(f32)
    total = parts[:, 0]
    for m in range(1, parts.shape[1]):
        total = total + parts[:, m]
    flat_ref[...] = total.astype(bf16).astype(f32)
    in_row = out_ref.shape[1] == 1
    shape = (experts, out_ref.shape[2])
    row = lax.broadcasted_iota(jnp.int32, shape, 0)
    lane = lax.broadcasted_iota(jnp.int32, shape, 1)

    def one(expert, table):
        products = jnp.sum(flat_ref[...] * flat_ref[pl.ds(expert, 1)], axis=1)
        here = lane == expert * experts + row if in_row else lane == expert
        return jnp.where(here, jnp.sum(products, axis=1, keepdims=True), table)

    table = lax.fori_loop(0, experts, one, jnp.zeros(shape, f32), unroll=experts <= 8)
    if in_row:
        table = jnp.sum(table, axis=0, keepdims=True)
    out_ref[...] = jnp.broadcast_to(table[None], out_ref.shape)


def cka_kernel(tables_ref, out_ref):
    totals = jnp.sum(tables_ref[...], axis=0)
    shape = out_ref.shape
    row = lax.broadcasted_iota(jnp.int32, shape, 0)
    lane = lax.broadcasted_iota(jnp.int32, shape, 1)
    if totals.shape != shape:
        experts = shape[0]
        wide = (experts, totals.shape[1])
        spread = jnp.broadcast_to(totals, wide)
        at = lax.broadcasted_iota(jnp.int32, wide, 1) - experts * lax.broadcasted_iota(
            jnp.int32, wide, 0
        )
        totals = jnp.zeros(shape, f32)
        for column in range(experts):
            values = jnp.sum(jnp.where(at == column, spread, 0.0), axis=1, keepdims=True)
            totals = jnp.where(lane == column, values, totals)
    kept = jnp.where(row == lane, totals, 0.0)
    down = jnp.sum(kept, axis=1, keepdims=True)
    across = jnp.sum(kept, axis=0, keepdims=True)
    out_ref[...] = totals / jnp.sqrt(down * across)


def shards(probe_states, norm_gain, gate_weight, up_weight, down_weight, route_weight):
    groups, members = lax.axis_size("grp"), lax.axis_size("tok")
    devices = groups * members
    experts = devices // HOLDERS
    rows, model = probe_states.shape
    tokens = rows * members
    depth = gate_weight.shape[0]
    part, token_part = model // HOLDERS, tokens // HOLDERS

    count = depth + TILE
    beside, first_x = depth // 4 // TILE * TILE, depth // 2 // TILE * TILE
    own, with_z, down_own, down_z, down_early, down_late = call(
        first_kernel,
        [jax.ShapeDtypeStruct((n, model // 2), bf16) for n in (rows, rows + beside)]
        + [
            jax.ShapeDtypeStruct((n, part), bf16)
            for n in (count, count - 2 * beside, count + first_x, count - first_x)
        ],
        [HBM] * 4,
        [
            pltpu.with_memory_space_constraint(a, pltpu.HBM)
            for a in (probe_states, norm_gain[None, :], down_weight, route_weight)
        ],
        scratch=[
            pltpu.VMEM((rows, model), bf16),
            pltpu.VMEM((1, model), f32),
            pltpu.VMEM(route_weight.shape, f32),
            pltpu.SemaphoreType.DMA((10,)),
        ],
    )
    down_early = swapped(down_early, "tok", 1)
    with_z = swapped(with_z, "tok", 2)
    pieces = [swapped(own, "tok", 2 * m) for m in range(members // 2 - 1, 1, -1)] + [with_z, own]
    near = call(
        stack_kernel,
        jax.ShapeDtypeStruct((tokens // 2, model // 2), bf16),
        [ANY] + [VMEM] * len(pieces),
        (down_early, *pieces),
    )
    far = swapped(near, "tok", 1)
    near2 = swapped(near, "grp", 1)
    down_z = call(
        join_kernel,
        jax.ShapeDtypeStruct((2 * (count - beside), part), bf16),
        [ANY, VMEM, VMEM],
        (near, down_z, down_early),
    )
    down_z = swapped(down_z, "tok", 2)
    down_late = swapped(held(down_late, far), "tok", 1)
    half_shape = (depth, tokens // 2)
    near_hidden, gate_part, up_part = call(
        near_kernel,
        [jax.ShapeDtypeStruct(half_shape, dtype) for dtype in (bf16, f32, f32)],
        [VMEM] * 5,
        (near, near2, far, gate_weight, up_weight),
    )
    hidden = call(
        far_kernel,
        jax.ShapeDtypeStruct((depth, tokens), bf16),
        [ANY] + [VMEM] * 6,
        (down_z, swapped(far, "grp", 1), gate_weight, up_weight, near_hidden, gate_part, up_part),
    )
    hiddens = [swapped(hidden, "tok", m) if m else hidden for m in range(HOLDERS)]
    entries = tokens * tokens // LANES
    *blocks, centered = call(
        features_kernel,
        [jax.ShapeDtypeStruct((token_part, part), bf16)] * HOLDERS
        + [jax.ShapeDtypeStruct((entries, LANES), bf16)],
        [VMEM] * (HOLDERS + 5),
        (*hiddens, down_own, with_z, down_z, down_early, down_late),
        out_specs=[VMEM] * HOLDERS + [HBM],
        scratch=[
            pltpu.VMEM((tokens, LANES), f32),
            pltpu.VMEM((tokens, part), bf16),
            pltpu.VMEM((tokens, tokens), bf16),
            pltpu.VMEM((entries, LANES), bf16),
            pltpu.SemaphoreType.DMA,
        ],
    )
    arrived = lax.all_to_all(centered, ("grp", "tok"), split_axis=0, concat_axis=0, tiled=True)
    arrived = arrived.reshape(experts, HOLDERS, entries // devices, LANES)
    direct = experts * experts <= LANES
    tables = call(
        pair_kernel,
        jax.ShapeDtypeStruct((devices, 1, LANES) if direct else (1, experts, experts), f32),
        [VMEM],
        (arrived,),
        scratch=[pltpu.VMEM((experts, entries // devices, LANES), f32)],
    )
    if direct:
        tables = lax.all_to_all(tables, ("grp", "tok"), split_axis=0, concat_axis=0, tiled=True)
    else:
        tables = lax.psum(tables, ("grp", "tok"))
    cka = call(cka_kernel, jax.ShapeDtypeStruct((experts, experts), f32), [VMEM], (tables,))

    blocks = [swapped(b, "tok", m) if m else b for m, b in enumerate(blocks)]
    features = call(
        place_kernel,
        jax.ShapeDtypeStruct((token_part, model), bf16),
        [VMEM] * HOLDERS,
        blocks,
        out_specs=ANY,
        scratch=[pltpu.SemaphoreType.DMA((HOLDERS,))],
    )
    return (features, cka)


def solution(mesh):
    return jax.shard_map(
        shards,
        mesh=mesh,
        in_specs=(
            P("tok", None),
            P(),
            P(("grp", "tok"), None),
            P(("grp", "tok"), None),
            P(("grp", "tok"), None),
            P(("grp", "tok"), None),
        ),
        out_specs=(P(("grp", "tok"), None), P()),
        check_vma=False,
    )
```

```python
import jax
import jax.numpy as jnp
from jax import lax
from jax.experimental import pallas as pl
from jax.experimental.pallas import tpu as pltpu
from jax.sharding import PartitionSpec as P

HOLDERS = 4
ORDER = (0, 2, 3, 1)
LANES = 128
TILE = 16
BIG = 24 * 1024 * 1024
TRANSPOSED = (((1,), (1,)), ((), ()))
VMEM = pl.BlockSpec(memory_space=pltpu.VMEM)
ANY = pl.BlockSpec(memory_space=pl.ANY)
HBM = pl.BlockSpec(memory_space=pltpu.HBM)
bf16 = jnp.bfloat16
f32 = jnp.float32


def swapped(array, axis, mask):
    return lax.ppermute(array, axis, [(i, i ^ mask) for i in range(lax.axis_size(axis))])


def dot_f32(a, b, dims):
    return lax.dot_general(a, b, dims, preferred_element_type=f32)


def call(body, outs, in_specs, operands, out_specs=None, scratch=(), aliases={}):
    return pl.pallas_call(
        body,
        out_shape=outs,
        in_specs=in_specs,
        out_specs=jax.tree.map(lambda _: VMEM, outs) if out_specs is None else out_specs,
        scratch_shapes=list(scratch),
        compiler_params=pltpu.CompilerParams(vmem_limit_bytes=BIG),
        input_output_aliases=aliases,
    )(*operands)


def core():
    return lax.axis_index("grp") & 1


def holder():
    return lax.axis_index("tok") & (HOLDERS - 1)


def columns_of(half, width):
    return pl.ds(pl.multiple_of(half * width, width), width)


def first_kernel(states_hbm, gain_hbm, down_hbm, route_hbm, out_ref, *refs):
    with_z_ref, kept_ref, z_ref, early_ref, late_ref = refs[:5]
    states_ref, gain_ref, route_ref, sems = refs[5:]
    depth, width = down_hbm.shape[0], kept_ref.shape[1]
    rows, count = states_ref.shape[0], depth + TILE
    beside, first_x = with_z_ref.shape[0] - rows, early_ref.shape[0] - count
    left, right = with_z_ref.at[pl.ds(rows, beside), pl.ds(0, width)], with_z_ref.at[
        pl.ds(rows, beside), pl.ds(width, width)
    ]
    blocks = (
        (0, 0, depth, kept_ref.at[pl.ds(0, depth)]),
        (2, 0, beside, left),
        (2, beside, beside, right),
        (2, 2 * beside, depth - 2 * beside, z_ref.at[pl.ds(0, depth - 2 * beside)]),
        (3, 0, depth, early_ref.at[pl.ds(0, depth)]),
        (1, 0, first_x, early_ref.at[pl.ds(count, first_x)]),
        (1, first_x, depth - first_x, late_ref.at[pl.ds(0, depth - first_x)]),
    )
    copies = [
        pltpu.make_async_copy(states_hbm, states_ref, sems.at[0]),
        pltpu.make_async_copy(gain_hbm, gain_ref, sems.at[1]),
        pltpu.make_async_copy(route_hbm, route_ref, sems.at[2]),
    ]
    for at, (m, top, size, block) in enumerate(blocks):
        source = down_hbm.at[pl.ds(top, size), columns_of(holder() ^ m, width)]
        copies.append(pltpu.make_async_copy(source, block, sems.at[3 + at]))
    for copy in copies:
        copy.start()
    for copy in copies[:3]:
        copy.wait()
    states = states_ref[...].astype(f32)
    scale = lax.rsqrt(jnp.mean(states * states, axis=1, keepdims=True) + 1e-06)
    own = columns_of(core(), out_ref.shape[1])
    normed = (states_ref[:, own].astype(f32) * scale * gain_ref[:, own]).astype(bf16)
    out_ref[...] = normed
    with_z_ref[:rows] = normed
    route = route_ref[...]
    high = route.astype(bf16).astype(f32)
    middle = (route - high).astype(bf16).astype(f32)
    low = route - high - middle
    part = route.shape[1]
    row = lax.broadcasted_iota(jnp.int32, (TILE, part), 0)
    terms = jnp.where(row == 0, high, jnp.where(row == 1, middle, jnp.where(row == 2, low, 0.0)))
    terms = jnp.concatenate([terms, jnp.zeros((TILE, width - part), f32)], 1)
    for ref, top in (
        (kept_ref, depth),
        (z_ref, depth - 2 * beside),
        (early_ref, depth),
        (late_ref, depth - first_x),
    ):
        ref[top : top + TILE] = terms.astype(bf16)
    for copy in copies[3:]:
        copy.wait()


def hold_kernel(*refs):
    pass


def held(array, after):
    return call(
        hold_kernel,
        jax.ShapeDtypeStruct(array.shape, array.dtype),
        [ANY] * 2,
        (array, after),
        out_specs=ANY,
        aliases={0: 0},
    )


def join_kernel(after_ref, first_ref, second_ref, out_ref):
    count = first_ref.shape[0]
    out_ref[:count] = first_ref[...]
    out_ref[count:] = second_ref[: out_ref.shape[0] - count]


def stack_kernel(after_ref, *refs):
    rows = refs[-2].shape[0]
    z = lax.axis_index("tok") >> 1
    for m, piece in enumerate(refs[-2::-1]):
        refs[-1][pl.ds(pl.multiple_of((z ^ m) * rows, rows), rows)] = piece[:rows]


def gated(gate, upward):
    return (gate / (1.0 + jnp.exp(-gate)) * upward).astype(bf16)


def near_kernel(near_ref, near2_ref, far_ref, gate_ref, up_ref, out_ref, gate_part_ref, up_part_ref):
    width = near_ref.shape[1]
    own, rest = columns_of(core(), width), columns_of(1 - core(), width)
    near, near2, far = near_ref[...], near2_ref[...], far_ref[...]
    gate, upward = [
        dot_f32(ref[:, own], near, TRANSPOSED) + dot_f32(ref[:, rest], near2, TRANSPOSED)
        for ref in (gate_ref, up_ref)
    ]
    out_ref[...] = gated(gate, upward)
    gate_part_ref[...] = dot_f32(gate_ref[:, own], far, TRANSPOSED)
    up_part_ref[...] = dot_f32(up_ref[:, own], far, TRANSPOSED)


def far_kernel(after_ref, far2_ref, gate_ref, up_ref, near_hidden_ref, gate_part_ref, up_part_ref, out_ref):
    count, width = far2_ref.shape
    rest = columns_of(1 - core(), width)
    far2 = far2_ref[...]
    gate, upward = [
        part_ref[...] + dot_f32(ref[:, rest], far2, TRANSPOSED)
        for ref, part_ref in ((gate_ref, gate_part_ref), (up_ref, up_part_ref))
    ]
    x = lax.axis_index("tok") & 1
    out_ref[:, columns_of(x, count)] = near_hidden_ref[...]
    out_ref[:, columns_of(1 - x, count)] = gated(gate, upward)


def features_kernel(*refs):
    hidden_refs, (kept_ref, with_z_ref, z_ref, early_ref, late_ref) = refs[:HOLDERS], refs[HOLDERS:][:5]
    block_refs, shares_hbm = refs[HOLDERS + 5 : 2 * HOLDERS + 5], refs[2 * HOLDERS + 5]
    route_ref, features_ref, whole_ref, shares_ref, sem = refs[2 * HOLDERS + 6 :]
    depth, tokens = hidden_refs[0].shape
    part, members = tokens // HOLDERS, lax.axis_size("tok")
    rows = tokens // members
    count, width = kept_ref.shape
    beside = (2 * count - z_ref.shape[0]) // 2
    x_block = jnp.concatenate([early_ref[count:], late_ref[...]])
    z_block = jnp.concatenate(
        [with_z_ref[rows:, :width], with_z_ref[rows:, width:], z_ref[: count - 2 * beside]]
    )
    downs = (kept_ref[...], x_block, z_block, z_ref[count - 2 * beside :])

    def place(m, piece):
        z = (holder() ^ m) * (members // HOLDERS // 2) + piece // 2
        return pl.ds(pl.multiple_of(piece % 2 * (tokens // 2) + z * rows, rows), rows)

    eye = lax.broadcasted_iota(jnp.int32, (part, part), 0) == lax.broadcasted_iota(
        jnp.int32, (part, part), 1
    )
    output = None
    for m, hidden_ref in zip(ORDER, hidden_refs):
        down = downs[m]
        product = dot_f32(hidden_ref[...], down[:depth], (((0,), (0,)), ((), ())))
        output = product if output is None else output + product
        terms = down[depth:, :part].astype(f32)
        route = jnp.sum(terms[:HOLDERS], axis=0, keepdims=True)
        column = jnp.sum(jnp.where(eye, route, 0.0), axis=1, keepdims=True)
        column = jnp.broadcast_to(column, (part, LANES))
        for piece in range(part // rows):
            route_ref[place(m, piece)] = column[piece * rows : (piece + 1) * rows]
    features = (output * route_ref[:, :1]).astype(bf16)
    features_ref[...] = features
    wide = features.astype(f32)
    mean = jnp.sum(wide, axis=0, keepdims=True) / tokens
    column = jnp.sum(wide * mean, axis=1, keepdims=True)
    row = jnp.transpose(jnp.broadcast_to(column, (tokens, LANES)))[:1]
    gram = dot_f32(features, features, TRANSPOSED)
    whole_ref[...] = (gram - column - row + jnp.sum(mean * mean)).astype(bf16)
    at = 0
    for i in range(tokens // TILE):
        for j in range(tokens // LANES):
            shares_ref[at * TILE : (at + 1) * TILE] = whole_ref[
                i * TILE : (i + 1) * TILE, j * LANES : (j + 1) * LANES
            ]
            at += 1
    copy = pltpu.make_async_copy(shares_ref, shares_hbm, sem)
    copy.start()
    for m, block_ref in enumerate(block_refs):
        for piece in range(part // rows):
            block_ref[piece * rows : (piece + 1) * rows] = features_ref[place(m, piece)]
    copy.wait()


def place_kernel(*refs):
    blocks, out_ref, sems = refs[:HOLDERS], refs[HOLDERS], refs[HOLDERS + 1]
    width = blocks[0].shape[1]
    copies = []
    for m, block in enumerate(blocks):
        columns = pl.ds(pl.multiple_of((holder() ^ m) * width, width), width)
        copies.append(pltpu.make_async_copy(block, out_ref.at[:, columns], sems.at[m]))
        copies[-1].start()
    for copy in copies:
        copy.wait()


def pair_kernel(parts_ref, out_ref, flat_ref):
    experts = flat_ref.shape[0]
    parts = parts_ref[...].astype(f32)
    total = parts[:, 0]
    for m in range(1, parts.shape[1]):
        total = total + parts[:, m]
    flat_ref[...] = total.astype(bf16).astype(f32)
    in_row = out_ref.shape[1] == 1
    shape = (experts, out_ref.shape[2])
    row = lax.broadcasted_iota(jnp.int32, shape, 0)
    lane = lax.broadcasted_iota(jnp.int32, shape, 1)

    def one(expert, table):
        products = jnp.sum(flat_ref[...] * flat_ref[pl.ds(expert, 1)], axis=1)
        here = lane == expert * experts + row if in_row else lane == expert
        return jnp.where(here, jnp.sum(products, axis=1, keepdims=True), table)

    table = lax.fori_loop(0, experts, one, jnp.zeros(shape, f32), unroll=experts <= 8)
    if in_row:
        table = jnp.sum(table, axis=0, keepdims=True)
    out_ref[...] = jnp.broadcast_to(table[None], out_ref.shape)


def cka_kernel(tables_ref, out_ref):
    totals = jnp.sum(tables_ref[...], axis=0)
    shape = out_ref.shape
    row = lax.broadcasted_iota(jnp.int32, shape, 0)
    lane = lax.broadcasted_iota(jnp.int32, shape, 1)
    if totals.shape != shape:
        experts = shape[0]
        wide = (experts, totals.shape[1])
        spread = jnp.broadcast_to(totals, wide)
        at = lax.broadcasted_iota(jnp.int32, wide, 1) - experts * lax.broadcasted_iota(
            jnp.int32, wide, 0
        )
        totals = jnp.zeros(shape, f32)
        for column in range(experts):
            values = jnp.sum(jnp.where(at == column, spread, 0.0), axis=1, keepdims=True)
            totals = jnp.where(lane == column, values, totals)
    kept = jnp.where(row == lane, totals, 0.0)
    down = jnp.sum(kept, axis=1, keepdims=True)
    across = jnp.sum(kept, axis=0, keepdims=True)
    out_ref[...] = totals / jnp.sqrt(down * across)


def shards(probe_states, norm_gain, gate_weight, up_weight, down_weight, route_weight):
    groups, members = lax.axis_size("grp"), lax.axis_size("tok")
    devices = groups * members
    experts = devices // HOLDERS
    rows, model = probe_states.shape
    tokens = rows * members
    depth = gate_weight.shape[0]
    part, token_part = model // HOLDERS, tokens // HOLDERS

    count = depth + TILE
    beside, first_x = depth // 4 // TILE * TILE, depth // 2 // TILE * TILE
    own, with_z, down_own, down_z, down_early, down_late = call(
        first_kernel,
        [jax.ShapeDtypeStruct((n, model // 2), bf16) for n in (rows, rows + beside)]
        + [
            jax.ShapeDtypeStruct((n, part), bf16)
            for n in (count, count - 2 * beside, count + first_x, count - first_x)
        ],
        [HBM] * 4,
        [
            pltpu.with_memory_space_constraint(a, pltpu.HBM)
            for a in (probe_states, norm_gain[None, :], down_weight, route_weight)
        ],
        scratch=[
            pltpu.VMEM((rows, model), bf16),
            pltpu.VMEM((1, model), f32),
            pltpu.VMEM(route_weight.shape, f32),
            pltpu.SemaphoreType.DMA((10,)),
        ],
    )
    down_early = swapped(down_early, "tok", 1)
    with_z = swapped(with_z, "tok", 2)
    pieces = [swapped(own, "tok", 2 * m) for m in range(members // 2 - 1, 1, -1)] + [with_z, own]
    near = call(
        stack_kernel,
        jax.ShapeDtypeStruct((tokens // 2, model // 2), bf16),
        [ANY] + [VMEM] * len(pieces),
        (down_early, *pieces),
    )
    far = swapped(near, "tok", 1)
    near2 = swapped(near, "grp", 1)
    down_z = call(
        join_kernel,
        jax.ShapeDtypeStruct((2 * (count - beside), part), bf16),
        [ANY, VMEM, VMEM],
        (near, down_z, down_early),
    )
    down_z = swapped(down_z, "tok", 2)
    down_late = swapped(held(down_late, far), "tok", 1)
    half_shape = (depth, tokens // 2)
    near_hidden, gate_part, up_part = call(
        near_kernel,
        [jax.ShapeDtypeStruct(half_shape, dtype) for dtype in (bf16, f32, f32)],
        [VMEM] * 5,
        (near, near2, far, gate_weight, up_weight),
    )
    hidden = call(
        far_kernel,
        jax.ShapeDtypeStruct((depth, tokens), bf16),
        [ANY] + [VMEM] * 6,
        (down_z, swapped(far, "grp", 1), gate_weight, up_weight, near_hidden, gate_part, up_part),
    )
    hiddens = [swapped(hidden, "tok", m) if m else hidden for m in ORDER]
    entries = tokens * tokens // LANES
    *blocks, centered = call(
        features_kernel,
        [jax.ShapeDtypeStruct((token_part, part), bf16)] * HOLDERS
        + [jax.ShapeDtypeStruct((entries, LANES), bf16)],
        [VMEM] * (HOLDERS + 5),
        (*hiddens, down_own, with_z, down_z, down_early, down_late),
        out_specs=[VMEM] * HOLDERS + [HBM],
        scratch=[
            pltpu.VMEM((tokens, LANES), f32),
            pltpu.VMEM((tokens, part), bf16),
            pltpu.VMEM((tokens, tokens), bf16),
            pltpu.VMEM((entries, LANES), bf16),
            pltpu.SemaphoreType.DMA,
        ],
    )
    arrived = lax.all_to_all(centered, ("grp", "tok"), split_axis=0, concat_axis=0, tiled=True)
    arrived = arrived.reshape(experts, HOLDERS, entries // devices, LANES)
    direct = experts * experts <= LANES
    tables = call(
        pair_kernel,
        jax.ShapeDtypeStruct((devices, 1, LANES) if direct else (1, experts, experts), f32),
        [VMEM],
        (arrived,),
        scratch=[pltpu.VMEM((experts, entries // devices, LANES), f32)],
    )
    if direct:
        tables = lax.all_to_all(tables, ("grp", "tok"), split_axis=0, concat_axis=0, tiled=True)
    else:
        tables = lax.psum(tables, ("grp", "tok"))
    cka = call(cka_kernel, jax.ShapeDtypeStruct((experts, experts), f32), [VMEM], (tables,))

    blocks = [swapped(b, "tok", m) if m else b for m, b in enumerate(blocks)]
    features = call(
        place_kernel,
        jax.ShapeDtypeStruct((token_part, model), bf16),
        [VMEM] * HOLDERS,
        blocks,
        out_specs=ANY,
        scratch=[pltpu.SemaphoreType.DMA((HOLDERS,))],
    )
    return (features, cka)


def solution(mesh):
    return jax.shard_map(
        shards,
        mesh=mesh,
        in_specs=(
            P("tok", None),
            P(),
            P(("grp", "tok"), None),
            P(("grp", "tok"), None),
            P(("grp", "tok"), None),
            P(("grp", "tok"), None),
        ),
        out_specs=(P(("grp", "tok"), None), P()),
        check_vma=False,
    )
```

```python
import jax
import jax.numpy as jnp
from jax import lax
from jax.experimental import pallas as pl
from jax.experimental.pallas import tpu as pltpu
from jax.sharding import PartitionSpec as P

HOLDERS = 4
ORDER = (0, 2, 1, 3)
LANES = 128
TILE = 16
BIG = 24 * 1024 * 1024
TRANSPOSED = (((1,), (1,)), ((), ()))
VMEM = pl.BlockSpec(memory_space=pltpu.VMEM)
ANY = pl.BlockSpec(memory_space=pl.ANY)
HBM = pl.BlockSpec(memory_space=pltpu.HBM)
bf16 = jnp.bfloat16
f32 = jnp.float32


def swapped(array, axis, mask):
    return lax.ppermute(array, axis, [(i, i ^ mask) for i in range(lax.axis_size(axis))])


def dot_f32(a, b, dims):
    return lax.dot_general(a, b, dims, preferred_element_type=f32)


def call(body, outs, in_specs, operands, out_specs=None, scratch=(), aliases={}):
    return pl.pallas_call(
        body,
        out_shape=outs,
        in_specs=in_specs,
        out_specs=jax.tree.map(lambda _: VMEM, outs) if out_specs is None else out_specs,
        scratch_shapes=list(scratch),
        compiler_params=pltpu.CompilerParams(vmem_limit_bytes=BIG),
        input_output_aliases=aliases,
    )(*operands)


def core():
    return lax.axis_index("grp") & 1


def holder():
    return lax.axis_index("tok") & (HOLDERS - 1)


def columns_of(half, width):
    return pl.ds(pl.multiple_of(half * width, width), width)


def first_kernel(states_hbm, gain_hbm, down_hbm, route_hbm, out_ref, *refs):
    with_z_ref, kept_ref, z_ref, early_ref, late_ref = refs[:5]
    states_ref, gain_ref, route_ref, sems = refs[5:]
    depth, width = down_hbm.shape[0], kept_ref.shape[1]
    rows, count = states_ref.shape[0], depth + TILE
    beside, first_x = with_z_ref.shape[0] - rows, early_ref.shape[0] - count
    left, right = with_z_ref.at[pl.ds(rows, beside), pl.ds(0, width)], with_z_ref.at[
        pl.ds(rows, beside), pl.ds(width, width)
    ]
    blocks = (
        (0, 0, depth, kept_ref.at[pl.ds(0, depth)]),
        (2, 0, beside, left),
        (2, beside, beside, right),
        (2, 2 * beside, depth - 2 * beside, z_ref.at[pl.ds(0, depth - 2 * beside)]),
        (3, 0, depth, early_ref.at[pl.ds(0, depth)]),
        (1, 0, first_x, early_ref.at[pl.ds(count, first_x)]),
        (1, first_x, depth - first_x, late_ref.at[pl.ds(0, depth - first_x)]),
    )
    copies = [
        pltpu.make_async_copy(states_hbm, states_ref, sems.at[0]),
        pltpu.make_async_copy(gain_hbm, gain_ref, sems.at[1]),
        pltpu.make_async_copy(route_hbm, route_ref, sems.at[2]),
    ]
    for at, (m, top, size, block) in enumerate(blocks):
        source = down_hbm.at[pl.ds(top, size), columns_of(holder() ^ m, width)]
        copies.append(pltpu.make_async_copy(source, block, sems.at[3 + at]))
    for copy in copies:
        copy.start()
    for copy in copies[:3]:
        copy.wait()
    states = states_ref[...].astype(f32)
    scale = lax.rsqrt(jnp.mean(states * states, axis=1, keepdims=True) + 1e-06)
    own = columns_of(core(), out_ref.shape[1])
    normed = (states_ref[:, own].astype(f32) * scale * gain_ref[:, own]).astype(bf16)
    out_ref[...] = normed
    with_z_ref[:rows] = normed
    route = route_ref[...]
    high = route.astype(bf16).astype(f32)
    middle = (route - high).astype(bf16).astype(f32)
    low = route - high - middle
    part = route.shape[1]
    row = lax.broadcasted_iota(jnp.int32, (TILE, part), 0)
    terms = jnp.where(row == 0, high, jnp.where(row == 1, middle, jnp.where(row == 2, low, 0.0)))
    terms = jnp.concatenate([terms, jnp.zeros((TILE, width - part), f32)], 1)
    for ref, top in (
        (kept_ref, depth),
        (z_ref, depth - 2 * beside),
        (early_ref, depth),
        (late_ref, depth - first_x),
    ):
        ref[top : top + TILE] = terms.astype(bf16)
    for copy in copies[3:]:
        copy.wait()


def hold_kernel(*refs):
    pass


def held(array, after):
    return call(
        hold_kernel,
        jax.ShapeDtypeStruct(array.shape, array.dtype),
        [ANY] * 2,
        (array, after),
        out_specs=ANY,
        aliases={0: 0},
    )


def join_kernel(after_ref, first_ref, second_ref, out_ref):
    count = first_ref.shape[0]
    out_ref[:count] = first_ref[...]
    out_ref[count:] = second_ref[: out_ref.shape[0] - count]


def stack_kernel(after_ref, *refs):
    rows = refs[-2].shape[0]
    z = lax.axis_index("tok") >> 1
    for m, piece in enumerate(refs[-2::-1]):
        refs[-1][pl.ds(pl.multiple_of((z ^ m) * rows, rows), rows)] = piece[:rows]


def gated(gate, upward):
    return (gate / (1.0 + jnp.exp(-gate)) * upward).astype(bf16)


def near_kernel(near_ref, near2_ref, far_ref, gate_ref, up_ref, out_ref, gate_part_ref, up_part_ref):
    width = near_ref.shape[1]
    own, rest = columns_of(core(), width), columns_of(1 - core(), width)
    near, near2, far = near_ref[...], near2_ref[...], far_ref[...]
    gate, upward = [
        dot_f32(ref[:, own], near, TRANSPOSED) + dot_f32(ref[:, rest], near2, TRANSPOSED)
        for ref in (gate_ref, up_ref)
    ]
    out_ref[...] = gated(gate, upward)
    gate_part_ref[...] = dot_f32(gate_ref[:, own], far, TRANSPOSED)
    up_part_ref[...] = dot_f32(up_ref[:, own], far, TRANSPOSED)


def far_kernel(after_ref, far2_ref, gate_ref, up_ref, near_hidden_ref, gate_part_ref, up_part_ref, out_ref):
    count, width = far2_ref.shape
    rest = columns_of(1 - core(), width)
    far2 = far2_ref[...]
    gate, upward = [
        part_ref[...] + dot_f32(ref[:, rest], far2, TRANSPOSED)
        for ref, part_ref in ((gate_ref, gate_part_ref), (up_ref, up_part_ref))
    ]
    x = lax.axis_index("tok") & 1
    out_ref[:, columns_of(x, count)] = near_hidden_ref[...]
    out_ref[:, columns_of(1 - x, count)] = gated(gate, upward)


def features_kernel(*refs):
    hidden_refs, (kept_ref, with_z_ref, z_ref, early_ref, late_ref) = refs[:HOLDERS], refs[HOLDERS:][:5]
    block_refs, shares_hbm = refs[HOLDERS + 5 : 2 * HOLDERS + 5], refs[2 * HOLDERS + 5]
    route_ref, features_ref, whole_ref, shares_ref, sem = refs[2 * HOLDERS + 6 :]
    depth, tokens = hidden_refs[0].shape
    part, members = tokens // HOLDERS, lax.axis_size("tok")
    rows = tokens // members
    count, width = kept_ref.shape
    beside = (2 * count - z_ref.shape[0]) // 2
    x_block = jnp.concatenate([early_ref[count:], late_ref[...]])
    z_block = jnp.concatenate(
        [with_z_ref[rows:, :width], with_z_ref[rows:, width:], z_ref[: count - 2 * beside]]
    )
    downs = (kept_ref[...], x_block, z_block, z_ref[count - 2 * beside :])

    def place(m, piece):
        z = (holder() ^ m) * (members // HOLDERS // 2) + piece // 2
        return pl.ds(pl.multiple_of(piece % 2 * (tokens // 2) + z * rows, rows), rows)

    eye = lax.broadcasted_iota(jnp.int32, (part, part), 0) == lax.broadcasted_iota(
        jnp.int32, (part, part), 1
    )
    output = None
    for m, hidden_ref in zip(ORDER, hidden_refs):
        down = downs[m]
        product = dot_f32(hidden_ref[...], down[:depth], (((0,), (0,)), ((), ())))
        output = product if output is None else output + product
        terms = down[depth:, :part].astype(f32)
        route = jnp.sum(terms[:HOLDERS], axis=0, keepdims=True)
        column = jnp.sum(jnp.where(eye, route, 0.0), axis=1, keepdims=True)
        column = jnp.broadcast_to(column, (part, LANES))
        for piece in range(part // rows):
            route_ref[place(m, piece)] = column[piece * rows : (piece + 1) * rows]
    features = (output * route_ref[:, :1]).astype(bf16)
    features_ref[...] = features
    wide = features.astype(f32)
    mean = jnp.sum(wide, axis=0, keepdims=True) / tokens
    column = jnp.sum(wide * mean, axis=1, keepdims=True)
    row = jnp.transpose(jnp.broadcast_to(column, (tokens, LANES)))[:1]
    gram = dot_f32(features, features, TRANSPOSED)
    whole_ref[...] = (gram - column - row + jnp.sum(mean * mean)).astype(bf16)
    at = 0
    for i in range(tokens // TILE):
        for j in range(tokens // LANES):
            shares_ref[at * TILE : (at + 1) * TILE] = whole_ref[
                i * TILE : (i + 1) * TILE, j * LANES : (j + 1) * LANES
            ]
            at += 1
    copy = pltpu.make_async_copy(shares_ref, shares_hbm, sem)
    copy.start()
    for m, block_ref in enumerate(block_refs):
        for piece in range(part // rows):
            block_ref[piece * rows : (piece + 1) * rows] = features_ref[place(m, piece)]
    copy.wait()


def place_kernel(*refs):
    blocks, out_ref, sems = refs[:HOLDERS], refs[HOLDERS], refs[HOLDERS + 1]
    width = blocks[0].shape[1]
    copies = []
    for m, block in enumerate(blocks):
        columns = pl.ds(pl.multiple_of((holder() ^ m) * width, width), width)
        copies.append(pltpu.make_async_copy(block, out_ref.at[:, columns], sems.at[m]))
        copies[-1].start()
    for copy in copies:
        copy.wait()


def pair_kernel(parts_ref, out_ref, flat_ref):
    experts = flat_ref.shape[0]
    parts = parts_ref[...].astype(f32)
    total = parts[:, 0]
    for m in range(1, parts.shape[1]):
        total = total + parts[:, m]
    flat_ref[...] = total.astype(bf16).astype(f32)
    in_row = out_ref.shape[1] == 1
    shape = (experts, out_ref.shape[2])
    row = lax.broadcasted_iota(jnp.int32, shape, 0)
    lane = lax.broadcasted_iota(jnp.int32, shape, 1)

    def one(expert, table):
        products = jnp.sum(flat_ref[...] * flat_ref[pl.ds(expert, 1)], axis=1)
        here = lane == expert * experts + row if in_row else lane == expert
        return jnp.where(here, jnp.sum(products, axis=1, keepdims=True), table)

    table = lax.fori_loop(0, experts, one, jnp.zeros(shape, f32), unroll=experts <= 8)
    if in_row:
        table = jnp.sum(table, axis=0, keepdims=True)
    out_ref[...] = jnp.broadcast_to(table[None], out_ref.shape)


def cka_kernel(tables_ref, out_ref):
    totals = jnp.sum(tables_ref[...], axis=0)
    shape = out_ref.shape
    row = lax.broadcasted_iota(jnp.int32, shape, 0)
    lane = lax.broadcasted_iota(jnp.int32, shape, 1)
    if totals.shape != shape:
        experts = shape[0]
        wide = (experts, totals.shape[1])
        spread = jnp.broadcast_to(totals, wide)
        at = lax.broadcasted_iota(jnp.int32, wide, 1) - experts * lax.broadcasted_iota(
            jnp.int32, wide, 0
        )
        totals = jnp.zeros(shape, f32)
        for column in range(experts):
            values = jnp.sum(jnp.where(at == column, spread, 0.0), axis=1, keepdims=True)
            totals = jnp.where(lane == column, values, totals)
    kept = jnp.where(row == lane, totals, 0.0)
    down = jnp.sum(kept, axis=1, keepdims=True)
    across = jnp.sum(kept, axis=0, keepdims=True)
    out_ref[...] = totals / jnp.sqrt(down * across)


def shards(probe_states, norm_gain, gate_weight, up_weight, down_weight, route_weight):
    groups, members = lax.axis_size("grp"), lax.axis_size("tok")
    devices = groups * members
    experts = devices // HOLDERS
    rows, model = probe_states.shape
    tokens = rows * members
    depth = gate_weight.shape[0]
    part, token_part = model // HOLDERS, tokens // HOLDERS

    count = depth + TILE
    beside, first_x = depth // 4 // TILE * TILE, depth // 2 // TILE * TILE
    own, with_z, down_own, down_z, down_early, down_late = call(
        first_kernel,
        [jax.ShapeDtypeStruct((n, model // 2), bf16) for n in (rows, rows + beside)]
        + [
            jax.ShapeDtypeStruct((n, part), bf16)
            for n in (count, count - 2 * beside, count + first_x, count - first_x)
        ],
        [HBM] * 4,
        [
            pltpu.with_memory_space_constraint(a, pltpu.HBM)
            for a in (probe_states, norm_gain[None, :], down_weight, route_weight)
        ],
        scratch=[
            pltpu.VMEM((rows, model), bf16),
            pltpu.VMEM((1, model), f32),
            pltpu.VMEM(route_weight.shape, f32),
            pltpu.SemaphoreType.DMA((10,)),
        ],
    )
    down_early = swapped(down_early, "tok", 1)
    with_z = swapped(with_z, "tok", 2)
    pieces = [swapped(own, "tok", 2 * m) for m in range(members // 2 - 1, 1, -1)] + [with_z, own]
    near = call(
        stack_kernel,
        jax.ShapeDtypeStruct((tokens // 2, model // 2), bf16),
        [ANY] + [VMEM] * len(pieces),
        (down_early, *pieces),
    )
    far = swapped(near, "tok", 1)
    near2 = swapped(near, "grp", 1)
    down_z = call(
        join_kernel,
        jax.ShapeDtypeStruct((2 * (count - beside), part), bf16),
        [ANY, VMEM, VMEM],
        (near, down_z, down_early),
    )
    down_z = swapped(down_z, "tok", 2)
    down_late = swapped(held(down_late, far), "tok", 1)
    half_shape = (depth, tokens // 2)
    near_hidden, gate_part, up_part = call(
        near_kernel,
        [jax.ShapeDtypeStruct(half_shape, dtype) for dtype in (bf16, f32, f32)],
        [VMEM] * 5,
        (near, near2, far, gate_weight, up_weight),
    )
    hidden = call(
        far_kernel,
        jax.ShapeDtypeStruct((depth, tokens), bf16),
        [ANY] + [VMEM] * 6,
        (down_z, swapped(far, "grp", 1), gate_weight, up_weight, near_hidden, gate_part, up_part),
    )
    hiddens = [swapped(hidden, "tok", m) if m else hidden for m in ORDER]
    entries = tokens * tokens // LANES
    *blocks, centered = call(
        features_kernel,
        [jax.ShapeDtypeStruct((token_part, part), bf16)] * HOLDERS
        + [jax.ShapeDtypeStruct((entries, LANES), bf16)],
        [VMEM] * (HOLDERS + 5),
        (*hiddens, down_own, with_z, down_z, down_early, down_late),
        out_specs=[VMEM] * HOLDERS + [HBM],
        scratch=[
            pltpu.VMEM((tokens, LANES), f32),
            pltpu.VMEM((tokens, part), bf16),
            pltpu.VMEM((tokens, tokens), bf16),
            pltpu.VMEM((entries, LANES), bf16),
            pltpu.SemaphoreType.DMA,
        ],
    )
    arrived = lax.all_to_all(centered, ("grp", "tok"), split_axis=0, concat_axis=0, tiled=True)
    arrived = arrived.reshape(experts, HOLDERS, entries // devices, LANES)
    direct = experts * experts <= LANES
    tables = call(
        pair_kernel,
        jax.ShapeDtypeStruct((devices, 1, LANES) if direct else (1, experts, experts), f32),
        [VMEM],
        (arrived,),
        scratch=[pltpu.VMEM((experts, entries // devices, LANES), f32)],
    )
    if direct:
        tables = lax.all_to_all(tables, ("grp", "tok"), split_axis=0, concat_axis=0, tiled=True)
    else:
        tables = lax.psum(tables, ("grp", "tok"))
    cka = call(cka_kernel, jax.ShapeDtypeStruct((experts, experts), f32), [VMEM], (tables,))

    blocks = [swapped(b, "tok", m) if m else b for m, b in enumerate(blocks)]
    features = call(
        place_kernel,
        jax.ShapeDtypeStruct((token_part, model), bf16),
        [VMEM] * HOLDERS,
        blocks,
        out_specs=ANY,
        scratch=[pltpu.SemaphoreType.DMA((HOLDERS,))],
    )
    return (features, cka)


def solution(mesh):
    return jax.shard_map(
        shards,
        mesh=mesh,
        in_specs=(
            P("tok", None),
            P(),
            P(("grp", "tok"), None),
            P(("grp", "tok"), None),
            P(("grp", "tok"), None),
            P(("grp", "tok"), None),
        ),
        out_specs=(P(("grp", "tok"), None), P()),
        check_vma=False,
    )
```

```python
import jax
import jax.numpy as jnp
from jax import lax
from jax.experimental import pallas as pl
from jax.experimental.pallas import tpu as pltpu
from jax.sharding import PartitionSpec as P

HOLDERS = 4
LANES = 128
TILE = 16
BIG = 24 * 1024 * 1024
TRANSPOSED = (((1,), (1,)), ((), ()))
VMEM = pl.BlockSpec(memory_space=pltpu.VMEM)
ANY = pl.BlockSpec(memory_space=pl.ANY)
HBM = pl.BlockSpec(memory_space=pltpu.HBM)
bf16 = jnp.bfloat16
f32 = jnp.float32


def swapped(array, axis, mask):
    return lax.ppermute(array, axis, [(i, i ^ mask) for i in range(lax.axis_size(axis))])


def dot_f32(a, b, dims):
    return lax.dot_general(a, b, dims, preferred_element_type=f32)


def call(body, outs, in_specs, operands, out_specs=None, scratch=(), aliases={}):
    return pl.pallas_call(
        body,
        out_shape=outs,
        in_specs=in_specs,
        out_specs=jax.tree.map(lambda _: VMEM, outs) if out_specs is None else out_specs,
        scratch_shapes=list(scratch),
        compiler_params=pltpu.CompilerParams(vmem_limit_bytes=BIG),
        input_output_aliases=aliases,
    )(*operands)


def core():
    return lax.axis_index("grp") & 1


def holder():
    return lax.axis_index("tok") & (HOLDERS - 1)


def columns_of(half, width):
    return pl.ds(pl.multiple_of(half * width, width), width)


def first_kernel(states_hbm, gain_hbm, down_hbm, route_hbm, out_ref, *refs):
    with_z_ref, z_ref, early_ref, late_ref = refs[:4]
    states_ref, gain_ref, route_ref, sems = refs[4:]
    depth, width = down_hbm.shape[0], early_ref.shape[1]
    rows, count = states_ref.shape[0], depth + TILE
    beside, first_x = with_z_ref.shape[0] - rows, early_ref.shape[0] - count
    left, right = with_z_ref.at[pl.ds(rows, beside), pl.ds(0, width)], with_z_ref.at[
        pl.ds(rows, beside), pl.ds(width, width)
    ]
    blocks = (
        (2, 0, beside, left),
        (2, beside, beside, right),
        (2, 2 * beside, depth - 2 * beside, z_ref.at[pl.ds(0, depth - 2 * beside)]),
        (3, 0, depth, early_ref.at[pl.ds(0, depth)]),
        (1, 0, first_x, early_ref.at[pl.ds(count, first_x)]),
        (1, first_x, depth - first_x, late_ref.at[pl.ds(0, depth - first_x)]),
    )
    copies = [
        pltpu.make_async_copy(states_hbm, states_ref, sems.at[0]),
        pltpu.make_async_copy(gain_hbm, gain_ref, sems.at[1]),
        pltpu.make_async_copy(route_hbm, route_ref, sems.at[2]),
    ]
    for at, (m, top, size, block) in enumerate(blocks):
        source = down_hbm.at[pl.ds(top, size), columns_of(holder() ^ m, width)]
        copies.append(pltpu.make_async_copy(source, block, sems.at[3 + at]))
    for copy in copies:
        copy.start()
    for copy in copies[:3]:
        copy.wait()
    states = states_ref[...].astype(f32)
    scale = lax.rsqrt(jnp.mean(states * states, axis=1, keepdims=True) + 1e-06)
    own = columns_of(core(), out_ref.shape[1])
    normed = (states_ref[:, own].astype(f32) * scale * gain_ref[:, own]).astype(bf16)
    out_ref[...] = normed
    with_z_ref[:rows] = normed
    route = route_ref[...]
    high = route.astype(bf16).astype(f32)
    middle = (route - high).astype(bf16).astype(f32)
    low = route - high - middle
    part = route.shape[1]
    row = lax.broadcasted_iota(jnp.int32, (TILE, part), 0)
    terms = jnp.where(row == 0, high, jnp.where(row == 1, middle, jnp.where(row == 2, low, 0.0)))
    terms = jnp.concatenate([terms, jnp.zeros((TILE, width - part), f32)], 1)
    for ref, top in (
        (z_ref, depth - 2 * beside),
        (early_ref, depth),
        (late_ref, depth - first_x),
    ):
        ref[top : top + TILE] = terms.astype(bf16)
    for copy in copies[3:]:
        copy.wait()


def hold_kernel(*refs):
    pass


def held(array, after):
    return call(
        hold_kernel,
        jax.ShapeDtypeStruct(array.shape, array.dtype),
        [ANY] * 2,
        (array, after),
        out_specs=ANY,
        aliases={0: 0},
    )


def join_kernel(after_ref, first_ref, second_ref, out_ref):
    count = first_ref.shape[0]
    out_ref[:count] = first_ref[...]
    out_ref[count:] = second_ref[: out_ref.shape[0] - count]


def stack_kernel(after_ref, *refs):
    rows = refs[-2].shape[0]
    z = lax.axis_index("tok") >> 1
    for m, piece in enumerate(refs[-2::-1]):
        refs[-1][pl.ds(pl.multiple_of((z ^ m) * rows, rows), rows)] = piece[:rows]


def gated(gate, upward):
    return (gate / (1.0 + jnp.exp(-gate)) * upward).astype(bf16)


def near_kernel(near_ref, near2_ref, far_ref, gate_ref, up_ref, out_ref, gate_part_ref, up_part_ref):
    width = near_ref.shape[1]
    own, rest = columns_of(core(), width), columns_of(1 - core(), width)
    near, near2, far = near_ref[...], near2_ref[...], far_ref[...]
    gate, upward = [
        dot_f32(ref[:, own], near, TRANSPOSED) + dot_f32(ref[:, rest], near2, TRANSPOSED)
        for ref in (gate_ref, up_ref)
    ]
    out_ref[...] = gated(gate, upward)
    gate_part_ref[...] = dot_f32(gate_ref[:, own], far, TRANSPOSED)
    up_part_ref[...] = dot_f32(up_ref[:, own], far, TRANSPOSED)


def far_kernel(after_ref, far2_ref, gate_ref, up_ref, near_hidden_ref, gate_part_ref, up_part_ref, out_ref):
    count, width = far2_ref.shape
    rest = columns_of(1 - core(), width)
    far2 = far2_ref[...]
    gate, upward = [
        part_ref[...] + dot_f32(ref[:, rest], far2, TRANSPOSED)
        for ref, part_ref in ((gate_ref, gate_part_ref), (up_ref, up_part_ref))
    ]
    x = lax.axis_index("tok") & 1
    out_ref[:, columns_of(x, count)] = near_hidden_ref[...]
    out_ref[:, columns_of(1 - x, count)] = gated(gate, upward)


def features_kernel(*refs):
    hidden_refs = refs[:HOLDERS]
    down_ref, own_route_ref, with_z_ref, z_ref, early_ref, late_ref = refs[HOLDERS:][:6]
    block_refs, shares_hbm = refs[HOLDERS + 6 : 2 * HOLDERS + 6], refs[2 * HOLDERS + 6]
    route_ref, features_ref, whole_ref, shares_ref, sems = refs[2 * HOLDERS + 7 :]
    depth, tokens = hidden_refs[0].shape
    part, members = tokens // HOLDERS, lax.axis_size("tok")
    rows = tokens // members
    count, width = depth + TILE, early_ref.shape[1]
    beside = (2 * count - z_ref.shape[0]) // 2
    x_block = jnp.concatenate([early_ref[count:], late_ref[...]])
    z_block = jnp.concatenate(
        [with_z_ref[rows:, :width], with_z_ref[rows:, width:], z_ref[: count - 2 * beside]]
    )
    own_block = down_ref[:, columns_of(holder(), width)]
    downs = (own_block, x_block, z_block, z_ref[count - 2 * beside :])

    def place(m, piece):
        z = (holder() ^ m) * (members // HOLDERS // 2) + piece // 2
        return pl.ds(pl.multiple_of(piece % 2 * (tokens // 2) + z * rows, rows), rows)

    eye = lax.broadcasted_iota(jnp.int32, (part, part), 0) == lax.broadcasted_iota(
        jnp.int32, (part, part), 1
    )
    output = None
    for m, (hidden_ref, down) in enumerate(zip(hidden_refs, downs)):
        product = dot_f32(hidden_ref[...], down[:depth], (((0,), (0,)), ((), ())))
        output = product if output is None else output + product
        if m:
            terms = down[depth:, :part].astype(f32)
            route = jnp.sum(terms[:HOLDERS], axis=0, keepdims=True)
        else:
            route = own_route_ref[...]
        column = jnp.sum(jnp.where(eye, route, 0.0), axis=1, keepdims=True)
        column = jnp.broadcast_to(column, (part, LANES))
        for piece in range(part // rows):
            route_ref[place(m, piece)] = column[piece * rows : (piece + 1) * rows]
    features = (output * route_ref[:, :1]).astype(bf16)
    features_ref[...] = features
    wide = features.astype(f32)
    mean = jnp.sum(wide, axis=0, keepdims=True) / tokens
    column = jnp.sum(wide * mean, axis=1, keepdims=True)
    row = jnp.transpose(jnp.broadcast_to(column, (tokens, LANES)))[:1]
    square = jnp.sum(mean * mean)
    copies = []
    half, size = tokens // 2, shares_ref.shape[0] // 2
    for side in range(2):
        top = side * half
        gram = dot_f32(features[top : top + half], features, TRANSPOSED)
        whole_ref[...] = (gram - column[top : top + half] - row + square).astype(bf16)
        at = side * size
        for i in range(half // TILE):
            for j in range(tokens // LANES):
                shares_ref[at : at + TILE] = whole_ref[
                    i * TILE : (i + 1) * TILE, j * LANES : (j + 1) * LANES
                ]
                at += TILE
        there = pl.ds(side * size, size)
        copies.append(pltpu.make_async_copy(shares_ref.at[there], shares_hbm.at[there], sems.at[side]))
        copies[-1].start()
    for m, block_ref in enumerate(block_refs):
        for piece in range(part // rows):
            block_ref[piece * rows : (piece + 1) * rows] = features_ref[place(m, piece)]
    for copy in copies:
        copy.wait()


def place_kernel(*refs):
    blocks, out_ref, sems = refs[:HOLDERS], refs[HOLDERS], refs[HOLDERS + 1]
    width = blocks[0].shape[1]
    copies = []
    for m, block in enumerate(blocks):
        columns = pl.ds(pl.multiple_of((holder() ^ m) * width, width), width)
        copies.append(pltpu.make_async_copy(block, out_ref.at[:, columns], sems.at[m]))
        copies[-1].start()
    for copy in copies:
        copy.wait()


def pair_kernel(parts_ref, out_ref, flat_ref):
    experts = flat_ref.shape[0]
    parts = parts_ref[...].astype(f32)
    total = parts[:, 0]
    for m in range(1, parts.shape[1]):
        total = total + parts[:, m]
    flat_ref[...] = total.astype(bf16).astype(f32)
    in_row = out_ref.shape[1] == 1
    shape = (experts, out_ref.shape[2])
    row = lax.broadcasted_iota(jnp.int32, shape, 0)
    lane = lax.broadcasted_iota(jnp.int32, shape, 1)

    def one(expert, table):
        products = jnp.sum(flat_ref[...] * flat_ref[pl.ds(expert, 1)], axis=1)
        here = lane == expert * experts + row if in_row else lane == expert
        return jnp.where(here, jnp.sum(products, axis=1, keepdims=True), table)

    table = lax.fori_loop(0, experts, one, jnp.zeros(shape, f32), unroll=experts <= 8)
    if in_row:
        table = jnp.sum(table, axis=0, keepdims=True)
    out_ref[...] = jnp.broadcast_to(table[None], out_ref.shape)


def cka_kernel(tables_ref, out_ref):
    totals = jnp.sum(tables_ref[...], axis=0)
    shape = out_ref.shape
    row = lax.broadcasted_iota(jnp.int32, shape, 0)
    lane = lax.broadcasted_iota(jnp.int32, shape, 1)
    if totals.shape != shape:
        experts = shape[0]
        wide = (experts, totals.shape[1])
        spread = jnp.broadcast_to(totals, wide)
        at = lax.broadcasted_iota(jnp.int32, wide, 1) - experts * lax.broadcasted_iota(
            jnp.int32, wide, 0
        )
        totals = jnp.zeros(shape, f32)
        for column in range(experts):
            values = jnp.sum(jnp.where(at == column, spread, 0.0), axis=1, keepdims=True)
            totals = jnp.where(lane == column, values, totals)
    kept = jnp.where(row == lane, totals, 0.0)
    down = jnp.sum(kept, axis=1, keepdims=True)
    across = jnp.sum(kept, axis=0, keepdims=True)
    out_ref[...] = totals / jnp.sqrt(down * across)


def shards(probe_states, norm_gain, gate_weight, up_weight, down_weight, route_weight):
    groups, members = lax.axis_size("grp"), lax.axis_size("tok")
    devices = groups * members
    experts = devices // HOLDERS
    rows, model = probe_states.shape
    tokens = rows * members
    depth = gate_weight.shape[0]
    part, token_part = model // HOLDERS, tokens // HOLDERS

    count = depth + TILE
    beside, first_x = depth // 4 // TILE * TILE, depth // 2 // TILE * TILE
    own, with_z, down_z, down_early, down_late = call(
        first_kernel,
        [jax.ShapeDtypeStruct((n, model // 2), bf16) for n in (rows, rows + beside)]
        + [
            jax.ShapeDtypeStruct((n, part), bf16)
            for n in (count - 2 * beside, count + first_x, count - first_x)
        ],
        [HBM] * 4,
        [
            pltpu.with_memory_space_constraint(a, pltpu.HBM)
            for a in (probe_states, norm_gain[None, :], down_weight, route_weight)
        ],
        scratch=[
            pltpu.VMEM((rows, model), bf16),
            pltpu.VMEM((1, model), f32),
            pltpu.VMEM(route_weight.shape, f32),
            pltpu.SemaphoreType.DMA((10,)),
        ],
    )
    down_early = swapped(down_early, "tok", 1)
    with_z = swapped(with_z, "tok", 2)
    pieces = [swapped(own, "tok", 2 * m) for m in range(members // 2 - 1, 1, -1)] + [with_z, own]
    near = call(
        stack_kernel,
        jax.ShapeDtypeStruct((tokens // 2, model // 2), bf16),
        [ANY] + [VMEM] * len(pieces),
        (down_early, *pieces),
    )
    far = swapped(near, "tok", 1)
    near2 = swapped(near, "grp", 1)
    down_z = call(
        join_kernel,
        jax.ShapeDtypeStruct((2 * (count - beside), part), bf16),
        [ANY, VMEM, VMEM],
        (near, down_z, down_early),
    )
    down_z = swapped(down_z, "tok", 2)
    down_late = swapped(held(down_late, far), "tok", 1)
    half_shape = (depth, tokens // 2)
    near_hidden, gate_part, up_part = call(
        near_kernel,
        [jax.ShapeDtypeStruct(half_shape, dtype) for dtype in (bf16, f32, f32)],
        [VMEM] * 5,
        (near, near2, far, gate_weight, up_weight),
    )
    hidden = call(
        far_kernel,
        jax.ShapeDtypeStruct((depth, tokens), bf16),
        [ANY] + [VMEM] * 6,
        (down_z, swapped(far, "grp", 1), gate_weight, up_weight, near_hidden, gate_part, up_part),
    )
    hiddens = [swapped(hidden, "tok", m) if m else hidden for m in range(HOLDERS)]
    entries = tokens * tokens // LANES
    *blocks, centered = call(
        features_kernel,
        [jax.ShapeDtypeStruct((token_part, part), bf16)] * HOLDERS
        + [jax.ShapeDtypeStruct((entries, LANES), bf16)],
        [VMEM] * (HOLDERS + 6),
        (*hiddens, down_weight, route_weight, with_z, down_z, down_early, down_late),
        out_specs=[VMEM] * HOLDERS + [HBM],
        scratch=[
            pltpu.VMEM((tokens, LANES), f32),
            pltpu.VMEM((tokens, part), bf16),
            pltpu.VMEM((tokens // 2, tokens), bf16),
            pltpu.VMEM((entries, LANES), bf16),
            pltpu.SemaphoreType.DMA((2,)),
        ],
    )
    arrived = lax.all_to_all(centered, ("grp", "tok"), split_axis=0, concat_axis=0, tiled=True)
    arrived = arrived.reshape(experts, HOLDERS, entries // devices, LANES)
    direct = experts * experts <= LANES
    tables = call(
        pair_kernel,
        jax.ShapeDtypeStruct((devices, 1, LANES) if direct else (1, experts, experts), f32),
        [VMEM],
        (arrived,),
        scratch=[pltpu.VMEM((experts, entries // devices, LANES), f32)],
    )
    if direct:
        tables = lax.all_to_all(tables, ("grp", "tok"), split_axis=0, concat_axis=0, tiled=True)
    else:
        tables = lax.psum(tables, ("grp", "tok"))
    cka = call(cka_kernel, jax.ShapeDtypeStruct((experts, experts), f32), [VMEM], (tables,))

    blocks = [swapped(b, "tok", m) if m else b for m, b in enumerate(blocks)]
    features = call(
        place_kernel,
        jax.ShapeDtypeStruct((token_part, model), bf16),
        [VMEM] * HOLDERS,
        blocks,
        out_specs=ANY,
        scratch=[pltpu.SemaphoreType.DMA((HOLDERS,))],
    )
    return (features, cka)


def solution(mesh):
    return jax.shard_map(
        shards,
        mesh=mesh,
        in_specs=(
            P("tok", None),
            P(),
            P(("grp", "tok"), None),
            P(("grp", "tok"), None),
            P(("grp", "tok"), None),
            P(("grp", "tok"), None),
        ),
        out_specs=(P(("grp", "tok"), None), P()),
        check_vma=False,
    )
```

```python
import jax
import jax.numpy as jnp
from jax import lax
from jax.experimental import pallas as pl
from jax.experimental.pallas import tpu as pltpu
from jax.sharding import PartitionSpec as P

HOLDERS = 4
LANES = 128
TILE = 16
BIG = 24 * 1024 * 1024
TRANSPOSED = (((1,), (1,)), ((), ()))
VMEM = pl.BlockSpec(memory_space=pltpu.VMEM)
ANY = pl.BlockSpec(memory_space=pl.ANY)
HBM = pl.BlockSpec(memory_space=pltpu.HBM)
bf16 = jnp.bfloat16
f32 = jnp.float32


def swapped(array, axis, mask):
    return lax.ppermute(array, axis, [(i, i ^ mask) for i in range(lax.axis_size(axis))])


def dot_f32(a, b, dims):
    return lax.dot_general(a, b, dims, preferred_element_type=f32)


def call(body, outs, in_specs, operands, out_specs=None, scratch=(), aliases={}):
    return pl.pallas_call(
        body,
        out_shape=outs,
        in_specs=in_specs,
        out_specs=jax.tree.map(lambda _: VMEM, outs) if out_specs is None else out_specs,
        scratch_shapes=list(scratch),
        compiler_params=pltpu.CompilerParams(vmem_limit_bytes=BIG),
        input_output_aliases=aliases,
    )(*operands)


def core():
    return lax.axis_index("grp") & 1


def holder():
    return lax.axis_index("tok") & (HOLDERS - 1)


def columns_of(half, width):
    return pl.ds(pl.multiple_of(half * width, width), width)


def first_kernel(states_hbm, gain_hbm, down_hbm, route_hbm, out_ref, *refs):
    with_z_ref, kept_ref, z_ref, early_ref, late_ref = refs[:5]
    states_ref, gain_ref, route_ref, sems = refs[5:]
    depth, width = down_hbm.shape[0], kept_ref.shape[1]
    rows, count = states_ref.shape[0], depth + TILE
    beside, first_x = with_z_ref.shape[0] - rows, early_ref.shape[0] - count
    left, right = with_z_ref.at[pl.ds(rows, beside), pl.ds(0, width)], with_z_ref.at[
        pl.ds(rows, beside), pl.ds(width, width)
    ]
    blocks = (
        (0, 0, depth, kept_ref.at[pl.ds(0, depth)]),
        (2, 0, beside, left),
        (2, beside, beside, right),
        (2, 2 * beside, depth - 2 * beside, z_ref.at[pl.ds(0, depth - 2 * beside)]),
        (3, 0, depth, early_ref.at[pl.ds(0, depth)]),
        (1, 0, first_x, early_ref.at[pl.ds(count, first_x)]),
        (1, first_x, depth - first_x, late_ref.at[pl.ds(0, depth - first_x)]),
    )
    copies = [
        pltpu.make_async_copy(states_hbm, states_ref, sems.at[0]),
        pltpu.make_async_copy(gain_hbm, gain_ref, sems.at[1]),
        pltpu.make_async_copy(route_hbm, route_ref, sems.at[2]),
    ]
    for at, (m, top, size, block) in enumerate(blocks):
        source = down_hbm.at[pl.ds(top, size), columns_of(holder() ^ m, width)]
        copies.append(pltpu.make_async_copy(source, block, sems.at[3 + at]))
    for copy in copies:
        copy.start()
    for copy in copies[:3]:
        copy.wait()
    states = states_ref[...].astype(f32)
    scale = lax.rsqrt(jnp.mean(states * states, axis=1, keepdims=True) + 1e-06)
    own = columns_of(core(), out_ref.shape[1])
    normed = (states_ref[:, own].astype(f32) * scale * gain_ref[:, own]).astype(bf16)
    out_ref[...] = normed
    with_z_ref[:rows] = normed
    route = route_ref[...]
    high = route.astype(bf16).astype(f32)
    middle = (route - high).astype(bf16).astype(f32)
    low = route - high - middle
    part = route.shape[1]
    row = lax.broadcasted_iota(jnp.int32, (TILE, part), 0)
    terms = jnp.where(row == 0, high, jnp.where(row == 1, middle, jnp.where(row == 2, low, 0.0)))
    terms = jnp.concatenate([terms, jnp.zeros((TILE, width - part), f32)], 1)
    for ref, top in (
        (kept_ref, depth),
        (z_ref, depth - 2 * beside),
        (early_ref, depth),
        (late_ref, depth - first_x),
    ):
        ref[top : top + TILE] = terms.astype(bf16)
    for copy in copies[3:]:
        copy.wait()


def hold_kernel(*refs):
    pass


def held(array, after):
    return call(
        hold_kernel,
        jax.ShapeDtypeStruct(array.shape, array.dtype),
        [ANY] * 2,
        (array, after),
        out_specs=ANY,
        aliases={0: 0},
    )


def join_kernel(after_ref, first_ref, second_ref, out_ref):
    count = first_ref.shape[0]
    out_ref[:count] = first_ref[...]
    out_ref[count:] = second_ref[: out_ref.shape[0] - count]


def stack_kernel(after_ref, *refs):
    rows = refs[-2].shape[0]
    z = lax.axis_index("tok") >> 1
    for m, piece in enumerate(refs[-2::-1]):
        refs[-1][pl.ds(pl.multiple_of((z ^ m) * rows, rows), rows)] = piece[:rows]


def gated(gate, upward):
    return (gate / (1.0 + jnp.exp(-gate)) * upward).astype(bf16)


def near_kernel(near_ref, near2_ref, far_ref, gate_ref, up_ref, out_ref, gate_part_ref, up_part_ref):
    width = near_ref.shape[1]
    own, rest = columns_of(core(), width), columns_of(1 - core(), width)
    near, near2, far = near_ref[...], near2_ref[...], far_ref[...]
    gate, upward = [
        dot_f32(ref[:, own], near, TRANSPOSED) + dot_f32(ref[:, rest], near2, TRANSPOSED)
        for ref in (gate_ref, up_ref)
    ]
    out_ref[...] = gated(gate, upward)
    gate_part_ref[...] = dot_f32(gate_ref[:, own], far, TRANSPOSED)
    up_part_ref[...] = dot_f32(up_ref[:, own], far, TRANSPOSED)


def far_kernel(after_ref, far2_ref, gate_ref, up_ref, near_hidden_ref, gate_part_ref, up_part_ref, out_ref):
    count, width = far2_ref.shape
    rest = columns_of(1 - core(), width)
    far2 = far2_ref[...]
    gate, upward = [
        part_ref[...] + dot_f32(ref[:, rest], far2, TRANSPOSED)
        for ref, part_ref in ((gate_ref, gate_part_ref), (up_ref, up_part_ref))
    ]
    x = lax.axis_index("tok") & 1
    out_ref[:, columns_of(x, count)] = near_hidden_ref[...]
    out_ref[:, columns_of(1 - x, count)] = gated(gate, upward)


def features_kernel(*refs):
    hidden_refs, (kept_ref, with_z_ref, z_ref, early_ref, late_ref) = refs[:HOLDERS], refs[HOLDERS:][:5]
    block_refs, shares_hbm = refs[HOLDERS + 5 : 2 * HOLDERS + 5], refs[2 * HOLDERS + 5]
    route_ref, features_ref, whole_ref, shares_ref, sem = refs[2 * HOLDERS + 6 :]
    depth, tokens = hidden_refs[0].shape
    part, members = tokens // HOLDERS, lax.axis_size("tok")
    rows = tokens // members
    count, width = kept_ref.shape
    beside = (2 * count - z_ref.shape[0]) // 2
    x_block = jnp.concatenate([early_ref[count:], late_ref[...]])
    z_block = jnp.concatenate(
        [with_z_ref[rows:, :width], with_z_ref[rows:, width:], z_ref[: count - 2 * beside]]
    )
    downs = (kept_ref[...], x_block, z_block, z_ref[count - 2 * beside :])

    def place(m, piece):
        z = (holder() ^ m) * (members // HOLDERS // 2) + piece // 2
        return pl.ds(pl.multiple_of(piece % 2 * (tokens // 2) + z * rows, rows), rows)

    eye = lax.broadcasted_iota(jnp.int32, (part, part), 0) == lax.broadcasted_iota(
        jnp.int32, (part, part), 1
    )
    output = None
    for m, (hidden_ref, down) in enumerate(zip(hidden_refs, downs)):
        product = dot_f32(hidden_ref[...], down[:depth], (((0,), (0,)), ((), ())))
        output = product if output is None else output + product
        terms = down[depth:, :part].astype(f32)
        route = jnp.sum(terms[:HOLDERS], axis=0, keepdims=True)
        column = jnp.sum(jnp.where(eye, route, 0.0), axis=1, keepdims=True)
        column = jnp.broadcast_to(column, (part, LANES))
        for piece in range(part // rows):
            route_ref[place(m, piece)] = column[piece * rows : (piece + 1) * rows]
    features = (output * route_ref[:, :1]).astype(bf16)
    features_ref[...] = features
    wide = features.astype(f32)
    mean = jnp.sum(wide, axis=0, keepdims=True) / tokens
    column = jnp.sum(wide * mean, axis=1, keepdims=True)
    row = jnp.transpose(jnp.broadcast_to(column, (tokens, LANES)))[:1]
    gram = dot_f32(features, features, TRANSPOSED)
    whole_ref[...] = (gram - column - row + jnp.sum(mean * mean)).astype(bf16)
    at = 0
    for i in range(tokens // TILE):
        for j in range(tokens // LANES):
            shares_ref[at * TILE : (at + 1) * TILE] = whole_ref[
                i * TILE : (i + 1) * TILE, j * LANES : (j + 1) * LANES
            ]
            at += 1
    copy = pltpu.make_async_copy(shares_ref, shares_hbm, sem)
    copy.start()
    for m, block_ref in enumerate(block_refs):
        for piece in range(part // rows):
            block_ref[piece * rows : (piece + 1) * rows] = features_ref[place(m, piece)]
    copy.wait()


def place_kernel(*refs):
    blocks, out_ref, sems = refs[:HOLDERS], refs[HOLDERS], refs[HOLDERS + 1]
    width = blocks[0].shape[1]
    copies = []
    for m, block in enumerate(blocks):
        columns = pl.ds(pl.multiple_of((holder() ^ m) * width, width), width)
        copies.append(pltpu.make_async_copy(block, out_ref.at[:, columns], sems.at[m]))
        copies[-1].start()
    for copy in copies:
        copy.wait()


def pair_kernel(parts_ref, out_ref, flat_ref):
    experts = flat_ref.shape[0]
    parts = parts_ref[...].astype(f32)
    total = parts[:, 0]
    for m in range(1, parts.shape[1]):
        total = total + parts[:, m]
    flat_ref[...] = total.astype(bf16).astype(f32)
    in_row = out_ref.shape[1] == 1
    shape = (experts, out_ref.shape[2])
    row = lax.broadcasted_iota(jnp.int32, shape, 0)
    lane = lax.broadcasted_iota(jnp.int32, shape, 1)

    def one(expert, table):
        products = jnp.sum(flat_ref[...] * flat_ref[pl.ds(expert, 1)], axis=1)
        here = lane == expert * experts + row if in_row else lane == expert
        return jnp.where(here, jnp.sum(products, axis=1, keepdims=True), table)

    table = lax.fori_loop(0, experts, one, jnp.zeros(shape, f32), unroll=experts <= 8)
    if in_row:
        table = jnp.sum(table, axis=0, keepdims=True)
    out_ref[...] = jnp.broadcast_to(table[None], out_ref.shape)


def cka_kernel(tables_ref, out_ref):
    totals = jnp.sum(tables_ref[...], axis=0)
    shape = out_ref.shape
    row = lax.broadcasted_iota(jnp.int32, shape, 0)
    lane = lax.broadcasted_iota(jnp.int32, shape, 1)
    if totals.shape != shape:
        experts = shape[0]
        wide = (experts, totals.shape[1])
        spread = jnp.broadcast_to(totals, wide)
        at = lax.broadcasted_iota(jnp.int32, wide, 1) - experts * lax.broadcasted_iota(
            jnp.int32, wide, 0
        )
        totals = jnp.zeros(shape, f32)
        for column in range(experts):
            values = jnp.sum(jnp.where(at == column, spread, 0.0), axis=1, keepdims=True)
            totals = jnp.where(lane == column, values, totals)
    kept = jnp.where(row == lane, totals, 0.0)
    down = jnp.sum(kept, axis=1, keepdims=True)
    across = jnp.sum(kept, axis=0, keepdims=True)
    out_ref[...] = totals / jnp.sqrt(down * across)


def shards(probe_states, norm_gain, gate_weight, up_weight, down_weight, route_weight):
    groups, members = lax.axis_size("grp"), lax.axis_size("tok")
    devices = groups * members
    experts = devices // HOLDERS
    rows, model = probe_states.shape
    tokens = rows * members
    depth = gate_weight.shape[0]
    part, token_part = model // HOLDERS, tokens // HOLDERS

    count = depth + TILE
    beside, first_x = depth // 4 // TILE * TILE, depth // 3 // TILE * TILE
    own, with_z, down_own, down_z, down_early, down_late = call(
        first_kernel,
        [jax.ShapeDtypeStruct((n, model // 2), bf16) for n in (rows, rows + beside)]
        + [
            jax.ShapeDtypeStruct((n, part), bf16)
            for n in (count, count - 2 * beside, count + first_x, count - first_x)
        ],
        [HBM] * 4,
        [
            pltpu.with_memory_space_constraint(a, pltpu.HBM)
            for a in (probe_states, norm_gain[None, :], down_weight, route_weight)
        ],
        scratch=[
            pltpu.VMEM((rows, model), bf16),
            pltpu.VMEM((1, model), f32),
            pltpu.VMEM(route_weight.shape, f32),
            pltpu.SemaphoreType.DMA((10,)),
        ],
    )
    down_early = swapped(down_early, "tok", 1)
    with_z = swapped(with_z, "tok", 2)
    pieces = [swapped(own, "tok", 2 * m) for m in range(members // 2 - 1, 1, -1)] + [with_z, own]
    near = call(
        stack_kernel,
        jax.ShapeDtypeStruct((tokens // 2, model // 2), bf16),
        [ANY] + [VMEM] * len(pieces),
        (down_early, *pieces),
    )
    far = swapped(near, "tok", 1)
    near2 = swapped(near, "grp", 1)
    down_z = call(
        join_kernel,
        jax.ShapeDtypeStruct((2 * (count - beside), part), bf16),
        [ANY, VMEM, VMEM],
        (near, down_z, down_early),
    )
    down_z = swapped(down_z, "tok", 2)
    down_late = swapped(held(down_late, far), "tok", 1)
    half_shape = (depth, tokens // 2)
    near_hidden, gate_part, up_part = call(
        near_kernel,
        [jax.ShapeDtypeStruct(half_shape, dtype) for dtype in (bf16, f32, f32)],
        [VMEM] * 5,
        (near, near2, far, gate_weight, up_weight),
    )
    hidden = call(
        far_kernel,
        jax.ShapeDtypeStruct((depth, tokens), bf16),
        [ANY] + [VMEM] * 6,
        (down_z, swapped(far, "grp", 1), gate_weight, up_weight, near_hidden, gate_part, up_part),
    )
    hiddens = [swapped(hidden, "tok", m) if m else hidden for m in range(HOLDERS)]
    entries = tokens * tokens // LANES
    *blocks, centered = call(
        features_kernel,
        [jax.ShapeDtypeStruct((token_part, part), bf16)] * HOLDERS
        + [jax.ShapeDtypeStruct((entries, LANES), bf16)],
        [VMEM] * (HOLDERS + 5),
        (*hiddens, down_own, with_z, down_z, down_early, down_late),
        out_specs=[VMEM] * HOLDERS + [HBM],
        scratch=[
            pltpu.VMEM((tokens, LANES), f32),
            pltpu.VMEM((tokens, part), bf16),
            pltpu.VMEM((tokens, tokens), bf16),
            pltpu.VMEM((entries, LANES), bf16),
            pltpu.SemaphoreType.DMA,
        ],
    )
    arrived = lax.all_to_all(centered, ("grp", "tok"), split_axis=0, concat_axis=0, tiled=True)
    arrived = arrived.reshape(experts, HOLDERS, entries // devices, LANES)
    direct = experts * experts <= LANES
    tables = call(
        pair_kernel,
        jax.ShapeDtypeStruct((devices, 1, LANES) if direct else (1, experts, experts), f32),
        [VMEM],
        (arrived,),
        scratch=[pltpu.VMEM((experts, entries // devices, LANES), f32)],
    )
    if direct:
        tables = lax.all_to_all(tables, ("grp", "tok"), split_axis=0, concat_axis=0, tiled=True)
    else:
        tables = lax.psum(tables, ("grp", "tok"))
    cka = call(cka_kernel, jax.ShapeDtypeStruct((experts, experts), f32), [VMEM], (tables,))

    blocks = [swapped(b, "tok", m) if m else b for m, b in enumerate(blocks)]
    features = call(
        place_kernel,
        jax.ShapeDtypeStruct((token_part, model), bf16),
        [VMEM] * HOLDERS,
        blocks,
        out_specs=ANY,
        scratch=[pltpu.SemaphoreType.DMA((HOLDERS,))],
    )
    return (features, cka)


def solution(mesh):
    return jax.shard_map(
        shards,
        mesh=mesh,
        in_specs=(
            P("tok", None),
            P(),
            P(("grp", "tok"), None),
            P(("grp", "tok"), None),
            P(("grp", "tok"), None),
            P(("grp", "tok"), None),
        ),
        out_specs=(P(("grp", "tok"), None), P()),
        check_vma=False,
    )
```

```python
import jax
import jax.numpy as jnp
from jax import lax
from jax.experimental import pallas as pl
from jax.experimental.pallas import tpu as pltpu
from jax.sharding import PartitionSpec as P

HOLDERS = 4
ORDER = (0, 2, 1, 3)
LANES = 128
TILE = 16
BIG = 24 * 1024 * 1024
TRANSPOSED = (((1,), (1,)), ((), ()))
VMEM = pl.BlockSpec(memory_space=pltpu.VMEM)
ANY = pl.BlockSpec(memory_space=pl.ANY)
HBM = pl.BlockSpec(memory_space=pltpu.HBM)
bf16 = jnp.bfloat16
f32 = jnp.float32


def swapped(array, axis, mask):
    return lax.ppermute(array, axis, [(i, i ^ mask) for i in range(lax.axis_size(axis))])


def dot_f32(a, b, dims):
    return lax.dot_general(a, b, dims, preferred_element_type=f32)


def call(body, outs, in_specs, operands, out_specs=None, scratch=(), aliases={}):
    return pl.pallas_call(
        body,
        out_shape=outs,
        in_specs=in_specs,
        out_specs=jax.tree.map(lambda _: VMEM, outs) if out_specs is None else out_specs,
        scratch_shapes=list(scratch),
        compiler_params=pltpu.CompilerParams(vmem_limit_bytes=BIG),
        input_output_aliases=aliases,
    )(*operands)


def core():
    return lax.axis_index("grp") & 1


def holder():
    return lax.axis_index("tok") & (HOLDERS - 1)


def columns_of(half, width):
    return pl.ds(pl.multiple_of(half * width, width), width)


def first_kernel(states_hbm, gain_hbm, down_hbm, route_hbm, out_ref, *refs):
    with_z_ref, kept_ref, z_ref, early_ref, late_ref = refs[:5]
    states_ref, gain_ref, route_ref, sems = refs[5:]
    depth, width = down_hbm.shape[0], kept_ref.shape[1]
    rows, count = states_ref.shape[0], depth + TILE
    beside, first_x = with_z_ref.shape[0] - rows, early_ref.shape[0] - count
    left, right = with_z_ref.at[pl.ds(rows, beside), pl.ds(0, width)], with_z_ref.at[
        pl.ds(rows, beside), pl.ds(width, width)
    ]
    blocks = (
        (0, 0, depth, kept_ref.at[pl.ds(0, depth)]),
        (2, 0, beside, left),
        (2, beside, beside, right),
        (2, 2 * beside, depth - 2 * beside, z_ref.at[pl.ds(0, depth - 2 * beside)]),
        (3, 0, depth, early_ref.at[pl.ds(0, depth)]),
        (1, 0, first_x, early_ref.at[pl.ds(count, first_x)]),
        (1, first_x, depth - first_x, late_ref.at[pl.ds(0, depth - first_x)]),
    )
    copies = [
        pltpu.make_async_copy(states_hbm, states_ref, sems.at[0]),
        pltpu.make_async_copy(gain_hbm, gain_ref, sems.at[1]),
        pltpu.make_async_copy(route_hbm, route_ref, sems.at[2]),
    ]
    for at, (m, top, size, block) in enumerate(blocks):
        source = down_hbm.at[pl.ds(top, size), columns_of(holder() ^ m, width)]
        copies.append(pltpu.make_async_copy(source, block, sems.at[3 + at]))
    for copy in copies:
        copy.start()
    for copy in copies[:3]:
        copy.wait()
    states = states_ref[...].astype(f32)
    scale = lax.rsqrt(jnp.mean(states * states, axis=1, keepdims=True) + 1e-06)
    own = columns_of(core(), out_ref.shape[1])
    normed = (states_ref[:, own].astype(f32) * scale * gain_ref[:, own]).astype(bf16)
    out_ref[...] = normed
    with_z_ref[:rows] = normed
    route = route_ref[...]
    high = route.astype(bf16).astype(f32)
    middle = (route - high).astype(bf16).astype(f32)
    low = route - high - middle
    part = route.shape[1]
    row = lax.broadcasted_iota(jnp.int32, (TILE, part), 0)
    terms = jnp.where(row == 0, high, jnp.where(row == 1, middle, jnp.where(row == 2, low, 0.0)))
    terms = jnp.concatenate([terms, jnp.zeros((TILE, width - part), f32)], 1)
    for ref, top in (
        (kept_ref, depth),
        (z_ref, depth - 2 * beside),
        (early_ref, depth),
        (late_ref, depth - first_x),
    ):
        ref[top : top + TILE] = terms.astype(bf16)
    for copy in copies[3:]:
        copy.wait()


def hold_kernel(*refs):
    pass


def held(array, after):
    return call(
        hold_kernel,
        jax.ShapeDtypeStruct(array.shape, array.dtype),
        [ANY] * 2,
        (array, after),
        out_specs=ANY,
        aliases={0: 0},
    )


def join_kernel(after_ref, first_ref, second_ref, out_ref):
    count = first_ref.shape[0]
    out_ref[:count] = first_ref[...]
    out_ref[count:] = second_ref[: out_ref.shape[0] - count]


def stack_kernel(after_ref, *refs):
    rows = refs[-2].shape[0]
    z = lax.axis_index("tok") >> 1
    for m, piece in enumerate(refs[-2::-1]):
        refs[-1][pl.ds(pl.multiple_of((z ^ m) * rows, rows), rows)] = piece[:rows]


def gated(gate, upward):
    return (gate / (1.0 + jnp.exp(-gate)) * upward).astype(bf16)


def near_kernel(near_ref, near2_ref, far_ref, gate_ref, up_ref, out_ref, gate_part_ref, up_part_ref):
    width = near_ref.shape[1]
    own, rest = columns_of(core(), width), columns_of(1 - core(), width)
    near, near2, far = near_ref[...], near2_ref[...], far_ref[...]
    gate, upward = [
        dot_f32(ref[:, own], near, TRANSPOSED) + dot_f32(ref[:, rest], near2, TRANSPOSED)
        for ref in (gate_ref, up_ref)
    ]
    out_ref[...] = gated(gate, upward)
    gate_part_ref[...] = dot_f32(gate_ref[:, own], far, TRANSPOSED)
    up_part_ref[...] = dot_f32(up_ref[:, own], far, TRANSPOSED)


def far_kernel(after_ref, far2_ref, gate_ref, up_ref, near_hidden_ref, gate_part_ref, up_part_ref, out_ref):
    count, width = far2_ref.shape
    rest = columns_of(1 - core(), width)
    far2 = far2_ref[...]
    gate, upward = [
        part_ref[...] + dot_f32(ref[:, rest], far2, TRANSPOSED)
        for ref, part_ref in ((gate_ref, gate_part_ref), (up_ref, up_part_ref))
    ]
    x = lax.axis_index("tok") & 1
    out_ref[:, columns_of(x, count)] = near_hidden_ref[...]
    out_ref[:, columns_of(1 - x, count)] = gated(gate, upward)


def features_kernel(*refs):
    hidden_refs, (kept_ref, with_z_ref, z_ref, early_ref, late_ref) = refs[:HOLDERS], refs[HOLDERS:][:5]
    block_refs, shares_hbm = refs[HOLDERS + 5 : 2 * HOLDERS + 5], refs[2 * HOLDERS + 5]
    route_ref, features_ref, whole_ref, shares_ref, sem = refs[2 * HOLDERS + 6 :]
    depth, tokens = hidden_refs[0].shape
    part, members = tokens // HOLDERS, lax.axis_size("tok")
    rows = tokens // members
    count, width = kept_ref.shape
    beside = (2 * count - z_ref.shape[0]) // 2
    x_block = jnp.concatenate([early_ref[count:], late_ref[...]])
    z_block = jnp.concatenate(
        [with_z_ref[rows:, :width], with_z_ref[rows:, width:], z_ref[: count - 2 * beside]]
    )
    downs = (kept_ref[...], x_block, z_block, z_ref[count - 2 * beside :])

    def place(m, piece):
        z = (holder() ^ m) * (members // HOLDERS // 2) + piece // 2
        return pl.ds(pl.multiple_of(piece % 2 * (tokens // 2) + z * rows, rows), rows)

    eye = lax.broadcasted_iota(jnp.int32, (part, part), 0) == lax.broadcasted_iota(
        jnp.int32, (part, part), 1
    )
    output = None
    for m, hidden_ref in zip(ORDER, hidden_refs):
        down = downs[m]
        product = dot_f32(hidden_ref[...], down[:depth], (((0,), (0,)), ((), ())))
        output = product if output is None else output + product
        terms = down[depth:, :part].astype(f32)
        route = jnp.sum(terms[:HOLDERS], axis=0, keepdims=True)
        column = jnp.sum(jnp.where(eye, route, 0.0), axis=1, keepdims=True)
        column = jnp.broadcast_to(column, (part, LANES))
        for piece in range(part // rows):
            route_ref[place(m, piece)] = column[piece * rows : (piece + 1) * rows]
    features = (output * route_ref[:, :1]).astype(bf16)
    features_ref[...] = features
    wide = features.astype(f32)
    mean = jnp.sum(wide, axis=0, keepdims=True) / tokens
    column = jnp.sum(wide * mean, axis=1, keepdims=True)
    row = jnp.transpose(jnp.broadcast_to(column, (tokens, LANES)))[:1]
    gram = dot_f32(features, features, TRANSPOSED)
    whole_ref[...] = (gram - column - row + jnp.sum(mean * mean)).astype(bf16)
    at = 0
    for i in range(tokens // TILE):
        for j in range(tokens // LANES):
            shares_ref[at * TILE : (at + 1) * TILE] = whole_ref[
                i * TILE : (i + 1) * TILE, j * LANES : (j + 1) * LANES
            ]
            at += 1
    copy = pltpu.make_async_copy(shares_ref, shares_hbm, sem)
    copy.start()
    for m, block_ref in enumerate(block_refs):
        for piece in range(part // rows):
            block_ref[piece * rows : (piece + 1) * rows] = features_ref[place(m, piece)]
    copy.wait()


def place_kernel(*refs):
    blocks, out_ref, sems = refs[:HOLDERS], refs[HOLDERS], refs[HOLDERS + 1]
    width = blocks[0].shape[1]
    copies = []
    for m, block in enumerate(blocks):
        columns = pl.ds(pl.multiple_of((holder() ^ m) * width, width), width)
        copies.append(pltpu.make_async_copy(block, out_ref.at[:, columns], sems.at[m]))
        copies[-1].start()
    for copy in copies:
        copy.wait()


def pair_kernel(parts_ref, out_ref, flat_ref):
    experts = flat_ref.shape[0]
    parts = parts_ref[...].astype(f32)
    total = parts[:, 0]
    for m in range(1, parts.shape[1]):
        total = total + parts[:, m]
    flat_ref[...] = total.astype(bf16).astype(f32)
    in_row = out_ref.shape[1] == 1
    shape = (experts, out_ref.shape[2])
    row = lax.broadcasted_iota(jnp.int32, shape, 0)
    lane = lax.broadcasted_iota(jnp.int32, shape, 1)

    def one(expert, table):
        products = jnp.sum(flat_ref[...] * flat_ref[pl.ds(expert, 1)], axis=1)
        here = lane == expert * experts + row if in_row else lane == expert
        return jnp.where(here, jnp.sum(products, axis=1, keepdims=True), table)

    table = lax.fori_loop(0, experts, one, jnp.zeros(shape, f32), unroll=experts <= 8)
    if in_row:
        table = jnp.sum(table, axis=0, keepdims=True)
    out_ref[...] = jnp.broadcast_to(table[None], out_ref.shape)


def cka_kernel(tables_ref, out_ref):
    totals = jnp.sum(tables_ref[...], axis=0)
    shape = out_ref.shape
    row = lax.broadcasted_iota(jnp.int32, shape, 0)
    lane = lax.broadcasted_iota(jnp.int32, shape, 1)
    if totals.shape != shape:
        experts = shape[0]
        wide = (experts, totals.shape[1])
        spread = jnp.broadcast_to(totals, wide)
        at = lax.broadcasted_iota(jnp.int32, wide, 1) - experts * lax.broadcasted_iota(
            jnp.int32, wide, 0
        )
        totals = jnp.zeros(shape, f32)
        for column in range(experts):
            values = jnp.sum(jnp.where(at == column, spread, 0.0), axis=1, keepdims=True)
            totals = jnp.where(lane == column, values, totals)
    kept = jnp.where(row == lane, totals, 0.0)
    down = jnp.sum(kept, axis=1, keepdims=True)
    across = jnp.sum(kept, axis=0, keepdims=True)
    out_ref[...] = totals / jnp.sqrt(down * across)


def shards(probe_states, norm_gain, gate_weight, up_weight, down_weight, route_weight):
    groups, members = lax.axis_size("grp"), lax.axis_size("tok")
    devices = groups * members
    experts = devices // HOLDERS
    rows, model = probe_states.shape
    tokens = rows * members
    depth = gate_weight.shape[0]
    part, token_part = model // HOLDERS, tokens // HOLDERS

    count = depth + TILE
    beside, first_x = depth // 4 // TILE * TILE, depth // 3 // TILE * TILE
    own, with_z, down_own, down_z, down_early, down_late = call(
        first_kernel,
        [jax.ShapeDtypeStruct((n, model // 2), bf16) for n in (rows, rows + beside)]
        + [
            jax.ShapeDtypeStruct((n, part), bf16)
            for n in (count, count - 2 * beside, count + first_x, count - first_x)
        ],
        [HBM] * 4,
        [
            pltpu.with_memory_space_constraint(a, pltpu.HBM)
            for a in (probe_states, norm_gain[None, :], down_weight, route_weight)
        ],
        scratch=[
            pltpu.VMEM((rows, model), bf16),
            pltpu.VMEM((1, model), f32),
            pltpu.VMEM(route_weight.shape, f32),
            pltpu.SemaphoreType.DMA((10,)),
        ],
    )
    down_early = swapped(down_early, "tok", 1)
    with_z = swapped(with_z, "tok", 2)
    pieces = [swapped(own, "tok", 2 * m) for m in range(members // 2 - 1, 1, -1)] + [with_z, own]
    near = call(
        stack_kernel,
        jax.ShapeDtypeStruct((tokens // 2, model // 2), bf16),
        [ANY] + [VMEM] * len(pieces),
        (down_early, *pieces),
    )
    far = swapped(near, "tok", 1)
    near2 = swapped(near, "grp", 1)
    down_z = call(
        join_kernel,
        jax.ShapeDtypeStruct((2 * (count - beside), part), bf16),
        [ANY, VMEM, VMEM],
        (near, down_z, down_early),
    )
    down_z = swapped(down_z, "tok", 2)
    down_late = swapped(held(down_late, far), "tok", 1)
    half_shape = (depth, tokens // 2)
    near_hidden, gate_part, up_part = call(
        near_kernel,
        [jax.ShapeDtypeStruct(half_shape, dtype) for dtype in (bf16, f32, f32)],
        [VMEM] * 5,
        (near, near2, far, gate_weight, up_weight),
    )
    hidden = call(
        far_kernel,
        jax.ShapeDtypeStruct((depth, tokens), bf16),
        [ANY] + [VMEM] * 6,
        (down_z, swapped(far, "grp", 1), gate_weight, up_weight, near_hidden, gate_part, up_part),
    )
    hiddens = [swapped(hidden, "tok", m) if m else hidden for m in ORDER]
    entries = tokens * tokens // LANES
    *blocks, centered = call(
        features_kernel,
        [jax.ShapeDtypeStruct((token_part, part), bf16)] * HOLDERS
        + [jax.ShapeDtypeStruct((entries, LANES), bf16)],
        [VMEM] * (HOLDERS + 5),
        (*hiddens, down_own, with_z, down_z, down_early, down_late),
        out_specs=[VMEM] * HOLDERS + [HBM],
        scratch=[
            pltpu.VMEM((tokens, LANES), f32),
            pltpu.VMEM((tokens, part), bf16),
            pltpu.VMEM((tokens, tokens), bf16),
            pltpu.VMEM((entries, LANES), bf16),
            pltpu.SemaphoreType.DMA,
        ],
    )
    arrived = lax.all_to_all(centered, ("grp", "tok"), split_axis=0, concat_axis=0, tiled=True)
    arrived = arrived.reshape(experts, HOLDERS, entries // devices, LANES)
    direct = experts * experts <= LANES
    tables = call(
        pair_kernel,
        jax.ShapeDtypeStruct((devices, 1, LANES) if direct else (1, experts, experts), f32),
        [VMEM],
        (arrived,),
        scratch=[pltpu.VMEM((experts, entries // devices, LANES), f32)],
    )
    if direct:
        tables = lax.all_to_all(tables, ("grp", "tok"), split_axis=0, concat_axis=0, tiled=True)
    else:
        tables = lax.psum(tables, ("grp", "tok"))
    cka = call(cka_kernel, jax.ShapeDtypeStruct((experts, experts), f32), [VMEM], (tables,))

    blocks = [swapped(b, "tok", m) if m else b for m, b in enumerate(blocks)]
    features = call(
        place_kernel,
        jax.ShapeDtypeStruct((token_part, model), bf16),
        [VMEM] * HOLDERS,
        blocks,
        out_specs=ANY,
        scratch=[pltpu.SemaphoreType.DMA((HOLDERS,))],
    )
    return (features, cka)


def solution(mesh):
    return jax.shard_map(
        shards,
        mesh=mesh,
        in_specs=(
            P("tok", None),
            P(),
            P(("grp", "tok"), None),
            P(("grp", "tok"), None),
            P(("grp", "tok"), None),
            P(("grp", "tok"), None),
        ),
        out_specs=(P(("grp", "tok"), None), P()),
        check_vma=False,
    )
```
